128 devices in a mesh: seq: 32 (over z, y, x_lo), tp: 4 (over x_hi, core).
Axes of the slice: x: 4 (x_hi: 2, x_lo: 2; x = x_hi * 2 + x_lo), y: 4, z: 4, core: 2. Of those that a mesh axis runs over, the one named last changes fastest.
Arguments:
- img: bfloat16 [4096, 2432], P('seq', 'tp'), may hold values from -0.119628906 to 0.119628906
- txt: bfloat16 [512, 2432], P('seq', 'tp'), may hold values from -0.119628906 to 0.119628906
- ctl: bfloat16 [4096, 2432], P('seq', 'tp'), may hold values from -6 to 6
- dy_img: bfloat16 [4096, 2432], P('seq', 'tp'), may hold values from -6 to 6
- text_output_cotangent: bfloat16 [512, 2432], P('seq', 'tp'), may hold values from -6 to 6
- live_text_length: int32 [1], replicated, may hold values from 128 to 512
- modulation: float32 [3, 3, 2432], replicated, may hold values from -3 to 3
- query_key_gains: float32 [3, 2, 64], replicated, may hold values from 0.1 to 1.9
- w_qkv_img: bfloat16 [2432, 3, 1536], P(None, None, 'tp'), may hold values from -0.125 to 0.125
- image_output_weight: bfloat16 [1536, 2432], P('tp'), may hold values from -0.15625 to 0.15625
- w_qkv_txt: bfloat16 [2432, 3, 1536], P(None, None, 'tp'), may hold values from -0.125 to 0.125
- text_output_weight: bfloat16 [1536, 2432], P('tp'), may hold values from -0.15625 to 0.15625
- w_qkv_ctl: bfloat16 [2432, 3, 1536], P(None, None, 'tp'), may hold values from -0.125 to 0.125
- w_out_ctl: bfloat16 [1536, 2432], P('tp'), may hold values from -0.15625 to 0.15625
Outputs:
- y_img: bfloat16 [4096, 2432], P('seq', 'tp')
- y_txt: bfloat16 [512, 2432], P('seq', 'tp')
- d_img: bfloat16 [4096, 2432], P('seq', 'tp')
- text_input_gradient: bfloat16 [512, 2432], P('seq', 'tp')
- control_input_gradient: bfloat16 [4096, 2432], P('seq', 'tp')
- grad_qkv_ctl: float32 [2432, 3, 1536], P('seq', None, 'tp')
- grad_out_ctl: float32 [1536, 2432], P('tp', 'seq')
The draws below stay inside these ranges and needn't reach their ends.
Inputs may be any that keep to these rules, and one draw needn't show every extreme that they name: `live_text_length`: the number of live text tokens of the sample; text slots from this number on are padding and never attended to.
All inputs are finite; a program needn't handle non-finite values.
Results may differ from the reference program's by a relative error of at most 0.033.
Values may be sent and summed in bfloat16 or wider, within the bound.
No kernel may reach another device: no remote copies, remote signals or barrier semaphores. Data moves between devices by JAX's collectives and lax.ppermute only.
A program may use at most 256 MiB of HBM per device.

```python
from functools import partial
import jax
import jax.numpy as jnp
from jax import lax

D = 2432
HEAD_SIZE = 64
LOCAL_HEADS = 24
IMAGE_PER_SHARD = 128
TXT_DEV = 16
IMAGE_TOKENS = 4096
TEXT_SLOTS = 512
N_SEQ = 32


def levels(own_key, dims, split, low, high):
    level = 1.0
    for position, blocks in split:
        heights = jax.random.uniform(jax.random.fold_in(jax.random.fold_in(own_key, 6), position), (blocks,), jnp.float32, low / len(split), high / len(split))
        level = level * jnp.repeat(jnp.exp(heights), dims[position] // blocks).reshape((-1,) + (1,) * (len(dims) - 1 - position))
    return level


def scatter_about(own_key, extent, spread, most, pieces=(), kind=jnp.bfloat16):
    factor_of = levels(own_key, extent, pieces, -0.22, 0.18) if pieces else 1.0
    drawn = jax.random.normal(own_key, extent, jnp.float32) * spread * factor_of
    return jnp.minimum(jnp.maximum(drawn, -most), most).astype(kind)


def setup_inputs(seed: int = 0) -> dict:
    key_of = jax.random.split(jax.random.key(seed), 15)
    return {
        "img": scatter_about(key_of[0], (IMAGE_TOKENS, D), 0.02, 0.119628906, ((0, 32), (1, 4))),
        "txt": scatter_about(key_of[1], (TEXT_SLOTS, D), 0.02, 0.119628906, ((0, 32), (1, 4))),
        "ctl": scatter_about(key_of[2], (IMAGE_TOKENS, D), 1.0, 6.0, ((0, 32), (1, 4))),
        "dy_img": scatter_about(key_of[3], (IMAGE_TOKENS, D), 1.0, 6.0, ((0, 32), (1, 4))),
        "text_output_cotangent": scatter_about(key_of[4], (TEXT_SLOTS, D), 1.0, 6.0, ((0, 32), (1, 4))),
        "live_text_length": jax.random.randint(key_of[5], (1,), TEXT_SLOTS // 4, TEXT_SLOTS + 1).astype(jnp.int32),
        "modulation": scatter_about(key_of[6], (3, 3, D), 0.5, 3.0, (), jnp.float32),
        "query_key_gains": jnp.clip(1.0 + 0.18 * jax.random.normal(key_of[7], (3, 2, HEAD_SIZE), jnp.float32), 0.1, 1.9),
        "w_qkv_img": scatter_about(key_of[8], (D, 3, LOCAL_HEADS * HEAD_SIZE), D ** -0.5, 0.125, ((2, 4),)),
        "image_output_weight": scatter_about(key_of[9], (LOCAL_HEADS * HEAD_SIZE, D), (LOCAL_HEADS * HEAD_SIZE) ** -0.5, 0.15625, ((0, 4),)),
        "w_qkv_txt": scatter_about(key_of[10], (D, 3, LOCAL_HEADS * HEAD_SIZE), D ** -0.5, 0.125, ((2, 4),)),
        "text_output_weight": scatter_about(key_of[11], (LOCAL_HEADS * HEAD_SIZE, D), (LOCAL_HEADS * HEAD_SIZE) ** -0.5, 0.15625, ((0, 4),)),
        "w_qkv_ctl": scatter_about(key_of[12], (D, 3, LOCAL_HEADS * HEAD_SIZE), D ** -0.5, 0.125, ((2, 4),)),
        "w_out_ctl": scatter_about(key_of[13], (LOCAL_HEADS * HEAD_SIZE, D), (LOCAL_HEADS * HEAD_SIZE) ** -0.5, 0.15625, ((0, 4),)),
    }


EPS = 1e-06
CONTRACT_ROWS = (((0,), (0,)), ((), ()))
CONTRACT_COLS = (((1,), (1,)), ((), ()))

def rounded(value_rows):
    return lax.optimization_barrier(value_rows.astype(jnp.bfloat16)).astype(jnp.float32)

def norm_rows(rows_in, modulation_params):
    values = rows_in.astype(jnp.float32)
    centered_input = values - lax.optimization_barrier(jnp.mean(values, axis=-1, keepdims=True))
    inverse_deviation = lax.rsqrt(lax.optimization_barrier(jnp.mean(centered_input * centered_input, axis=-1, keepdims=True)) + EPS)
    standardized_input = centered_input * inverse_deviation
    normalized_input = (standardized_input * (1.0 + modulation_params[1]) + modulation_params[0]).astype(jnp.bfloat16)
    return (normalized_input, standardized_input, inverse_deviation)

def head_norm(values, gain):
    return values * lax.rsqrt(lax.optimization_barrier(jnp.mean(values * values, axis=-1, keepdims=True)) + EPS) * gain

def project(normalized_input, w_qkv, gains):
    row_count = normalized_input.shape[0]
    heads_on_shard = w_qkv.shape[2] // HEAD_SIZE
    proj = jnp.dot(normalized_input, w_qkv.reshape(w_qkv.shape[0], -1), preferred_element_type=jnp.float32)
    proj = proj.reshape(row_count, 3, heads_on_shard, HEAD_SIZE)
    query = head_norm(proj[:, 0], gains[0]).astype(jnp.bfloat16)
    key_portion = head_norm(proj[:, 1], gains[1]).astype(jnp.bfloat16)
    value_rows = proj[:, 2].astype(jnp.bfloat16)
    return (proj, query, key_portion, value_rows)

def projection_gradient(proj, gains, dquery, dkey, dvalue):
    ignored, back_query = jax.vjp(lambda values: head_norm(values, gains[0]), proj[:, 0])
    ignored, back_key = jax.vjp(lambda values: head_norm(values, gains[1]), proj[:, 1])
    stacked = jnp.stack([back_query(dquery)[0], back_key(dkey)[0], dvalue], 1)
    return stacked.astype(jnp.bfloat16).reshape(proj.shape[0], -1)

def scores(query, key_portion, valid_mask):
    score = jnp.einsum('qhd,khd->hqk', query.astype(jnp.float32), key_portion.astype(jnp.float32)) * HEAD_SIZE ** (-0.5)
    return jnp.where(valid_mask[None, None, :], score, -jnp.inf)

def forward_attention_block(query, key_portion, value_rows, valid_mask):
    score = scores(query, key_portion, valid_mask)
    top = lax.optimization_barrier(jnp.max(score, axis=-1, keepdims=True))
    lse = top + jnp.log(lax.optimization_barrier(jnp.sum(jnp.exp(score - top), axis=-1, keepdims=True)))
    weights = rounded(jnp.exp(score - lse))
    attended = jnp.einsum('hqk,khd->qhd', weights, value_rows.astype(jnp.float32)).astype(jnp.bfloat16)
    return (attended, lse)

def backward_block(query, key_portion, value_rows, valid_mask, attended, dout, lse):
    probability = jnp.exp(scores(query, key_portion, valid_mask) - lse)
    weights = rounded(probability)
    dout_wide = dout.astype(jnp.float32)
    row_delta = lax.optimization_barrier(jnp.sum(dout_wide * attended.astype(jnp.float32), axis=-1))
    prob_grad = jnp.einsum('qhd,khd->hqk', dout_wide, value_rows.astype(jnp.float32))
    dscore = rounded(probability * (prob_grad - row_delta.T[:, :, None]) * HEAD_SIZE ** (-0.5))
    dquery = jnp.einsum('hqk,khd->qhd', dscore, key_portion.astype(jnp.float32))
    dkey = rounded(jnp.einsum('hqk,qhd->khd', dscore, query.astype(jnp.float32)))
    dvalue = rounded(jnp.einsum('hqk,qhd->khd', weights, dout_wide))
    return (dquery, dkey, dvalue)

def backward_loop(query_block_list, o_blocks, d_blocks, lse_blocks, key_portion, value_rows, valid_mask):
    zero_keys = jnp.zeros(key_portion.shape, jnp.float32)

    def advance(totals, inputs):
        dquery, dkey, dvalue = backward_block(inputs[0], key_portion, value_rows, valid_mask, inputs[1], inputs[2], inputs[3])
        return ((totals[0] + dkey, totals[1] + dvalue), dquery)
    summed, dquery_all = lax.scan(advance, (zero_keys, zero_keys), (query_block_list, o_blocks, d_blocks, lse_blocks))
    return (dquery_all, summed[0], summed[1])

def output_backward(grads, w_out):
    result = lax.dot_general(grads, w_out, CONTRACT_COLS, preferred_element_type=jnp.float32)
    return result.astype(jnp.bfloat16).reshape(grads.shape[0], -1, HEAD_SIZE)

def qkv_back(grads, w_qkv):
    return lax.dot_general(grads, w_qkv.reshape(w_qkv.shape[0], -1), CONTRACT_COLS, preferred_element_type=jnp.float32)

def norm_backward(normed_gradient, modulation_params, standardized_input, inverse_deviation):
    scaled_input = normed_gradient * (1.0 + modulation_params[1])
    centered_input = scaled_input - lax.optimization_barrier(jnp.mean(scaled_input, axis=-1, keepdims=True))
    return (centered_input - standardized_input * lax.optimization_barrier(jnp.mean(scaled_input * standardized_input, axis=-1, keepdims=True))) * inverse_deviation

def reference(img, txt, ctl, dy_img, text_output_cotangent, live_text_length, modulation, query_key_gains, w_qkv_img, image_output_weight, w_qkv_txt, text_output_weight, w_qkv_ctl, w_out_ctl):
    head_feature_width = LOCAL_HEADS * HEAD_SIZE
    n_img, image_normalized, rs_img = norm_rows(img, modulation[0])
    n_txt, text_normalized, rs_txt = norm_rows(txt, modulation[1])
    n_ctl, control_normalized, rs_ctl = norm_rows(ctl, modulation[2])
    image_projected, image_query, image_key, image_value = project(n_img, w_qkv_img, query_key_gains[0])
    text_projected, text_query, text_key, text_value = project(n_txt, w_qkv_txt, query_key_gains[1])
    control_projected, control_query, k_ctl, v_ctl = project(n_ctl, w_qkv_ctl, query_key_gains[2])
    main_keys = jnp.concatenate([image_key, text_key], 0)
    main_values = jnp.concatenate([image_value, text_value], 0)
    main_valid_mask = jnp.concatenate([jnp.ones((IMAGE_TOKENS,), jnp.bool_), jnp.arange(TEXT_SLOTS) < live_text_length[0]])
    valid_ctl = jnp.ones((IMAGE_TOKENS,), jnp.bool_)
    query_block_list = jnp.concatenate([image_query.reshape(N_SEQ, IMAGE_PER_SHARD, LOCAL_HEADS, HEAD_SIZE), text_query.reshape(N_SEQ, TXT_DEV, LOCAL_HEADS, HEAD_SIZE)], 1)
    qc_blocks = control_query.reshape(N_SEQ, IMAGE_PER_SHARD, LOCAL_HEADS, HEAD_SIZE)
    main_output, main_logsumexp = lax.map(partial(forward_attention_block, key_portion=main_keys, value_rows=main_values, valid_mask=main_valid_mask), query_block_list)
    o_cblk, control_logsumexp = lax.map(partial(forward_attention_block, key_portion=k_ctl, value_rows=v_ctl, valid_mask=valid_ctl), qc_blocks)
    image_output = main_output[:, :IMAGE_PER_SHARD].reshape(IMAGE_TOKENS, head_feature_width)
    text_output = main_output[:, IMAGE_PER_SHARD:].reshape(TEXT_SLOTS, head_feature_width)
    o_ctl = o_cblk.reshape(IMAGE_TOKENS, head_feature_width)
    gate_img = modulation[0, 2]
    gate_txt = modulation[1, 2]
    gate_ctl = modulation[2, 2]
    mix_img = gate_img * jnp.dot(image_output, image_output_weight, preferred_element_type=jnp.float32) + gate_ctl * jnp.dot(o_ctl, w_out_ctl, preferred_element_type=jnp.float32)
    y_img = (img.astype(jnp.float32) + mix_img).astype(jnp.bfloat16)
    y_txt = (txt.astype(jnp.float32) + gate_txt * jnp.dot(text_output, text_output_weight, preferred_element_type=jnp.float32)).astype(jnp.bfloat16)
    image_modulation = (gate_img * dy_img.astype(jnp.float32)).astype(jnp.bfloat16)
    text_modulation = (gate_txt * text_output_cotangent.astype(jnp.float32)).astype(jnp.bfloat16)
    e_ctl = (gate_ctl * dy_img.astype(jnp.float32)).astype(jnp.bfloat16)
    do_img = output_backward(image_modulation, image_output_weight)
    do_txt = output_backward(text_modulation, text_output_weight)
    control_output_gradient = output_backward(e_ctl, w_out_ctl)
    output_gradient_blocks = jnp.concatenate([do_img.reshape(N_SEQ, IMAGE_PER_SHARD, LOCAL_HEADS, HEAD_SIZE), do_txt.reshape(N_SEQ, TXT_DEV, LOCAL_HEADS, HEAD_SIZE)], 1)
    main_query_gradient, main_key_gradient, main_value_gradient = backward_loop(query_block_list, main_output, output_gradient_blocks, main_logsumexp, main_keys, main_values, main_valid_mask)
    dq_cblk, control_key_gradient, control_value_gradient = backward_loop(qc_blocks, o_cblk, control_output_gradient.reshape(N_SEQ, IMAGE_PER_SHARD, LOCAL_HEADS, HEAD_SIZE), control_logsumexp, k_ctl, v_ctl, valid_ctl)
    image_query_gradient = main_query_gradient[:, :IMAGE_PER_SHARD].reshape(IMAGE_TOKENS, LOCAL_HEADS, HEAD_SIZE)
    text_query_gradient = main_query_gradient[:, IMAGE_PER_SHARD:].reshape(TEXT_SLOTS, LOCAL_HEADS, HEAD_SIZE)
    image_projection_gradient = projection_gradient(image_projected, query_key_gains[0], image_query_gradient, main_key_gradient[:IMAGE_TOKENS], main_value_gradient[:IMAGE_TOKENS])
    text_projection_gradient = projection_gradient(text_projected, query_key_gains[1], text_query_gradient, main_key_gradient[IMAGE_TOKENS:], main_value_gradient[IMAGE_TOKENS:])
    dp_ctl = projection_gradient(control_projected, query_key_gains[2], dq_cblk.reshape(IMAGE_TOKENS, LOCAL_HEADS, HEAD_SIZE), control_key_gradient, control_value_gradient)

    def accumulate(totals, inputs):
        term_qkv = rounded(lax.dot_general(inputs[0], inputs[1], CONTRACT_ROWS, preferred_element_type=jnp.float32))
        term_out = rounded(lax.dot_general(inputs[2], inputs[3], CONTRACT_ROWS, preferred_element_type=jnp.float32))
        return ((totals[0] + term_qkv, totals[1] + term_out), None)
    start_totals = (jnp.zeros((D, 3 * head_feature_width), jnp.float32), jnp.zeros((head_feature_width, D), jnp.float32))
    weight_sums, ignored = lax.scan(accumulate, start_totals, (n_ctl.reshape(N_SEQ, IMAGE_PER_SHARD, D), dp_ctl.reshape(N_SEQ, IMAGE_PER_SHARD, 3 * head_feature_width), o_ctl.reshape(N_SEQ, IMAGE_PER_SHARD, head_feature_width), e_ctl.reshape(N_SEQ, IMAGE_PER_SHARD, D)))
    d_img = (dy_img.astype(jnp.float32) + norm_backward(qkv_back(image_projection_gradient, w_qkv_img), modulation[0], image_normalized, rs_img)).astype(jnp.bfloat16)
    text_input_gradient = (text_output_cotangent.astype(jnp.float32) + norm_backward(qkv_back(text_projection_gradient, w_qkv_txt), modulation[1], text_normalized, rs_txt)).astype(jnp.bfloat16)
    control_input_gradient = norm_backward(qkv_back(dp_ctl, w_qkv_ctl), modulation[2], control_normalized, rs_ctl).astype(jnp.bfloat16)
    return (y_img, y_txt, d_img, text_input_gradient, control_input_gradient, weight_sums[0].reshape(D, 3, head_feature_width), weight_sums[1])
```

```python
import jax
import jax.numpy as jnp
from jax import lax
from jax.experimental import pallas as pl
from jax.experimental.pallas import tpu as pltpu
from jax.sharding import Mesh, PartitionSpec as P

EPS = 1e-06
HEAD = 64
HEADS = 6
WIDTH = HEADS * HEAD
D = 2432
SHARE = 608
PIECE = 152
ROWS = 3 * SHARE + PIECE
IMG = 128
TXT = 16
BLOCKS = 32
CHUNK = 192
IMAGE_KEYS = BLOCKS * IMG
TEXT_KEYS = BLOCKS * TXT
MAIN_Q = 48
CTL_Q = 64
MAIN_PARTS = 3
CTL_PARTS = 2
CTL_AT = HEADS * MAIN_PARTS
TQ = 512
TK = 512
F32 = jnp.float32
BF16 = jnp.bfloat16
NT = (((1,), (1,)), ((), ()))
VMEM = pl.BlockSpec(memory_space=pltpu.VMEM)
SMEM = pl.BlockSpec(memory_space=pltpu.SMEM)
ANY = pl.BlockSpec(memory_space=pl.ANY)
HBM = pl.BlockSpec(memory_space=pltpu.HBM)


def params(mib):
    return pltpu.CompilerParams(vmem_limit_bytes=mib * 1024 * 1024)


def dot(a, b):
    return jnp.dot(a, b, preferred_element_type=F32)


def dot_nt(a, b):
    return lax.dot_general(a, b, NT, preferred_element_type=F32)


def head(values, h):
    return values[:, h * HEAD : (h + 1) * HEAD]


def inverse_rms(values):
    return lax.rsqrt(jnp.mean(values * values, axis=-1, keepdims=True) + EPS)


def spread_text(packed):
    return jnp.concatenate([packed] + [pltpu.roll(packed, 128 - 32 * a, 1) for a in (1, 2, 3)], 0)


def pack_text(columns):
    pieces = [columns[PIECE * a : PIECE * (a + 1)] for a in range(4)]
    return pieces[0] + sum(pltpu.roll(pieces[a], 32 * a, 1) for a in (1, 2, 3))


def load_kernel(after, *refs):
    sources, targets, token, sems = refs[0:3], refs[3:6], refs[6], refs[7]
    token[...] = jnp.zeros_like(token)
    copies = [pltpu.make_async_copy(a, b, sems.at[i]) for i, (a, b) in enumerate(zip(sources, targets))]
    for copy in copies:
        copy.start()
    for copy in copies:
        copy.wait()


def load(weights, after):
    return pl.pallas_call(
        load_kernel,
        out_shape=[jax.ShapeDtypeStruct(w.shape, w.dtype) for w in weights] + [jax.ShapeDtypeStruct((8, 128), F32)],
        in_specs=[ANY] + [HBM] * 3,
        out_specs=[VMEM] * 4,
        scratch_shapes=[pltpu.SemaphoreType.DMA((3,))],
        compiler_params=params(40),
        cost_estimate=pl.CostEstimate(flops=0, bytes_accessed=30_000_000, transcendentals=0),
        name="load",
    )(after, *weights)


def order_kernel(x, after, out):
    pass


def ordered(x, after):
    return pl.pallas_call(
        order_kernel,
        out_shape=jax.ShapeDtypeStruct(x.shape, x.dtype),
        in_specs=[ANY] * 2,
        out_specs=ANY,
        input_output_aliases={0: 0},
        compiler_params=params(1),
        name="order",
    )(x, after)


def pack_kernel(img, ctl, dy, txt, dy_txt, out, token, text_rows, sems):
    token[...] = jnp.zeros_like(token)
    copies = [
        pltpu.make_async_copy(part, text_rows.at[i], sems.at[3 + i]) for i, part in enumerate((txt, dy_txt))
    ] + [
        pltpu.make_async_copy(part, out.at[pl.ds(SHARE * i, SHARE)], sems.at[i])
        for i, part in enumerate((img, ctl, dy))
    ]
    for copy in copies:
        copy.start()
    copies[0].wait()
    copies[1].wait()
    text = text_rows[...].reshape(2 * TXT, SHARE).astype(F32)
    text = jnp.concatenate([text, jnp.zeros((IMG - 2 * TXT, SHARE), F32)], 0)
    text = jnp.concatenate([text, jnp.zeros((IMG, 640 - SHARE), F32)], 1)
    out[3 * SHARE :, :] = pack_text(text.T).astype(BF16)
    for copy in copies[2:]:
        copy.wait()


def pre_kernel(
    in0, in1, in2, in3, mod, gains, wq_img, wq_txt, wq_ctl, wo_img, wo_txt, wo_ctl,
    send, proj, xhat, rstd, nz0, nz1, nz2, nz3, ny0, ny1, ny2, ny3,
    gat, nz, ny,
):
    for i, part in enumerate((in0, in1, in2, in3)):
        gat[lax.axis_index("tp") ^ i] = part[...]

    def rows(slab):
        return gat[:, SHARE * slab : SHARE * (slab + 1), :].reshape(D, IMG).T.astype(F32)

    def stream(s, x, e, at):
        count = x.shape[0]
        centered = x - jnp.mean(x, axis=-1, keepdims=True)
        inverse = lax.rsqrt(jnp.mean(centered * centered, axis=-1, keepdims=True) + EPS)
        standard = centered * inverse
        xhat[at : at + count, :] = standard
        rstd[at : at + count, :] = jnp.broadcast_to(inverse, (count, 128))
        n = (standard * (1.0 + mod[s, 1:2, :]) + mod[s, 0:1, :]).astype(BF16)
        wq, wo = ((wq_img, wo_img), (wq_txt, wo_txt), (wq_ctl, wo_ctl))[s]
        pq = dot(n, wq[0])
        pk = dot(n, wq[1])
        pv = dot(n, wq[2])
        proj[at : at + count, 0:WIDTH] = pq
        proj[at : at + count, WIDTH : 2 * WIDTH] = pk
        g = dot_nt(e, wo[...])
        kv, qg = [], []
        for h in range(HEADS):
            q_h, k_h = head(pq, h), head(pk, h)
            q_h = q_h * inverse_rms(q_h) * (gains[s, 0:1, :] * 0.125)
            k_h = k_h * inverse_rms(k_h) * gains[s, 1:2, :]
            kv.append(jnp.concatenate([k_h, head(pv, h)], 1).astype(BF16))
            qg.append(jnp.concatenate([q_h, head(g, h)], 1).astype(BF16))
        return n, kv, qg

    dy = rows(2)
    text = jnp.concatenate([spread_text(gat[c, 3 * SHARE :, :].astype(F32)) for c in range(4)], 0).astype(BF16).T.astype(F32)
    e_img = (mod[0, 2:3, :] * dy).astype(BF16)
    n, kv, qg = stream(0, rows(0), e_img, 0)
    for h in range(HEADS):
        for t in range(MAIN_PARTS):
            to = MAIN_PARTS * h + t
            send[to, 0:IMG, :] = kv[h]
            last = min(IMG, MAIN_Q * (t + 1))
            send[to, IMG + TXT : IMG + TXT + last - MAIN_Q * t, :] = qg[h][MAIN_Q * t : last]
    e_txt = (mod[1, 2:3, :] * text[TXT : 2 * TXT]).astype(BF16)
    n, kv, qg = stream(1, text[0:TXT], e_txt, IMG)
    for h in range(HEADS):
        for t in range(MAIN_PARTS):
            send[MAIN_PARTS * h + t, IMG : IMG + TXT, :] = kv[h]
        send[MAIN_PARTS * h + 2, CHUNK - TXT : CHUNK, :] = qg[h]
    e_ctl = mod[2, 2:3, :] * dy
    n, kv, qg = stream(2, rows(1), e_ctl.astype(BF16), IMG + TXT)
    for h in range(HEADS):
        for u in range(CTL_PARTS):
            to = CTL_AT + CTL_PARTS * h + u
            send[to, 0:IMG, :] = kv[h]
            send[to, IMG:CHUNK, :] = qg[h][CTL_Q * u : CTL_Q * (u + 1)]
    for to in range(CTL_AT + CTL_PARTS * HEADS, BLOCKS):
        send[to] = jnp.zeros((CHUNK, 128), BF16)
    n_t, e_t = n.T, e_ctl.astype(BF16).T
    nz[...] = n_t.reshape(4, SHARE, IMG)
    n_t, e_t = n_t.astype(F32), e_t.astype(F32)
    for y in range(4):
        for j, values in enumerate((n_t, e_t)):
            pieces = [values[SHARE * z + PIECE * y : SHARE * z + PIECE * (y + 1)] for z in range(4)]
            ny[y, j] = jnp.concatenate(pieces, 0).astype(BF16)
    for d, out in enumerate((nz0, nz1, nz2, nz3)):
        out[...] = nz[lax.rem(lax.axis_index("z") + d, 4)]
    for d, out in enumerate((ny0, ny1, ny2, ny3)):
        out[...] = ny[lax.rem(lax.axis_index("y") + d, 4)]


def attention_kernel(role, recv, after, dkv_out, odq, kv, kt, vt, qg, probs, dkv):
    is_main = role[0]
    live = role[1]

    for b in range(BLOCKS):
        kv[IMG * b : IMG * (b + 1), :] = recv[b, 0:IMG, :]

    @pl.when(is_main == 1)
    def _():
        for b in range(BLOCKS):
            kv[IMAGE_KEYS + TXT * b : IMAGE_KEYS + TXT * (b + 1), :] = recv[b, IMG : IMG + TXT, :]
            qg[MAIN_Q * b : MAIN_Q * (b + 1), :] = recv[b, IMG + TXT : CHUNK, :]

    @pl.when(is_main == 0)
    def _():
        kv[IMAGE_KEYS:, :] = jnp.zeros((TEXT_KEYS, 128), BF16)
        for b in range(BLOCKS):
            qg[CTL_Q * b : CTL_Q * (b + 1), :] = recv[b, IMG:CHUNK, :]

    for i in range((IMAGE_KEYS + TEXT_KEYS) // 128):
        block = kv[128 * i : 128 * (i + 1), :].T
        kt[:, 128 * i : 128 * (i + 1)] = block[0:HEAD]
        vt[:, 128 * i : 128 * (i + 1)] = block[HEAD:128]
    dkv[...] = jnp.zeros_like(dkv)
    zeros_half = jnp.zeros((HEAD, TQ), BF16)
    low_lanes = lax.broadcasted_iota(jnp.int32, (TQ, 128), 1) < HEAD

    def q_tile(i, carry):
        q_at = pl.multiple_of(i * TQ, TQ)
        tile = qg[pl.ds(q_at, TQ), :]
        tile_t = tile.T
        g_t = tile_t[HEAD:128].astype(F32)
        q_rhs = jnp.concatenate([tile_t[0:HEAD], zeros_half], 0)
        g_rhs = jnp.concatenate([zeros_half, tile_t[HEAD:128]], 0)
        tile = tile.astype(F32)
        q_only = jnp.where(low_lanes, tile, 0.0).astype(BF16)
        g_only = jnp.where(low_lanes, 0.0, tile).astype(BF16)
        qg_rhs = jnp.concatenate([q_only, g_only], 0)

        def forward(at, state, masked):
            total, o_t = state
            p = jnp.exp(dot(kv[pl.ds(at, TK), :], q_rhs))
            if masked:
                p = jnp.where(lax.broadcasted_iota(jnp.int32, (TK, TQ), 0) < live, p, 0.0)
            probs[pl.ds(at, TK), :] = p
            total = total + jnp.sum(p.reshape(TK // 8, 8, TQ), 0)
            o_t = o_t + dot(vt[:, pl.ds(at, TK)], p.astype(BF16))
            return total, o_t

        state = (jnp.zeros((8, TQ), F32), jnp.zeros((HEAD, TQ), F32))
        state = lax.fori_loop(
            0, IMAGE_KEYS // TK, lambda j, c: forward(pl.multiple_of(j * TK, TK), c, False), state,
            unroll=2,
        )
        total, o_t = lax.fori_loop(0, is_main, lambda j, c: forward(IMAGE_KEYS, c, True), state)
        inverse = 1.0 / jnp.sum(total, axis=0, keepdims=True)
        o_t = (o_t * inverse).astype(BF16).astype(F32)
        delta = jnp.sum(g_t * o_t, axis=0, keepdims=True)

        def backward(at, dq_t):
            p = probs[pl.ds(at, TK), :] * inverse
            ds = (p * (dot(kv[pl.ds(at, TK), :], g_rhs) - delta)).astype(BF16)
            dkv[pl.ds(at, TK), :] += dot(jnp.concatenate([ds, p.astype(BF16)], 1), qg_rhs)
            return dq_t + dot(kt[:, pl.ds(at, TK)], ds)

        dq_t = jnp.zeros((HEAD, TQ), F32)
        dq_t = lax.fori_loop(
            0, IMAGE_KEYS // TK, lambda j, c: backward(pl.multiple_of(j * TK, TK), c), dq_t, unroll=2
        )
        dq_t = lax.fori_loop(0, is_main, lambda j, c: backward(IMAGE_KEYS, c), dq_t)
        odq[pl.ds(q_at, TQ), :] = jnp.concatenate([o_t, dq_t * 0.125], 0).astype(BF16).T
        return carry

    tiles = jnp.where(is_main == 1, BLOCKS * MAIN_Q // TQ, BLOCKS * CTL_Q // TQ)
    lax.fori_loop(0, tiles, q_tile, 0)

    dkv_out[...] = dkv[...].astype(BF16)


def scatter_kernel(role, dkv, odq, after0, after1, after2, after3, after4, out):
    for b in range(BLOCKS):
        out[b, 0:IMG, :] = dkv[IMG * b : IMG * (b + 1), :]

    @pl.when(role[0] == 1)
    def _():
        for b in range(BLOCKS):
            out[b, IMG : IMG + TXT, :] = dkv[IMAGE_KEYS + TXT * b : IMAGE_KEYS + TXT * (b + 1), :]
            out[b, IMG + TXT : CHUNK, :] = odq[MAIN_Q * b : MAIN_Q * (b + 1), :]

    @pl.when(role[0] == 0)
    def _():
        for b in range(BLOCKS):
            out[b, IMG:CHUNK, :] = odq[CTL_Q * b : CTL_Q * (b + 1), :]


def head_norm_back(x, gain, dy):
    inverse = inverse_rms(x)
    dy = dy * gain
    return inverse * dy - x * (inverse * inverse * inverse * jnp.mean(x * dy, axis=-1, keepdims=True))


def head_back(s, at, count, dkv, odq, proj, gains):
    o, dq, dk, dv = [], [], [], []
    for h in range(HEADS):
        x_q = proj[at : at + count, h * HEAD : (h + 1) * HEAD]
        x_k = proj[at : at + count, WIDTH + h * HEAD : WIDTH + (h + 1) * HEAD]
        o.append(odq[h][:, 0:HEAD])
        dq.append(head_norm_back(x_q, gains[s, 0:1, :], odq[h][:, HEAD:128]))
        dk.append(head_norm_back(x_k, gains[s, 1:2, :], dkv[h][:, 0:HEAD]))
        dv.append(dkv[h][:, HEAD:128])
    return [jnp.concatenate(parts, 1).astype(BF16) for parts in (dq, dk, dv, o)]


def head_back_ctl_kernel(recv, proj, gains, by_z, by_y):
    dkv, odq = [], []
    for h in range(HEADS):
        parts = [recv[CTL_AT + CTL_PARTS * h + u].astype(F32) for u in range(CTL_PARTS)]
        dkv.append(parts[0][0:IMG] + parts[1][0:IMG])
        odq.append(jnp.concatenate([parts[0][IMG:], parts[1][IMG:]], 0))
    dq, dk, dv, o = head_back(2, IMG + TXT, IMG, dkv, odq, proj, gains)
    by_z[:, 0:WIDTH] = dq
    by_z[:, WIDTH:] = dk
    by_y[:, 0:WIDTH] = dv
    by_y[:, WIDTH:] = o


def head_back_main(recv, proj, gains, main):
    kv_img, kv_txt, oq_img, oq_txt = [], [], [], []
    for h in range(HEADS):
        parts = [recv[MAIN_PARTS * h + t].astype(F32) for t in range(MAIN_PARTS)]
        kv = parts[0][0 : IMG + TXT] + parts[1][0 : IMG + TXT] + parts[2][0 : IMG + TXT]
        kv_img.append(kv[0:IMG])
        kv_txt.append(kv[IMG:])
        oq_img.append(
            jnp.concatenate(
                [parts[0][IMG + TXT :], parts[1][IMG + TXT :], parts[2][IMG + TXT : CHUNK - TXT]], 0
            )
        )
        oq_txt.append(parts[2][CHUNK - TXT :])
    for j, part in enumerate(head_back(0, 0, IMG, kv_img, oq_img, proj, gains)):
        main[0:IMG, j * WIDTH : (j + 1) * WIDTH] = part
    for j, part in enumerate(head_back(1, IMG, TXT, kv_txt, oq_txt, proj, gains)):
        main[IMG:, j * WIDTH : (j + 1) * WIDTH] = part


def back(s, dq, dk, dv, o, wq, wo, mod, standard, inverse):
    u = dot_nt(dq, wq[0]) + dot_nt(dk, wq[1]) + dot_nt(dv, wq[2])
    u = u * (1.0 + mod[s, 1:2, :])
    u = u - jnp.mean(u, axis=-1, keepdims=True) - standard * jnp.mean(u * standard, axis=-1, keepdims=True)
    return u * inverse, mod[s, 2:3, :] * dot(o, wo[...])


def slab(values):
    return values.astype(BF16).T.reshape(4, SHARE, IMG)


def post_kernel(
    recv, proj, gains, by_z, by_y, xhat, rstd, mod, wq_img, wq_txt, wq_ctl, wo_img, wo_txt, wo_ctl,
    mine0, mine1, theirs0, theirs1, token,
    wq, wo, main, slabs, sems,
):
    token[...] = jnp.zeros_like(token)
    copies = []
    for s, (a, b) in enumerate(((wq_img, wo_img), (wq_txt, wo_txt), (wq_ctl, wo_ctl))):
        copies.append((
            pltpu.make_async_copy(a, wq.at[s], sems.at[s]),
            pltpu.make_async_copy(b, wo.at[s], sems.at[3 + s]),
        ))
    for s in (2, 0, 1):
        copies[s][0].start()
        copies[s][1].start()

    def stream(s, parts, at):
        count = parts[0].shape[0]
        copies[s][0].wait()
        copies[s][1].wait()
        return back(s, *parts, wq.at[s], wo.at[s], mod, xhat[at : at + count, :], rstd[at : at + count, 0:1])

    def joint(at, count):
        return [main[at : at + count, j * WIDTH : (j + 1) * WIDTH] for j in range(4)]

    head_back_main(recv, proj, gains, main)
    u, y_ctl = stream(2, [r[:, j * WIDTH : (j + 1) * WIDTH] for r in (by_z, by_y) for j in range(2)], IMG + TXT)
    slabs[:, 2 * SHARE : 3 * SHARE, :] = slab(u)
    u, y = stream(0, joint(0, IMG), 0)
    slabs[:, SHARE : 2 * SHARE, :] = slab(u)
    slabs[:, 0:SHARE, :] = slab(y + y_ctl)
    u, y = stream(1, joint(IMG, TXT), IMG)
    text = jnp.concatenate([y, u, jnp.zeros((IMG - 2 * TXT, D), F32)], 0).astype(BF16).T.astype(F32)
    for c in range(4):
        slabs[c, 3 * SHARE :, :] = pack_text(text[SHARE * c : SHARE * (c + 1)]).astype(BF16)
    tp = lax.axis_index("tp")
    mine0[...] = slabs[tp]
    mine1[...] = slabs[tp ^ 2]
    theirs0[...] = slabs[tp ^ 1]
    theirs1[...] = slabs[tp ^ 3]


def weight_kernel(
    nz0, nz1, nz2, nz3, ny0, ny1, ny2, ny3, bz0, bz1, bz2, bz3, by0, by1, by2, by3,
    after, out_z, out_y,
):
    nz, ny = (nz0, nz1, nz2, nz3), (ny0, ny1, ny2, ny3)
    bz, by = (bz0, bz1, bz2, bz3), (by0, by1, by2, by3)
    qk = dot(jnp.concatenate([r[...] for r in nz], 1), jnp.concatenate([r[...] for r in bz], 0))
    v = dot(jnp.concatenate([r[0] for r in ny], 1), jnp.concatenate([r[:, 0:WIDTH] for r in by], 0))
    o = dot(jnp.concatenate([r[1] for r in ny], 1), jnp.concatenate([r[:, WIDTH:] for r in by], 0))
    for p in range(4):
        out_z[p] = qk[PIECE * p : PIECE * (p + 1)].astype(BF16)
        out_y[p, :, 0:WIDTH] = v[PIECE * p : PIECE * (p + 1)].astype(BF16)
        out_y[p, :, WIDTH:] = o[PIECE * p : PIECE * (p + 1)].astype(BF16)


def weight_sum_kernel(terms_z, terms_y, mine, theirs):
    half = PIECE // 2
    low = lax.axis_index("w") == 0
    for j, terms in enumerate((terms_z, terms_y)):
        total = terms[0].astype(F32) + terms[1].astype(F32) + terms[2].astype(F32) + terms[3].astype(F32)
        first, second = total[0:half], total[half:]
        columns = slice(2 * WIDTH * j, 2 * WIDTH * (j + 1))
        mine[:, columns] = jnp.where(low, first, second)
        theirs[:, columns] = jnp.where(low, second, first).astype(BF16)


def weight_out_kernel(mine, other, qkv, out):
    for j in range(4):
        columns = slice(WIDTH * j, WIDTH * (j + 1))
        total = mine[:, columns] + other[:, columns].astype(F32)
        if j < 3:
            qkv[j] = total
        else:
            out[...] = total


def final_kernel(img, dy, txt, dy_txt, part0, part1, part2, y_img, d_img, d_ctl, y_txt, d_txt):
    total = part0[...].astype(F32) + part1[...].astype(F32) + part2[...].astype(F32)
    y_img[...] = (img[...].astype(F32) + total[0:SHARE]).astype(BF16)
    d_img[...] = (dy[...].astype(F32) + total[SHARE : 2 * SHARE]).astype(BF16)
    d_ctl[...] = total[2 * SHARE : 3 * SHARE].astype(BF16)
    text = jnp.concatenate([spread_text(total[3 * SHARE :]), jnp.zeros((640 - SHARE, IMG), F32)], 0).T
    y_txt[...] = (txt[...].astype(F32) + text[0:TXT, 0:SHARE]).astype(BF16)
    d_txt[...] = (dy_txt[...].astype(F32) + text[TXT : 2 * TXT, 0:SHARE]).astype(BF16)


def shifted(parts, axis):
    return [parts[0]] + [
        lax.ppermute(parts[d], axis, [(i, (i + d) % 4) for i in range(4)]) for d in (1, 2, 3)
    ]


def per_device(
    img, txt, ctl, dy_img, dy_txt, live_text_length, modulation, query_key_gains,
    w_qkv_img, wo_img, w_qkv_txt, wo_txt, w_qkv_ctl, wo_ctl,
):
    seq = ("z", "y", "w")
    seq_pos = lax.axis_index(seq)
    role = jnp.stack([(seq_pos < CTL_AT).astype(jnp.int32), live_text_length[0]])
    mod, gains = modulation, query_key_gains
    weights = (
        w_qkv_img.transpose(1, 0, 2), w_qkv_txt.transpose(1, 0, 2), w_qkv_ctl.transpose(1, 0, 2),
        wo_img, wo_txt, wo_ctl,
    )
    shape = jax.ShapeDtypeStruct
    rows = shape((ROWS, IMG), BF16)
    other_core = [(i, i ^ 1) for i in range(4)]
    other_chip = [(i, i ^ 2) for i in range(4)]

    own, token = pl.pallas_call(
        pack_kernel,
        out_shape=[rows, shape((8, 128), F32)],
        in_specs=[HBM] * 5,
        out_specs=[VMEM] * 2,
        scratch_shapes=[pltpu.VMEM((2, TXT, SHARE), BF16), pltpu.SemaphoreType.DMA((5,))],
        compiler_params=pltpu.CompilerParams(vmem_limit_bytes=63_400_000),
        name="pack",
    )(img.T, ctl.T, dy_img.T, txt, dy_txt)
    from_chip = lax.ppermute(own, "tp", other_chip)
    from_core = lax.ppermute(own, "tp", other_core)
    *loaded, token = load(weights[0:3], token)
    from_chip = ordered(from_chip, token)
    from_both = lax.ppermute(from_chip, "tp", other_core)

    send, proj, xhat, rstd, *slabs = pl.pallas_call(
        pre_kernel,
        out_shape=[
            shape((BLOCKS, CHUNK, 128), BF16),
            shape((2 * IMG + TXT, 2 * WIDTH), F32),
            shape((2 * IMG + TXT, D), F32),
            shape((2 * IMG + TXT, 128), F32),
        ] + [shape((SHARE, IMG), BF16)] * 4 + [shape((2, SHARE, IMG), BF16)] * 4,
        in_specs=[VMEM] * 12,
        out_specs=[VMEM] * 12,
        scratch_shapes=[
            pltpu.VMEM((4, ROWS, IMG), BF16),
            pltpu.VMEM((4, SHARE, IMG), BF16),
            pltpu.VMEM((4, 2, SHARE, IMG), BF16),
        ],
        compiler_params=params(33),
        name="pre",
    )(own, from_core, from_chip, from_both, mod, gains, *loaded, *weights[3:])

    recv = lax.all_to_all(send, seq, 0, 0, tiled=True)
    nz = shifted(slabs[0:4], "z")
    ny = shifted(slabs[4:8], "y")
    keys = IMAGE_KEYS + TEXT_KEYS
    dkv, odq = pl.pallas_call(
        attention_kernel,
        out_shape=[shape((keys, 128), BF16), shape((BLOCKS * CTL_Q, 128), BF16)],
        in_specs=[SMEM, VMEM, ANY],
        out_specs=[VMEM] * 2,
        scratch_shapes=[
            pltpu.VMEM((keys, 128), BF16),
            pltpu.VMEM((HEAD, keys), BF16),
            pltpu.VMEM((HEAD, keys), BF16),
            pltpu.VMEM((BLOCKS * CTL_Q, 128), BF16),
            pltpu.VMEM((keys, TQ), F32),
            pltpu.VMEM((keys, 128), F32),
        ],
        compiler_params=params(32),
        cost_estimate=pl.CostEstimate(flops=40_000_000_000, bytes_accessed=3_200_000, transcendentals=8_400_000),
        name="attention",
    )(role, recv, nz[3])
    back = pl.pallas_call(
        scatter_kernel,
        out_shape=shape((BLOCKS, CHUNK, 128), BF16),
        in_specs=[SMEM] + [VMEM] * 2 + [ANY] * 5,
        out_specs=VMEM,
        compiler_params=params(16),
        name="scatter",
    )(role, dkv, odq, *nz[1:3], *ny[1:])
    back = lax.all_to_all(back, seq, 0, 0, tiled=True)

    by_z, by_y = pl.pallas_call(
        head_back_ctl_kernel,
        out_shape=[shape((IMG, 2 * WIDTH), BF16)] * 2,
        in_specs=[VMEM] * 3,
        out_specs=[VMEM] * 2,
        compiler_params=params(16),
        name="head_back_ctl",
    )(back, proj, gains)
    blocks_z = shifted([by_z] * 4, "z")
    blocks_y = shifted([by_y] * 4, "y")
    mine0, mine1, theirs0, theirs1, token = pl.pallas_call(
        post_kernel,
        out_shape=[rows] * 4 + [shape((8, 128), F32)],
        in_specs=[VMEM] * 8 + [HBM] * 6,
        out_specs=[VMEM] * 5,
        scratch_shapes=[
            pltpu.VMEM((3, 3, D, WIDTH), BF16),
            pltpu.VMEM((3, WIDTH, D), BF16),
            pltpu.VMEM((IMG + TXT, 4 * WIDTH), BF16),
            pltpu.VMEM((4, ROWS, IMG), BF16),
            pltpu.SemaphoreType.DMA((6,)),
        ],
        compiler_params=params(54),
        cost_estimate=pl.CostEstimate(flops=14_000_000_000, bytes_accessed=30_000_000, transcendentals=0),
        name="post",
    )(back, proj, gains, by_z, by_y, xhat, rstd, mod, *weights)
    got1 = lax.ppermute(theirs1, "tp", other_core)
    got0 = lax.ppermute(theirs0, "tp", other_core)
    passed = (mine1.astype(F32) + got1.astype(F32)).astype(BF16)
    passed = lax.ppermute(passed, "tp", other_chip)

    terms_z, terms_y = pl.pallas_call(
        weight_kernel,
        out_shape=[shape((4, PIECE, 2 * WIDTH), BF16)] * 2,
        in_specs=[VMEM] * 16 + [ANY],
        out_specs=[VMEM] * 2,
        compiler_params=params(20),
        cost_estimate=pl.CostEstimate(flops=3_000_000_000, bytes_accessed=5_000_000, transcendentals=0),
        name="weight",
    )(*nz, *ny, *blocks_z, *blocks_y, token)
    terms_z = lax.all_to_all(terms_z, "y", 0, 0, tiled=True)
    terms_y = lax.all_to_all(terms_y, "z", 0, 0, tiled=True)
    mine, theirs = pl.pallas_call(
        weight_sum_kernel,
        out_shape=[shape((PIECE // 2, 4 * WIDTH), F32), shape((PIECE // 2, 4 * WIDTH), BF16)],
        in_specs=[VMEM] * 2,
        out_specs=[VMEM] * 2,
        compiler_params=params(16),
        name="weight_sum",
    )(terms_z, terms_y)
    theirs = lax.ppermute(theirs, "w", [(0, 1), (1, 0)])
    grad_qkv, grad_out = pl.pallas_call(
        weight_out_kernel,
        out_shape=[shape((3, PIECE // 2, WIDTH), F32), shape((PIECE // 2, WIDTH), F32)],
        in_specs=[VMEM] * 2,
        out_specs=[VMEM] * 2,
        compiler_params=params(16),
        name="weight_out",
    )(mine, theirs)

    y_img, d_img, d_ctl, y_txt, d_txt = pl.pallas_call(
        final_kernel,
        out_shape=[shape((SHARE, IMG), BF16)] * 3 + [shape((TXT, SHARE), BF16)] * 2,
        in_specs=[VMEM] * 7,
        out_specs=[VMEM] * 5,
        compiler_params=params(16),
        name="final",
    )(img.T, dy_img.T, txt, dy_txt, mine0, got0, passed)
    return y_img.T, y_txt, d_img.T, d_txt, d_ctl.T, grad_qkv.transpose(1, 0, 2), grad_out.T


def solution(mesh):
    fine = Mesh(mesh.devices.reshape(4, 4, 2, 4), ("z", "y", "w", "tp"))
    seq = ("z", "y", "w")
    rows = P(seq, "tp")
    qkv = P(None, None, "tp")
    out = P("tp", None)
    in_specs = (rows,) * 5 + (P(), P(), P(), qkv, out, qkv, out, qkv, out)
    out_specs = (rows,) * 5 + (P(seq, None, "tp"), P("tp", seq))
    return jax.shard_map(
        per_device, mesh=fine, in_specs=in_specs, out_specs=out_specs, check_vma=False
    )
```

```python
import jax
import jax.numpy as jnp
from jax import lax
from jax.experimental import pallas as pl
from jax.experimental.pallas import tpu as pltpu
from jax.sharding import Mesh, PartitionSpec as P

EPS = 1e-06
HEAD = 64
HEADS = 6
WIDTH = HEADS * HEAD
D = 2432
SHARE = 608
PIECE = 152
ROWS = 3 * SHARE + PIECE
IMG = 128
TXT = 16
BLOCKS = 32
CHUNK = 192
IMAGE_KEYS = BLOCKS * IMG
TEXT_KEYS = BLOCKS * TXT
MAIN_Q = 48
CTL_Q = 64
MAIN_PARTS = 3
CTL_PARTS = 2
CTL_AT = HEADS * MAIN_PARTS
TQ = 512
TK = 512
F32 = jnp.float32
BF16 = jnp.bfloat16
NT = (((1,), (1,)), ((), ()))
VMEM = pl.BlockSpec(memory_space=pltpu.VMEM)
SMEM = pl.BlockSpec(memory_space=pltpu.SMEM)
ANY = pl.BlockSpec(memory_space=pl.ANY)
HBM = pl.BlockSpec(memory_space=pltpu.HBM)


def params(mib):
    return pltpu.CompilerParams(vmem_limit_bytes=mib * 1024 * 1024)


def dot(a, b):
    return jnp.dot(a, b, preferred_element_type=F32)


def dot_nt(a, b):
    return lax.dot_general(a, b, NT, preferred_element_type=F32)


def head(values, h):
    return values[:, h * HEAD : (h + 1) * HEAD]


def inverse_rms(values):
    return lax.rsqrt(jnp.mean(values * values, axis=-1, keepdims=True) + EPS)


def spread_text(packed):
    return jnp.concatenate([packed] + [pltpu.roll(packed, 128 - 32 * a, 1) for a in (1, 2, 3)], 0)


def pack_text(columns):
    pieces = [columns[PIECE * a : PIECE * (a + 1)] for a in range(4)]
    return pieces[0] + sum(pltpu.roll(pieces[a], 32 * a, 1) for a in (1, 2, 3))


def weight_copies(sources, wq, wo, sems):
    return [
        (
            pltpu.make_async_copy(sources[s], wq.at[s], sems.at[s]),
            pltpu.make_async_copy(sources[3 + s], wo.at[s], sems.at[3 + s]),
        )
        for s in range(3)
    ]


def pack_kernel(img, ctl, dy, txt, dy_txt, out, text_rows, sems):
    copies = [
        pltpu.make_async_copy(part, text_rows.at[i], sems.at[3 + i]) for i, part in enumerate((txt, dy_txt))
    ] + [
        pltpu.make_async_copy(part, out.at[pl.ds(SHARE * i, SHARE)], sems.at[i])
        for i, part in enumerate((img, ctl, dy))
    ]
    for copy in copies:
        copy.start()
    copies[0].wait()
    copies[1].wait()
    text = text_rows[...].reshape(2 * TXT, SHARE).astype(F32)
    text = jnp.concatenate([text, jnp.zeros((IMG - 2 * TXT, SHARE), F32)], 0)
    text = jnp.concatenate([text, jnp.zeros((IMG, 640 - SHARE), F32)], 1)
    out[3 * SHARE :, :] = pack_text(text.T).astype(BF16)
    for copy in copies[2:]:
        copy.wait()


def pre_kernel(
    in0, in1, in2, in3, mod, gains, wq_img, wq_txt, wq_ctl, wo_img, wo_txt, wo_ctl,
    send, proj, xhat, rstd, nz0, nz1, nz2, nz3, ny0, ny1, ny2, ny3,
    wq, wo, gat, nz, ny, sems,
):
    copies = weight_copies((wq_img, wq_txt, wq_ctl, wo_img, wo_txt, wo_ctl), wq, wo, sems)
    copies[0][0].start()

    for i, part in enumerate((in0, in1, in2, in3)):
        gat[lax.axis_index("tp") ^ i] = part[...]

    def rows(slab):
        return gat[:, SHARE * slab : SHARE * (slab + 1), :].reshape(D, IMG).T.astype(F32)

    def stream(s, x, e, at, later):
        count = x.shape[0]
        centered = x - jnp.mean(x, axis=-1, keepdims=True)
        inverse = lax.rsqrt(jnp.mean(centered * centered, axis=-1, keepdims=True) + EPS)
        standard = centered * inverse
        xhat[at : at + count, :] = standard
        rstd[at : at + count, :] = jnp.broadcast_to(inverse, (count, 128))
        n = (standard * (1.0 + mod[s, 1:2, :]) + mod[s, 0:1, :]).astype(BF16)
        copies[s][0].wait()
        copies[s][1].start()
        if later is not None:
            copies[later][0].start()
        pq = dot(n, wq[s, 0])
        pk = dot(n, wq[s, 1])
        pv = dot(n, wq[s, 2])
        proj[at : at + count, 0:WIDTH] = pq
        proj[at : at + count, WIDTH : 2 * WIDTH] = pk
        copies[s][1].wait()
        g = dot_nt(e, wo[s])
        kv, qg = [], []
        for h in range(HEADS):
            q_h, k_h = head(pq, h), head(pk, h)
            q_h = q_h * inverse_rms(q_h) * (gains[s, 0:1, :] * 0.125)
            k_h = k_h * inverse_rms(k_h) * gains[s, 1:2, :]
            kv.append(jnp.concatenate([k_h, head(pv, h)], 1).astype(BF16))
            qg.append(jnp.concatenate([q_h, head(g, h)], 1).astype(BF16))
        return n, kv, qg

    dy = rows(2)
    text = jnp.concatenate([spread_text(gat[c, 3 * SHARE :, :].astype(F32)) for c in range(4)], 0).astype(BF16).T.astype(F32)
    e_img = (mod[0, 2:3, :] * dy).astype(BF16)
    n, kv, qg = stream(0, rows(0), e_img, 0, 2)
    for h in range(HEADS):
        for t in range(MAIN_PARTS):
            to = MAIN_PARTS * h + t
            send[to, 0:IMG, :] = kv[h]
            last = min(IMG, MAIN_Q * (t + 1))
            send[to, IMG + TXT : IMG + TXT + last - MAIN_Q * t, :] = qg[h][MAIN_Q * t : last]
    e_ctl = mod[2, 2:3, :] * dy
    n, kv, qg = stream(2, rows(1), e_ctl.astype(BF16), IMG + TXT, 1)
    for h in range(HEADS):
        for u in range(CTL_PARTS):
            to = CTL_AT + CTL_PARTS * h + u
            send[to, 0:IMG, :] = kv[h]
            send[to, IMG:CHUNK, :] = qg[h][CTL_Q * u : CTL_Q * (u + 1)]
    e_txt = (mod[1, 2:3, :] * text[TXT : 2 * TXT]).astype(BF16)
    unused, kv, qg = stream(1, text[0:TXT], e_txt, IMG, None)
    for h in range(HEADS):
        for t in range(MAIN_PARTS):
            send[MAIN_PARTS * h + t, IMG : IMG + TXT, :] = kv[h]
        send[MAIN_PARTS * h + 2, CHUNK - TXT : CHUNK, :] = qg[h]
    for to in range(CTL_AT + CTL_PARTS * HEADS, BLOCKS):
        send[to] = jnp.zeros((CHUNK, 128), BF16)
    n_t, e_t = n.T, e_ctl.astype(BF16).T
    nz[...] = n_t.reshape(4, SHARE, IMG)
    n_t, e_t = n_t.astype(F32), e_t.astype(F32)
    for y in range(4):
        for j, values in enumerate((n_t, e_t)):
            pieces = [values[SHARE * z + PIECE * y : SHARE * z + PIECE * (y + 1)] for z in range(4)]
            ny[y, j] = jnp.concatenate(pieces, 0).astype(BF16)
    for d, out in enumerate((nz0, nz1, nz2, nz3)):
        out[...] = nz[lax.rem(lax.axis_index("z") + d, 4)]
    for d, out in enumerate((ny0, ny1, ny2, ny3)):
        out[...] = ny[lax.rem(lax.axis_index("y") + d, 4)]


def attention_kernel(role, recv, after, dkv_out, odq, kv, kt, vt, qg, probs, dkv):
    is_main = role[0]
    live = role[1]

    for b in range(BLOCKS):
        kv[IMG * b : IMG * (b + 1), :] = recv[b, 0:IMG, :]

    @pl.when(is_main == 1)
    def _():
        for b in range(BLOCKS):
            kv[IMAGE_KEYS + TXT * b : IMAGE_KEYS + TXT * (b + 1), :] = recv[b, IMG : IMG + TXT, :]
            qg[MAIN_Q * b : MAIN_Q * (b + 1), :] = recv[b, IMG + TXT : CHUNK, :]

    @pl.when(is_main == 0)
    def _():
        kv[IMAGE_KEYS:, :] = jnp.zeros((TEXT_KEYS, 128), BF16)
        for b in range(BLOCKS):
            qg[CTL_Q * b : CTL_Q * (b + 1), :] = recv[b, IMG:CHUNK, :]

    for i in range((IMAGE_KEYS + TEXT_KEYS) // 128):
        block = kv[128 * i : 128 * (i + 1), :].T
        kt[:, 128 * i : 128 * (i + 1)] = block[0:HEAD]
        vt[:, 128 * i : 128 * (i + 1)] = block[HEAD:128]
    dkv[...] = jnp.zeros_like(dkv)
    zeros_half = jnp.zeros((HEAD, TQ), BF16)
    low_lanes = lax.broadcasted_iota(jnp.int32, (TQ, 128), 1) < HEAD

    def q_tile(i, carry):
        q_at = pl.multiple_of(i * TQ, TQ)
        tile = qg[pl.ds(q_at, TQ), :]
        tile_t = tile.T
        g_t = tile_t[HEAD:128].astype(F32)
        q_rhs = jnp.concatenate([tile_t[0:HEAD], zeros_half], 0)
        g_rhs = jnp.concatenate([zeros_half, tile_t[HEAD:128]], 0)
        tile = tile.astype(F32)
        q_only = jnp.where(low_lanes, tile, 0.0).astype(BF16)
        g_only = jnp.where(low_lanes, 0.0, tile).astype(BF16)
        qg_rhs = jnp.concatenate([q_only, g_only], 0)

        def forward(at, state, masked):
            total, o_t = state
            p = jnp.exp(dot(kv[pl.ds(at, TK), :], q_rhs))
            if masked:
                p = jnp.where(lax.broadcasted_iota(jnp.int32, (TK, TQ), 0) < live, p, 0.0)
            probs[pl.ds(at, TK), :] = p
            total = total + jnp.sum(p.reshape(TK // 8, 8, TQ), 0)
            o_t = o_t + dot(vt[:, pl.ds(at, TK)], p.astype(BF16))
            return total, o_t

        state = (jnp.zeros((8, TQ), F32), jnp.zeros((HEAD, TQ), F32))
        state = lax.fori_loop(
            0, IMAGE_KEYS // TK, lambda j, c: forward(pl.multiple_of(j * TK, TK), c, False), state,
            unroll=4,
        )
        total, o_t = lax.fori_loop(0, is_main, lambda j, c: forward(IMAGE_KEYS, c, True), state)
        inverse = 1.0 / jnp.sum(total, axis=0, keepdims=True)
        o_t = (o_t * inverse).astype(BF16).astype(F32)
        delta = jnp.sum(g_t * o_t, axis=0, keepdims=True)

        def backward(at, dq_t):
            p = probs[pl.ds(at, TK), :] * inverse
            ds = (p * (dot(kv[pl.ds(at, TK), :], g_rhs) - delta)).astype(BF16)
            dkv[pl.ds(at, TK), :] += dot(jnp.concatenate([ds, p.astype(BF16)], 1), qg_rhs)
            return dq_t + dot(kt[:, pl.ds(at, TK)], ds)

        dq_t = jnp.zeros((HEAD, TQ), F32)
        dq_t = lax.fori_loop(
            0, IMAGE_KEYS // TK, lambda j, c: backward(pl.multiple_of(j * TK, TK), c), dq_t, unroll=4
        )
        dq_t = lax.fori_loop(0, is_main, lambda j, c: backward(IMAGE_KEYS, c), dq_t)
        odq[pl.ds(q_at, TQ), :] = jnp.concatenate([o_t, dq_t * 0.125], 0).astype(BF16).T
        return carry

    tiles = jnp.where(is_main == 1, BLOCKS * MAIN_Q // TQ, BLOCKS * CTL_Q // TQ)
    lax.fori_loop(0, tiles, q_tile, 0)

    dkv_out[...] = dkv[...].astype(BF16)


def scatter_kernel(role, dkv, odq, after0, after1, after2, after3, after4, out):
    for b in range(BLOCKS):
        out[b, 0:IMG, :] = dkv[IMG * b : IMG * (b + 1), :]

    @pl.when(role[0] == 1)
    def _():
        for b in range(BLOCKS):
            out[b, IMG : IMG + TXT, :] = dkv[IMAGE_KEYS + TXT * b : IMAGE_KEYS + TXT * (b + 1), :]
            out[b, IMG + TXT : CHUNK, :] = odq[MAIN_Q * b : MAIN_Q * (b + 1), :]

    @pl.when(role[0] == 0)
    def _():
        for b in range(BLOCKS):
            out[b, IMG:CHUNK, :] = odq[CTL_Q * b : CTL_Q * (b + 1), :]


def head_norm_back(x, gain, dy):
    inverse = inverse_rms(x)
    dy = dy * gain
    return inverse * dy - x * (inverse * inverse * inverse * jnp.mean(x * dy, axis=-1, keepdims=True))


def head_back(s, at, count, dkv, odq, proj, gains):
    o, dq, dk, dv = [], [], [], []
    for h in range(HEADS):
        x_q = proj[at : at + count, h * HEAD : (h + 1) * HEAD]
        x_k = proj[at : at + count, WIDTH + h * HEAD : WIDTH + (h + 1) * HEAD]
        o.append(odq[h][:, 0:HEAD])
        dq.append(head_norm_back(x_q, gains[s, 0:1, :], odq[h][:, HEAD:128]))
        dk.append(head_norm_back(x_k, gains[s, 1:2, :], dkv[h][:, 0:HEAD]))
        dv.append(dkv[h][:, HEAD:128])
    return [jnp.concatenate(parts, 1).astype(BF16) for parts in (dq, dk, dv, o)]


def head_back_ctl_kernel(recv, proj, gains, by_z, by_y):
    dkv, odq = [], []
    for h in range(HEADS):
        parts = [recv[CTL_AT + CTL_PARTS * h + u].astype(F32) for u in range(CTL_PARTS)]
        dkv.append(parts[0][0:IMG] + parts[1][0:IMG])
        odq.append(jnp.concatenate([parts[0][IMG:], parts[1][IMG:]], 0))
    dq, dk, dv, o = head_back(2, IMG + TXT, IMG, dkv, odq, proj, gains)
    by_z[:, 0:WIDTH] = dq
    by_z[:, WIDTH:] = dk
    by_y[:, 0:WIDTH] = dv
    by_y[:, WIDTH:] = o


def head_back_main(recv, proj, gains, main):
    kv_img, kv_txt, oq_img, oq_txt = [], [], [], []
    for h in range(HEADS):
        parts = [recv[MAIN_PARTS * h + t].astype(F32) for t in range(MAIN_PARTS)]
        kv = parts[0][0 : IMG + TXT] + parts[1][0 : IMG + TXT] + parts[2][0 : IMG + TXT]
        kv_img.append(kv[0:IMG])
        kv_txt.append(kv[IMG:])
        oq_img.append(
            jnp.concatenate(
                [parts[0][IMG + TXT :], parts[1][IMG + TXT :], parts[2][IMG + TXT : CHUNK - TXT]], 0
            )
        )
        oq_txt.append(parts[2][CHUNK - TXT :])
    for j, part in enumerate(head_back(0, 0, IMG, kv_img, oq_img, proj, gains)):
        main[0:IMG, j * WIDTH : (j + 1) * WIDTH] = part
    for j, part in enumerate(head_back(1, IMG, TXT, kv_txt, oq_txt, proj, gains)):
        main[IMG:, j * WIDTH : (j + 1) * WIDTH] = part


def back(s, dq, dk, dv, o, wq, wo, mod, standard, inverse):
    u = dot_nt(dq, wq[0]) + dot_nt(dk, wq[1]) + dot_nt(dv, wq[2])
    u = u * (1.0 + mod[s, 1:2, :])
    u = u - jnp.mean(u, axis=-1, keepdims=True) - standard * jnp.mean(u * standard, axis=-1, keepdims=True)
    return u * inverse, mod[s, 2:3, :] * dot(o, wo[...])


def slab(values):
    return values.astype(BF16).T.reshape(4, SHARE, IMG)


def post_kernel(
    recv, proj, gains, by_z, by_y, xhat, rstd, mod, wq_img, wq_txt, wq_ctl, wo_img, wo_txt, wo_ctl,
    slabs,
    wq, wo, main, sems,
):
    copies = weight_copies((wq_img, wq_txt, wq_ctl, wo_img, wo_txt, wo_ctl), wq, wo, sems)
    for copy in (copies[2][0], copies[2][1], copies[0][0]):
        copy.start()

    def stream(s, parts, at, later):
        count = parts[0].shape[0]
        copies[s][0].wait()
        copies[s][1].wait()
        for copy in later:
            copy.start()
        return back(s, *parts, wq.at[s], wo.at[s], mod, xhat[at : at + count, :], rstd[at : at + count, 0:1])

    def joint(at, count):
        return [main[at : at + count, j * WIDTH : (j + 1) * WIDTH] for j in range(4)]

    head_back_main(recv, proj, gains, main)
    u, y_ctl = stream(2, [r[:, j * WIDTH : (j + 1) * WIDTH] for r in (by_z, by_y) for j in range(2)], IMG + TXT, (copies[0][1], copies[1][0]))
    slabs[:, 2 * SHARE : 3 * SHARE, :] = slab(u)
    u, y = stream(0, joint(0, IMG), 0, (copies[1][1],))
    slabs[:, SHARE : 2 * SHARE, :] = slab(u)
    slabs[:, 0:SHARE, :] = slab(y + y_ctl)
    u, y = stream(1, joint(IMG, TXT), IMG, ())
    text = jnp.concatenate([y, u, jnp.zeros((IMG - 2 * TXT, D), F32)], 0).astype(BF16).T.astype(F32)
    for c in range(4):
        slabs[c, 3 * SHARE :, :] = pack_text(text[SHARE * c : SHARE * (c + 1)]).astype(BF16)


def weight_kernel(
    nz0, nz1, nz2, nz3, ny0, ny1, ny2, ny3, bz0, bz1, bz2, bz3, by0, by1, by2, by3,
    slabs, out_z, out_y0, out_y1, out_y2, out_y3, mine0, mine1, theirs0, theirs1,
    chunks,
):
    tp = lax.axis_index("tp")
    mine0[...] = slabs[tp]
    mine1[...] = slabs[tp ^ 2]
    theirs0[...] = slabs[tp ^ 1]
    theirs1[...] = slabs[tp ^ 3]
    nz, ny = (nz0, nz1, nz2, nz3), (ny0, ny1, ny2, ny3)
    bz, by = (bz0, bz1, bz2, bz3), (by0, by1, by2, by3)
    qk = dot(jnp.concatenate([r[...] for r in nz], 1), jnp.concatenate([r[...] for r in bz], 0))
    v = dot(jnp.concatenate([r[0] for r in ny], 1), jnp.concatenate([r[:, 0:WIDTH] for r in by], 0))
    o = dot(jnp.concatenate([r[1] for r in ny], 1), jnp.concatenate([r[:, WIDTH:] for r in by], 0))
    for p in range(4):
        out_z[p] = qk[PIECE * p : PIECE * (p + 1)].astype(BF16)
        chunks[p, :, 0:WIDTH] = v[PIECE * p : PIECE * (p + 1)].astype(BF16)
        chunks[p, :, WIDTH:] = o[PIECE * p : PIECE * (p + 1)].astype(BF16)
    for d, out in enumerate((out_y0, out_y1, out_y2, out_y3)):
        out[...] = chunks[lax.rem(lax.axis_index("z") + d, 4)]


def weight_sum_kernel(terms_z, y0, y1, y2, y3, mine, theirs):
    half = PIECE // 2
    low = lax.axis_index("w") == 0
    for j, terms in enumerate(([terms_z[p] for p in range(4)], [y0[...], y1[...], y2[...], y3[...]])):
        total = sum(term.astype(F32) for term in terms)
        first, second = total[0:half], total[half:]
        columns = slice(2 * WIDTH * j, 2 * WIDTH * (j + 1))
        mine[:, columns] = jnp.where(low, first, second)
        theirs[:, columns] = jnp.where(low, second, first).astype(BF16)


def weight_out_kernel(mine, other, qkv, out):
    for j in range(4):
        columns = slice(WIDTH * j, WIDTH * (j + 1))
        total = mine[:, columns] + other[:, columns].astype(F32)
        if j < 3:
            qkv[j] = total
        else:
            out[...] = total


def final_kernel(img, dy, txt, dy_txt, part0, part1, part2, y_img, d_img, d_ctl, y_txt, d_txt):
    total = part0[...].astype(F32) + part1[...].astype(F32) + part2[...].astype(F32)
    y_img[...] = (img[...].astype(F32) + total[0:SHARE]).astype(BF16)
    d_img[...] = (dy[...].astype(F32) + total[SHARE : 2 * SHARE]).astype(BF16)
    d_ctl[...] = total[2 * SHARE : 3 * SHARE].astype(BF16)
    text = jnp.concatenate([spread_text(total[3 * SHARE :]), jnp.zeros((640 - SHARE, IMG), F32)], 0).T
    y_txt[...] = (txt[...].astype(F32) + text[0:TXT, 0:SHARE]).astype(BF16)
    d_txt[...] = (dy_txt[...].astype(F32) + text[TXT : 2 * TXT, 0:SHARE]).astype(BF16)


def shifted(parts, axis):
    return [parts[0]] + [
        lax.ppermute(parts[d], axis, [(i, (i + d) % 4) for i in range(4)]) for d in (1, 2, 3)
    ]


def per_device(
    img, txt, ctl, dy_img, dy_txt, live_text_length, modulation, query_key_gains,
    w_qkv_img, wo_img, w_qkv_txt, wo_txt, w_qkv_ctl, wo_ctl,
):
    seq = ("z", "y", "w")
    seq_pos = lax.axis_index(seq)
    role = jnp.stack([(seq_pos < CTL_AT).astype(jnp.int32), live_text_length[0]])
    mod, gains = modulation, query_key_gains
    weights = (
        w_qkv_img.transpose(1, 0, 2), w_qkv_txt.transpose(1, 0, 2), w_qkv_ctl.transpose(1, 0, 2),
        wo_img, wo_txt, wo_ctl,
    )
    shape = jax.ShapeDtypeStruct
    rows = shape((ROWS, IMG), BF16)
    other_core = [(i, i ^ 1) for i in range(4)]
    other_chip = [(i, i ^ 2) for i in range(4)]

    own = pl.pallas_call(
        pack_kernel,
        out_shape=rows,
        in_specs=[HBM] * 5,
        out_specs=VMEM,
        scratch_shapes=[pltpu.VMEM((2, TXT, SHARE), BF16), pltpu.SemaphoreType.DMA((5,))],
        compiler_params=pltpu.CompilerParams(vmem_limit_bytes=63_400_000),
        name="pack",
    )(img.T, ctl.T, dy_img.T, txt, dy_txt)
    from_chip = lax.ppermute(own, "tp", other_chip)
    from_core = lax.ppermute(own, "tp", other_core)
    from_both = lax.ppermute(from_chip, "tp", other_core)

    send, proj, xhat, rstd, *slabs = pl.pallas_call(
        pre_kernel,
        out_shape=[
            shape((BLOCKS, CHUNK, 128), BF16),
            shape((2 * IMG + TXT, 2 * WIDTH), F32),
            shape((2 * IMG + TXT, D), F32),
            shape((2 * IMG + TXT, 128), F32),
        ] + [shape((SHARE, IMG), BF16)] * 4 + [shape((2, SHARE, IMG), BF16)] * 4,
        in_specs=[VMEM] * 6 + [HBM] * 6,
        out_specs=[VMEM] * 12,
        scratch_shapes=[
            pltpu.VMEM((3, 3, D, WIDTH), BF16),
            pltpu.VMEM((3, WIDTH, D), BF16),
            pltpu.VMEM((4, ROWS, IMG), BF16),
            pltpu.VMEM((4, SHARE, IMG), BF16),
            pltpu.VMEM((4, 2, SHARE, IMG), BF16),
            pltpu.SemaphoreType.DMA((6,)),
        ],
        compiler_params=params(56),
        name="pre",
    )(own, from_core, from_chip, from_both, mod, gains, *weights)

    recv = lax.all_to_all(send, seq, 0, 0, tiled=True)
    nz = shifted(slabs[0:4], "z")
    ny = shifted(slabs[4:8], "y")
    keys = IMAGE_KEYS + TEXT_KEYS
    dkv, odq = pl.pallas_call(
        attention_kernel,
        out_shape=[shape((keys, 128), BF16), shape((BLOCKS * CTL_Q, 128), BF16)],
        in_specs=[SMEM, VMEM, ANY],
        out_specs=[VMEM] * 2,
        scratch_shapes=[
            pltpu.VMEM((keys, 128), BF16),
            pltpu.VMEM((HEAD, keys), BF16),
            pltpu.VMEM((HEAD, keys), BF16),
            pltpu.VMEM((BLOCKS * CTL_Q, 128), BF16),
            pltpu.VMEM((keys, TQ), F32),
            pltpu.VMEM((keys, 128), F32),
        ],
        compiler_params=params(32),
        cost_estimate=pl.CostEstimate(flops=40_000_000_000, bytes_accessed=3_200_000, transcendentals=8_400_000),
        name="attention",
    )(role, recv, nz[3])
    back = pl.pallas_call(
        scatter_kernel,
        out_shape=shape((BLOCKS, CHUNK, 128), BF16),
        in_specs=[SMEM] + [VMEM] * 2 + [ANY] * 5,
        out_specs=VMEM,
        compiler_params=params(16),
        name="scatter",
    )(role, dkv, odq, *nz[1:3], *ny[1:])
    back = lax.all_to_all(back, seq, 0, 0, tiled=True)

    by_z, by_y = pl.pallas_call(
        head_back_ctl_kernel,
        out_shape=[shape((IMG, 2 * WIDTH), BF16)] * 2,
        in_specs=[VMEM] * 3,
        out_specs=[VMEM] * 2,
        compiler_params=params(16),
        name="head_back_ctl",
    )(back, proj, gains)
    blocks_z = shifted([by_z] * 4, "z")
    blocks_y = shifted([by_y] * 4, "y")
    slabs = pl.pallas_call(
        post_kernel,
        out_shape=shape((4, ROWS, IMG), BF16),
        in_specs=[VMEM] * 8 + [HBM] * 6,
        out_specs=VMEM,
        scratch_shapes=[
            pltpu.VMEM((3, 3, D, WIDTH), BF16),
            pltpu.VMEM((3, WIDTH, D), BF16),
            pltpu.VMEM((IMG + TXT, 4 * WIDTH), BF16),
            pltpu.SemaphoreType.DMA((6,)),
        ],
        compiler_params=params(54),
        cost_estimate=pl.CostEstimate(flops=14_000_000_000, bytes_accessed=30_000_000, transcendentals=0),
        name="post",
    )(back, proj, gains, by_z, by_y, xhat, rstd, mod, *weights)
    terms_z, *outs = pl.pallas_call(
        weight_kernel,
        out_shape=[shape((4, PIECE, 2 * WIDTH), BF16)] + [shape((PIECE, 2 * WIDTH), BF16)] * 4 + [rows] * 4,
        in_specs=[VMEM] * 17,
        out_specs=[VMEM] * 9,
        scratch_shapes=[pltpu.VMEM((4, PIECE, 2 * WIDTH), BF16)],
        compiler_params=params(24),
        cost_estimate=pl.CostEstimate(flops=3_000_000_000, bytes_accessed=5_000_000, transcendentals=0),
        name="weight",
    )(*nz, *ny, *blocks_z, *blocks_y, slabs)
    terms_y, (mine0, mine1, theirs0, theirs1) = outs[0:4], outs[4:8]
    got1 = lax.ppermute(theirs1, "tp", other_core)
    got0 = lax.ppermute(theirs0, "tp", other_core)
    passed = (mine1.astype(F32) + got1.astype(F32)).astype(BF16)
    passed = lax.ppermute(passed, "tp", other_chip)
    terms_y = shifted(terms_y, "z")
    terms_z = lax.all_to_all(terms_z, "y", 0, 0, tiled=True)
    mine, theirs = pl.pallas_call(
        weight_sum_kernel,
        out_shape=[shape((PIECE // 2, 4 * WIDTH), F32), shape((PIECE // 2, 4 * WIDTH), BF16)],
        in_specs=[VMEM] * 5,
        out_specs=[VMEM] * 2,
        compiler_params=params(16),
        name="weight_sum",
    )(terms_z, *terms_y)
    theirs = lax.ppermute(theirs, "w", [(0, 1), (1, 0)])
    grad_qkv, grad_out = pl.pallas_call(
        weight_out_kernel,
        out_shape=[shape((3, PIECE // 2, WIDTH), F32), shape((PIECE // 2, WIDTH), F32)],
        in_specs=[VMEM] * 2,
        out_specs=[VMEM] * 2,
        compiler_params=params(16),
        name="weight_out",
    )(mine, theirs)

    y_img, d_img, d_ctl, y_txt, d_txt = pl.pallas_call(
        final_kernel,
        out_shape=[shape((SHARE, IMG), BF16)] * 3 + [shape((TXT, SHARE), BF16)] * 2,
        in_specs=[VMEM] * 7,
        out_specs=[VMEM] * 5,
        compiler_params=params(16),
        name="final",
    )(img.T, dy_img.T, txt, dy_txt, mine0, got0, passed)
    return y_img.T, y_txt, d_img.T, d_txt, d_ctl.T, grad_qkv.transpose(1, 0, 2), grad_out.T


def solution(mesh):
    fine = Mesh(mesh.devices.reshape(4, 4, 2, 4), ("z", "y", "w", "tp"))
    seq = ("z", "y", "w")
    rows = P(seq, "tp")
    qkv = P(None, None, "tp")
    out = P("tp", None)
    in_specs = (rows,) * 5 + (P(), P(), P(), qkv, out, qkv, out, qkv, out)
    out_specs = (rows,) * 5 + (P(seq, None, "tp"), P("tp", seq))
    return jax.shard_map(
        per_device, mesh=fine, in_specs=in_specs, out_specs=out_specs, check_vma=False
    )
```

```python
import jax
import jax.numpy as jnp
from jax import lax
from jax.experimental import pallas as pl
from jax.experimental.pallas import tpu as pltpu
from jax.sharding import Mesh, PartitionSpec as P

EPS = 1e-06
HEAD = 64
HEADS = 6
WIDTH = HEADS * HEAD
D = 2432
SHARE = 608
PIECE = 152
ROWS = 3 * SHARE + PIECE
IMG = 128
TXT = 16
BLOCKS = 32
CHUNK = 192
IMAGE_KEYS = BLOCKS * IMG
TEXT_KEYS = BLOCKS * TXT
MAIN_Q = 48
CTL_Q = 64
MAIN_PARTS = 3
CTL_PARTS = 2
CTL_AT = HEADS * MAIN_PARTS
TQ = 512
TK = 512
F32 = jnp.float32
BF16 = jnp.bfloat16
NT = (((1,), (1,)), ((), ()))
VMEM = pl.BlockSpec(memory_space=pltpu.VMEM)
SMEM = pl.BlockSpec(memory_space=pltpu.SMEM)
ANY = pl.BlockSpec(memory_space=pl.ANY)
HBM = pl.BlockSpec(memory_space=pltpu.HBM)


def params(mib):
    return pltpu.CompilerParams(vmem_limit_bytes=mib * 1024 * 1024)


def dot(a, b):
    return jnp.dot(a, b, preferred_element_type=F32)


def dot_nt(a, b):
    return lax.dot_general(a, b, NT, preferred_element_type=F32)


def head(values, h):
    return values[:, h * HEAD : (h + 1) * HEAD]


def inverse_rms(values):
    return lax.rsqrt(jnp.mean(values * values, axis=-1, keepdims=True) + EPS)


def spread_text(packed):
    return jnp.concatenate([packed] + [pltpu.roll(packed, 128 - 32 * a, 1) for a in (1, 2, 3)], 0)


def pack_text(columns):
    pieces = [columns[PIECE * a : PIECE * (a + 1)] for a in range(4)]
    return pieces[0] + sum(pltpu.roll(pieces[a], 32 * a, 1) for a in (1, 2, 3))


def weight_copies(sources, wq, wo, sems):
    return [
        (
            pltpu.make_async_copy(sources[s], wq.at[s], sems.at[s]),
            pltpu.make_async_copy(sources[3 + s], wo.at[s], sems.at[3 + s]),
        )
        for s in range(3)
    ]


def pack_kernel(img, ctl, dy, txt, dy_txt, out, text_rows, sems):
    copies = [
        pltpu.make_async_copy(part, text_rows.at[i], sems.at[3 + i]) for i, part in enumerate((txt, dy_txt))
    ] + [
        pltpu.make_async_copy(part, out.at[pl.ds(SHARE * i, SHARE)], sems.at[i])
        for i, part in enumerate((img, ctl, dy))
    ]
    for copy in copies:
        copy.start()
    copies[0].wait()
    copies[1].wait()
    text = text_rows[...].reshape(2 * TXT, SHARE).astype(F32)
    text = jnp.concatenate([text, jnp.zeros((IMG - 2 * TXT, SHARE), F32)], 0)
    text = jnp.concatenate([text, jnp.zeros((IMG, 640 - SHARE), F32)], 1)
    out[3 * SHARE :, :] = pack_text(text.T).astype(BF16)
    for copy in copies[2:]:
        copy.wait()


class Results:
    def __init__(self, sems):
        self.sems, self.copies = sems, []

    def send(self, source, target):
        copy = pltpu.make_async_copy(source, target, self.sems.at[len(self.copies)])
        copy.start()
        self.copies.append(copy)

    def finish(self):
        for copy in self.copies:
            copy.wait()


def pre_kernel(
    in0, in1, in2, in3, mod, gains, wq_img, wq_txt, wq_ctl, wo_img, wo_txt, wo_ctl,
    send_out, proj_out, xhat_out, rstd_out, nz0, nz1, nz2, nz3, ny0, ny1, ny2, ny3,
    wq, wo, gat, send, send_ctl, proj, xhat, rstd, nz, ny, sems, in_sems, out_sems,
):
    arrivals = [
        pltpu.make_async_copy(part, gat.at[lax.axis_index("tp") ^ i], in_sems.at[i])
        for i, part in enumerate((in0, in1, in2, in3))
    ]
    for copy in arrivals:
        copy.start()
    copies = weight_copies((wq_img, wq_txt, wq_ctl, wo_img, wo_txt, wo_ctl), wq, wo, sems)
    for copy in (copies[0][0], copies[0][1], copies[2][0]):
        copy.start()
    results = Results(out_sems)
    for copy in arrivals:
        copy.wait()

    def rows(slab):
        return gat[:, SHARE * slab : SHARE * (slab + 1), :].reshape(D, IMG).T.astype(F32)

    def stream(s, x, e, at, later):
        count = x.shape[0]
        centered = x - jnp.mean(x, axis=-1, keepdims=True)
        inverse = lax.rsqrt(jnp.mean(centered * centered, axis=-1, keepdims=True) + EPS)
        standard = centered * inverse
        xhat[at : at + count, :] = standard
        rstd[at : at + count, :] = jnp.broadcast_to(inverse, (count, 128))
        n = (standard * (1.0 + mod[s, 1:2, :]) + mod[s, 0:1, :]).astype(BF16)
        copies[s][0].wait()
        for copy in later:
            copy.start()
        pq = dot(n, wq[s, 0])
        pk = dot(n, wq[s, 1])
        pv = dot(n, wq[s, 2])
        proj[at : at + count, 0:WIDTH] = pq
        proj[at : at + count, WIDTH : 2 * WIDTH] = pk
        for source, target in ((proj, proj_out), (xhat, xhat_out), (rstd, rstd_out)):
            results.send(source.at[pl.ds(at, count)], target.at[pl.ds(at, count)])
        copies[s][1].wait()
        g = dot_nt(e, wo[s])
        kv, qg = [], []
        for h in range(HEADS):
            q_h, k_h = head(pq, h), head(pk, h)
            q_h = q_h * inverse_rms(q_h) * (gains[s, 0:1, :] * 0.125)
            k_h = k_h * inverse_rms(k_h) * gains[s, 1:2, :]
            kv.append(jnp.concatenate([k_h, head(pv, h)], 1).astype(BF16))
            qg.append(jnp.concatenate([q_h, head(g, h)], 1).astype(BF16))
        return n, kv, qg

    dy = rows(2)
    text = jnp.concatenate([spread_text(gat[c, 3 * SHARE :, :].astype(F32)) for c in range(4)], 0).astype(BF16).T.astype(F32)
    e_img = (mod[0, 2:3, :] * dy).astype(BF16)
    n, kv, qg = stream(0, rows(0), e_img, 0, (copies[2][1], copies[1][0]))
    for h in range(HEADS):
        for t in range(MAIN_PARTS):
            to = MAIN_PARTS * h + t
            send[to, 0:IMG, :] = kv[h]
            last = min(IMG, MAIN_Q * (t + 1))
            send[to, IMG + TXT : IMG + TXT + last - MAIN_Q * t, :] = qg[h][MAIN_Q * t : last]
    e_ctl = mod[2, 2:3, :] * dy
    n, kv, qg = stream(2, rows(1), e_ctl.astype(BF16), IMG + TXT, (copies[1][1],))
    for h in range(HEADS):
        for u in range(CTL_PARTS):
            to = CTL_PARTS * h + u
            send_ctl[to, 0:IMG, :] = kv[h]
            send_ctl[to, IMG:CHUNK, :] = qg[h][CTL_Q * u : CTL_Q * (u + 1)]
    for to in range(CTL_PARTS * HEADS, BLOCKS - CTL_AT):
        send_ctl[to] = jnp.zeros((CHUNK, 128), BF16)
    results.send(send_ctl, send_out.at[pl.ds(CTL_AT, BLOCKS - CTL_AT)])
    n_t, e_t = n.T, e_ctl.astype(BF16).T
    nz[...] = n_t.reshape(4, SHARE, IMG)
    n_t, e_t = n_t.astype(F32), e_t.astype(F32)
    for y in range(4):
        for j, values in enumerate((n_t, e_t)):
            pieces = [values[SHARE * z + PIECE * y : SHARE * z + PIECE * (y + 1)] for z in range(4)]
            ny[y, j] = jnp.concatenate(pieces, 0).astype(BF16)
    for d, out in enumerate((nz0, nz1, nz2, nz3)):
        results.send(nz.at[lax.rem(lax.axis_index("z") + d, 4)], out)
    for d, out in enumerate((ny0, ny1, ny2, ny3)):
        results.send(ny.at[lax.rem(lax.axis_index("y") + d, 4)], out)
    e_txt = (mod[1, 2:3, :] * text[TXT : 2 * TXT]).astype(BF16)
    unused, kv, qg = stream(1, text[0:TXT], e_txt, IMG, ())
    for h in range(HEADS):
        for t in range(MAIN_PARTS):
            send[MAIN_PARTS * h + t, IMG : IMG + TXT, :] = kv[h]
        send[MAIN_PARTS * h + 2, CHUNK - TXT : CHUNK, :] = qg[h]
    results.send(send, send_out.at[pl.ds(0, CTL_AT)])
    results.finish()


def attention_kernel(role, recv, after, dkv_out, odq, kv, kt, vt, qg, probs, dkv):
    is_main = role[0]
    live = role[1]

    for b in range(BLOCKS):
        kv[IMG * b : IMG * (b + 1), :] = recv[b, 0:IMG, :]

    @pl.when(is_main == 1)
    def _():
        for b in range(BLOCKS):
            kv[IMAGE_KEYS + TXT * b : IMAGE_KEYS + TXT * (b + 1), :] = recv[b, IMG : IMG + TXT, :]
            qg[MAIN_Q * b : MAIN_Q * (b + 1), :] = recv[b, IMG + TXT : CHUNK, :]

    @pl.when(is_main == 0)
    def _():
        kv[IMAGE_KEYS:, :] = jnp.zeros((TEXT_KEYS, 128), BF16)
        for b in range(BLOCKS):
            qg[CTL_Q * b : CTL_Q * (b + 1), :] = recv[b, IMG:CHUNK, :]

    for i in range((IMAGE_KEYS + TEXT_KEYS) // 128):
        block = kv[128 * i : 128 * (i + 1), :].T
        kt[:, 128 * i : 128 * (i + 1)] = block[0:HEAD]
        vt[:, 128 * i : 128 * (i + 1)] = block[HEAD:128]
    dkv[...] = jnp.zeros_like(dkv)
    zeros_half = jnp.zeros((HEAD, TQ), BF16)
    low_lanes = lax.broadcasted_iota(jnp.int32, (TQ, 128), 1) < HEAD

    def q_tile(i, carry):
        q_at = pl.multiple_of(i * TQ, TQ)
        tile = qg[pl.ds(q_at, TQ), :]
        tile_t = tile.T
        g_t = tile_t[HEAD:128].astype(F32)
        q_rhs = jnp.concatenate([tile_t[0:HEAD], zeros_half], 0)
        g_rhs = jnp.concatenate([zeros_half, tile_t[HEAD:128]], 0)
        tile = tile.astype(F32)
        q_only = jnp.where(low_lanes, tile, 0.0).astype(BF16)
        g_only = jnp.where(low_lanes, 0.0, tile).astype(BF16)
        qg_rhs = jnp.concatenate([q_only, g_only], 0)

        def forward(at, state, masked):
            total, o_t = state
            p = jnp.exp(dot(kv[pl.ds(at, TK), :], q_rhs))
            if masked:
                p = jnp.where(lax.broadcasted_iota(jnp.int32, (TK, TQ), 0) < live, p, 0.0)
            probs[pl.ds(at, TK), :] = p
            total = total + jnp.sum(p.reshape(TK // 8, 8, TQ), 0)
            o_t = o_t + dot(vt[:, pl.ds(at, TK)], p.astype(BF16))
            return total, o_t

        state = (jnp.zeros((8, TQ), F32), jnp.zeros((HEAD, TQ), F32))
        state = lax.fori_loop(
            0, IMAGE_KEYS // TK, lambda j, c: forward(pl.multiple_of(j * TK, TK), c, False), state,
            unroll=8,
        )
        total, o_t = lax.fori_loop(0, is_main, lambda j, c: forward(IMAGE_KEYS, c, True), state)
        inverse = 1.0 / jnp.sum(total, axis=0, keepdims=True)
        o_t = (o_t * inverse).astype(BF16).astype(F32)
        delta = jnp.sum(g_t * o_t, axis=0, keepdims=True)

        def backward(at, dq_t):
            p = probs[pl.ds(at, TK), :] * inverse
            ds = (p * (dot(kv[pl.ds(at, TK), :], g_rhs) - delta)).astype(BF16)
            dkv[pl.ds(at, TK), :] += dot(jnp.concatenate([ds, p.astype(BF16)], 1), qg_rhs)
            return dq_t + dot(kt[:, pl.ds(at, TK)], ds)

        dq_t = jnp.zeros((HEAD, TQ), F32)
        dq_t = lax.fori_loop(
            0, IMAGE_KEYS // TK, lambda j, c: backward(pl.multiple_of(j * TK, TK), c), dq_t, unroll=8
        )
        dq_t = lax.fori_loop(0, is_main, lambda j, c: backward(IMAGE_KEYS, c), dq_t)
        odq[pl.ds(q_at, TQ), :] = jnp.concatenate([o_t, dq_t * 0.125], 0).astype(BF16).T
        return carry

    tiles = jnp.where(is_main == 1, BLOCKS * MAIN_Q // TQ, BLOCKS * CTL_Q // TQ)
    lax.fori_loop(0, tiles, q_tile, 0)

    dkv_out[...] = dkv[...].astype(BF16)


def scatter_kernel(role, dkv, odq, after0, after1, after2, after3, after4, out):
    for b in range(BLOCKS):
        out[b, 0:IMG, :] = dkv[IMG * b : IMG * (b + 1), :]

    @pl.when(role[0] == 1)
    def _():
        for b in range(BLOCKS):
            out[b, IMG : IMG + TXT, :] = dkv[IMAGE_KEYS + TXT * b : IMAGE_KEYS + TXT * (b + 1), :]
            out[b, IMG + TXT : CHUNK, :] = odq[MAIN_Q * b : MAIN_Q * (b + 1), :]

    @pl.when(role[0] == 0)
    def _():
        for b in range(BLOCKS):
            out[b, IMG:CHUNK, :] = odq[CTL_Q * b : CTL_Q * (b + 1), :]


def head_norm_back(x, gain, dy):
    inverse = inverse_rms(x)
    dy = dy * gain
    return inverse * dy - x * (inverse * inverse * inverse * jnp.mean(x * dy, axis=-1, keepdims=True))


def head_back(s, at, count, dkv, odq, proj, gains):
    o, dq, dk, dv = [], [], [], []
    for h in range(HEADS):
        x_q = proj[at : at + count, h * HEAD : (h + 1) * HEAD]
        x_k = proj[at : at + count, WIDTH + h * HEAD : WIDTH + (h + 1) * HEAD]
        o.append(odq[h][:, 0:HEAD])
        dq.append(head_norm_back(x_q, gains[s, 0:1, :], odq[h][:, HEAD:128]))
        dk.append(head_norm_back(x_k, gains[s, 1:2, :], dkv[h][:, 0:HEAD]))
        dv.append(dkv[h][:, HEAD:128])
    return [jnp.concatenate(parts, 1).astype(BF16) for parts in (dq, dk, dv, o)]


def head_back_ctl_kernel(recv, proj, gains, by_z, by_y):
    dkv, odq = [], []
    for h in range(HEADS):
        parts = [recv[CTL_AT + CTL_PARTS * h + u].astype(F32) for u in range(CTL_PARTS)]
        dkv.append(parts[0][0:IMG] + parts[1][0:IMG])
        odq.append(jnp.concatenate([parts[0][IMG:], parts[1][IMG:]], 0))
    dq, dk, dv, o = head_back(2, IMG + TXT, IMG, dkv, odq, proj, gains)
    by_z[:, 0:WIDTH] = dq
    by_z[:, WIDTH:] = dk
    by_y[:, 0:WIDTH] = dv
    by_y[:, WIDTH:] = o


def head_back_main(recv, proj, gains, main):
    kv_img, kv_txt, oq_img, oq_txt = [], [], [], []
    for h in range(HEADS):
        parts = [recv[MAIN_PARTS * h + t].astype(F32) for t in range(MAIN_PARTS)]
        kv = parts[0][0 : IMG + TXT] + parts[1][0 : IMG + TXT] + parts[2][0 : IMG + TXT]
        kv_img.append(kv[0:IMG])
        kv_txt.append(kv[IMG:])
        oq_img.append(
            jnp.concatenate(
                [parts[0][IMG + TXT :], parts[1][IMG + TXT :], parts[2][IMG + TXT : CHUNK - TXT]], 0
            )
        )
        oq_txt.append(parts[2][CHUNK - TXT :])
    for j, part in enumerate(head_back(0, 0, IMG, kv_img, oq_img, proj, gains)):
        main[0:IMG, j * WIDTH : (j + 1) * WIDTH] = part
    for j, part in enumerate(head_back(1, IMG, TXT, kv_txt, oq_txt, proj, gains)):
        main[IMG:, j * WIDTH : (j + 1) * WIDTH] = part


def back(s, dq, dk, dv, o, wq, wo, mod, standard, inverse):
    u = dot_nt(dq, wq[0]) + dot_nt(dk, wq[1]) + dot_nt(dv, wq[2])
    u = u * (1.0 + mod[s, 1:2, :])
    u = u - jnp.mean(u, axis=-1, keepdims=True) - standard * jnp.mean(u * standard, axis=-1, keepdims=True)
    return u * inverse, mod[s, 2:3, :] * dot(o, wo[...])


def slab(values):
    return values.astype(BF16).T.reshape(4, SHARE, IMG)


def post_kernel(
    recv, proj, gains, by_z, by_y, xhat_in, rstd_in, mod, wq_img, wq_txt, wq_ctl, wo_img, wo_txt, wo_ctl,
    mine0, mine1, theirs0, theirs1,
    wq, wo, main, xhat, rstd, slabs, sems, in_sems, out_sems,
):
    arrivals = [
        pltpu.make_async_copy(xhat_in, xhat, in_sems.at[0]),
        pltpu.make_async_copy(rstd_in, rstd, in_sems.at[1]),
    ]
    for copy in arrivals:
        copy.start()
    results = Results(out_sems)
    copies = weight_copies((wq_img, wq_txt, wq_ctl, wo_img, wo_txt, wo_ctl), wq, wo, sems)
    for copy in (copies[2][0], copies[2][1], copies[0][0]):
        copy.start()

    def stream(s, parts, at, later):
        count = parts[0].shape[0]
        copies[s][0].wait()
        copies[s][1].wait()
        for copy in later:
            copy.start()
        return back(s, *parts, wq.at[s], wo.at[s], mod, xhat[at : at + count, :], rstd[at : at + count, 0:1])

    def joint(at, count):
        return [main[at : at + count, j * WIDTH : (j + 1) * WIDTH] for j in range(4)]

    def leave(at, count):
        for other, out in enumerate((mine0, theirs0, mine1, theirs1)):
            results.send(slabs.at[lax.axis_index("tp") ^ other, pl.ds(at, count)], out.at[pl.ds(at, count)])

    head_back_main(recv, proj, gains, main)
    for copy in arrivals:
        copy.wait()
    u, y_ctl = stream(2, [r[:, j * WIDTH : (j + 1) * WIDTH] for r in (by_z, by_y) for j in range(2)], IMG + TXT, (copies[0][1], copies[1][0]))
    slabs[:, 2 * SHARE : 3 * SHARE, :] = slab(u)
    leave(2 * SHARE, SHARE)
    u, y = stream(0, joint(0, IMG), 0, (copies[1][1],))
    slabs[:, SHARE : 2 * SHARE, :] = slab(u)
    slabs[:, 0:SHARE, :] = slab(y + y_ctl)
    leave(0, 2 * SHARE)
    u, y = stream(1, joint(IMG, TXT), IMG, ())
    text = jnp.concatenate([y, u, jnp.zeros((IMG - 2 * TXT, D), F32)], 0).astype(BF16).T.astype(F32)
    for c in range(4):
        slabs[c, 3 * SHARE :, :] = pack_text(text[SHARE * c : SHARE * (c + 1)]).astype(BF16)
    leave(3 * SHARE, PIECE)
    results.finish()


def weight_kernel(
    nz0, nz1, nz2, nz3, ny0, ny1, ny2, ny3, bz0, bz1, bz2, bz3, by0, by1, by2, by3,
    theirs0, theirs1, out_z, out_y0, out_y1, out_y2, out_y3, same0, same1,
    chunks,
):
    nz, ny = (nz0, nz1, nz2, nz3), (ny0, ny1, ny2, ny3)
    bz, by = (bz0, bz1, bz2, bz3), (by0, by1, by2, by3)
    qk = dot(jnp.concatenate([r[...] for r in nz], 1), jnp.concatenate([r[...] for r in bz], 0))
    v = dot(jnp.concatenate([r[0] for r in ny], 1), jnp.concatenate([r[:, 0:WIDTH] for r in by], 0))
    o = dot(jnp.concatenate([r[1] for r in ny], 1), jnp.concatenate([r[:, WIDTH:] for r in by], 0))
    for p in range(4):
        out_z[p] = qk[PIECE * p : PIECE * (p + 1)].astype(BF16)
        chunks[p, :, 0:WIDTH] = v[PIECE * p : PIECE * (p + 1)].astype(BF16)
        chunks[p, :, WIDTH:] = o[PIECE * p : PIECE * (p + 1)].astype(BF16)
    for d, out in enumerate((out_y0, out_y1, out_y2, out_y3)):
        out[...] = chunks[lax.rem(lax.axis_index("z") + d, 4)]


def weight_sum_kernel(terms_z, y0, y1, y2, y3, mine, theirs):
    half = PIECE // 2
    low = lax.axis_index("w") == 0
    for j, terms in enumerate(([terms_z[p] for p in range(4)], [y0[...], y1[...], y2[...], y3[...]])):
        total = sum(term.astype(F32) for term in terms)
        first, second = total[0:half], total[half:]
        columns = slice(2 * WIDTH * j, 2 * WIDTH * (j + 1))
        mine[:, columns] = jnp.where(low, first, second)
        theirs[:, columns] = jnp.where(low, second, first).astype(BF16)


def weight_out_kernel(mine, other, qkv, out):
    for j in range(4):
        columns = slice(WIDTH * j, WIDTH * (j + 1))
        total = mine[:, columns] + other[:, columns].astype(F32)
        if j < 3:
            qkv[j] = total
        else:
            out[...] = total


def final_kernel(img, dy, txt, dy_txt, part0, part1, part2, y_img, d_img, d_ctl, y_txt, d_txt):
    total = part0[...].astype(F32) + part1[...].astype(F32) + part2[...].astype(F32)
    y_img[...] = (img[...].astype(F32) + total[0:SHARE]).astype(BF16)
    d_img[...] = (dy[...].astype(F32) + total[SHARE : 2 * SHARE]).astype(BF16)
    d_ctl[...] = total[2 * SHARE : 3 * SHARE].astype(BF16)
    text = jnp.concatenate([spread_text(total[3 * SHARE :]), jnp.zeros((640 - SHARE, IMG), F32)], 0).T
    y_txt[...] = (txt[...].astype(F32) + text[0:TXT, 0:SHARE]).astype(BF16)
    d_txt[...] = (dy_txt[...].astype(F32) + text[TXT : 2 * TXT, 0:SHARE]).astype(BF16)


def shifted(parts, axis):
    return [parts[0]] + [
        lax.ppermute(parts[d], axis, [(i, (i + d) % 4) for i in range(4)]) for d in (1, 2, 3)
    ]


def per_device(
    img, txt, ctl, dy_img, dy_txt, live_text_length, modulation, query_key_gains,
    w_qkv_img, wo_img, w_qkv_txt, wo_txt, w_qkv_ctl, wo_ctl,
):
    seq = ("z", "y", "w")
    seq_pos = lax.axis_index(seq)
    role = jnp.stack([(seq_pos < CTL_AT).astype(jnp.int32), live_text_length[0]])
    mod, gains = modulation, query_key_gains
    weights = (
        w_qkv_img.transpose(1, 0, 2), w_qkv_txt.transpose(1, 0, 2), w_qkv_ctl.transpose(1, 0, 2),
        wo_img, wo_txt, wo_ctl,
    )
    shape = jax.ShapeDtypeStruct
    rows = shape((ROWS, IMG), BF16)
    other_core = [(i, i ^ 1) for i in range(4)]
    other_chip = [(i, i ^ 2) for i in range(4)]

    own = pl.pallas_call(
        pack_kernel,
        out_shape=rows,
        in_specs=[HBM] * 5,
        out_specs=VMEM,
        scratch_shapes=[pltpu.VMEM((2, TXT, SHARE), BF16), pltpu.SemaphoreType.DMA((5,))],
        compiler_params=pltpu.CompilerParams(vmem_limit_bytes=63_400_000),
        name="pack",
    )(img.T, ctl.T, dy_img.T, txt, dy_txt)
    from_chip = lax.ppermute(own, "tp", other_chip)
    from_core = lax.ppermute(own, "tp", other_core)
    from_both = lax.ppermute(from_chip, "tp", other_core)

    send, proj, xhat, rstd, *slabs = pl.pallas_call(
        pre_kernel,
        out_shape=[
            shape((BLOCKS, CHUNK, 128), BF16),
            shape((2 * IMG + TXT, 2 * WIDTH), F32),
            shape((2 * IMG + TXT, D), F32),
            shape((2 * IMG + TXT, 128), F32),
        ] + [shape((SHARE, IMG), BF16)] * 4 + [shape((2, SHARE, IMG), BF16)] * 4,
        in_specs=[HBM] * 4 + [VMEM] * 2 + [HBM] * 6,
        out_specs=[ANY] * 12,
        scratch_shapes=[
            pltpu.VMEM((3, 3, D, WIDTH), BF16),
            pltpu.VMEM((3, WIDTH, D), BF16),
            pltpu.VMEM((4, ROWS, IMG), BF16),
            pltpu.VMEM((CTL_AT, CHUNK, 128), BF16),
            pltpu.VMEM((BLOCKS - CTL_AT, CHUNK, 128), BF16),
            pltpu.VMEM((2 * IMG + TXT, 2 * WIDTH), F32),
            pltpu.VMEM((2 * IMG + TXT, D), F32),
            pltpu.VMEM((2 * IMG + TXT, 128), F32),
            pltpu.VMEM((4, SHARE, IMG), BF16),
            pltpu.VMEM((4, 2, SHARE, IMG), BF16),
            pltpu.SemaphoreType.DMA((6,)),
            pltpu.SemaphoreType.DMA((4,)),
            pltpu.SemaphoreType.DMA((19,)),
        ],
        compiler_params=params(56),
        name="pre",
    )(own, from_core, from_chip, from_both, mod, gains, *weights)

    recv = lax.all_to_all(send, seq, 0, 0, tiled=True)
    nz = shifted(slabs[0:4], "z")
    ny = shifted(slabs[4:8], "y")
    keys = IMAGE_KEYS + TEXT_KEYS
    dkv, odq = pl.pallas_call(
        attention_kernel,
        out_shape=[shape((keys, 128), BF16), shape((BLOCKS * CTL_Q, 128), BF16)],
        in_specs=[SMEM, VMEM, ANY],
        out_specs=[VMEM] * 2,
        scratch_shapes=[
            pltpu.VMEM((keys, 128), BF16),
            pltpu.VMEM((HEAD, keys), BF16),
            pltpu.VMEM((HEAD, keys), BF16),
            pltpu.VMEM((BLOCKS * CTL_Q, 128), BF16),
            pltpu.VMEM((keys, TQ), F32),
            pltpu.VMEM((keys, 128), F32),
        ],
        compiler_params=params(32),
        cost_estimate=pl.CostEstimate(flops=40_000_000_000, bytes_accessed=3_200_000, transcendentals=8_400_000),
        name="attention",
    )(role, recv, nz[3])
    back = pl.pallas_call(
        scatter_kernel,
        out_shape=shape((BLOCKS, CHUNK, 128), BF16),
        in_specs=[SMEM] + [VMEM] * 2 + [ANY] * 5,
        out_specs=VMEM,
        compiler_params=params(16),
        name="scatter",
    )(role, dkv, odq, *nz[1:3], *ny[1:])
    back = lax.all_to_all(back, seq, 0, 0, tiled=True)

    by_z, by_y = pl.pallas_call(
        head_back_ctl_kernel,
        out_shape=[shape((IMG, 2 * WIDTH), BF16)] * 2,
        in_specs=[VMEM] * 3,
        out_specs=[VMEM] * 2,
        compiler_params=params(16),
        name="head_back_ctl",
    )(back, proj, gains)
    blocks_z = shifted([by_z] * 4, "z")
    blocks_y = shifted([by_y] * 4, "y")
    mine0, mine1, theirs0, theirs1 = pl.pallas_call(
        post_kernel,
        out_shape=[rows] * 4,
        in_specs=[VMEM] * 5 + [HBM] * 2 + [VMEM] + [HBM] * 6,
        out_specs=[ANY] * 4,
        scratch_shapes=[
            pltpu.VMEM((3, 3, D, WIDTH), BF16),
            pltpu.VMEM((3, WIDTH, D), BF16),
            pltpu.VMEM((IMG + TXT, 4 * WIDTH), BF16),
            pltpu.VMEM((2 * IMG + TXT, D), F32),
            pltpu.VMEM((2 * IMG + TXT, 128), F32),
            pltpu.VMEM((4, ROWS, IMG), BF16),
            pltpu.SemaphoreType.DMA((6,)),
            pltpu.SemaphoreType.DMA((2,)),
            pltpu.SemaphoreType.DMA((12,)),
        ],
        compiler_params=params(54),
        cost_estimate=pl.CostEstimate(flops=14_000_000_000, bytes_accessed=30_000_000, transcendentals=0),
        name="post",
    )(back, proj, gains, by_z, by_y, xhat, rstd, mod, *weights)
    terms_z, *outs = pl.pallas_call(
        weight_kernel,
        out_shape=[shape((4, PIECE, 2 * WIDTH), BF16)] + [shape((PIECE, 2 * WIDTH), BF16)] * 4 + [rows] * 2,
        in_specs=[VMEM] * 16 + [ANY] * 2,
        out_specs=[VMEM] * 5 + [ANY] * 2,
        input_output_aliases={16: 5, 17: 6},
        scratch_shapes=[pltpu.VMEM((4, PIECE, 2 * WIDTH), BF16)],
        compiler_params=params(24),
        cost_estimate=pl.CostEstimate(flops=3_000_000_000, bytes_accessed=5_000_000, transcendentals=0),
        name="weight",
    )(*nz, *ny, *blocks_z, *blocks_y, theirs0, theirs1)
    terms_y, (theirs0, theirs1) = outs[0:4], outs[4:6]
    got1 = lax.ppermute(theirs1, "tp", other_core)
    got0 = lax.ppermute(theirs0, "tp", other_core)
    passed = (mine1.astype(F32) + got1.astype(F32)).astype(BF16)
    passed = lax.ppermute(passed, "tp", other_chip)
    terms_y = shifted(terms_y, "z")
    terms_z = lax.all_to_all(terms_z, "y", 0, 0, tiled=True)
    mine, theirs = pl.pallas_call(
        weight_sum_kernel,
        out_shape=[shape((PIECE // 2, 4 * WIDTH), F32), shape((PIECE // 2, 4 * WIDTH), BF16)],
        in_specs=[VMEM] * 5,
        out_specs=[VMEM] * 2,
        compiler_params=params(16),
        name="weight_sum",
    )(terms_z, *terms_y)
    theirs = lax.ppermute(theirs, "w", [(0, 1), (1, 0)])
    grad_qkv, grad_out = pl.pallas_call(
        weight_out_kernel,
        out_shape=[shape((3, PIECE // 2, WIDTH), F32), shape((PIECE // 2, WIDTH), F32)],
        in_specs=[VMEM] * 2,
        out_specs=[VMEM] * 2,
        compiler_params=params(16),
        name="weight_out",
    )(mine, theirs)

    y_img, d_img, d_ctl, y_txt, d_txt = pl.pallas_call(
        final_kernel,
        out_shape=[shape((SHARE, IMG), BF16)] * 3 + [shape((TXT, SHARE), BF16)] * 2,
        in_specs=[VMEM] * 7,
        out_specs=[VMEM] * 5,
        compiler_params=params(16),
        name="final",
    )(img.T, dy_img.T, txt, dy_txt, mine0, got0, passed)
    return y_img.T, y_txt, d_img.T, d_txt, d_ctl.T, grad_qkv.transpose(1, 0, 2), grad_out.T


def solution(mesh):
    fine = Mesh(mesh.devices.reshape(4, 4, 2, 4), ("z", "y", "w", "tp"))
    seq = ("z", "y", "w")
    rows = P(seq, "tp")
    qkv = P(None, None, "tp")
    out = P("tp", None)
    in_specs = (rows,) * 5 + (P(), P(), P(), qkv, out, qkv, out, qkv, out)
    out_specs = (rows,) * 5 + (P(seq, None, "tp"), P("tp", seq))
    return jax.shard_map(
        per_device, mesh=fine, in_specs=in_specs, out_specs=out_specs, check_vma=False
    )
```

```python
import jax
import jax.numpy as jnp
from jax import lax
from jax.experimental import pallas as pl
from jax.experimental.pallas import tpu as pltpu
from jax.sharding import Mesh, PartitionSpec as P

EPS = 1e-06
HEAD = 64
HEADS = 6
WIDTH = HEADS * HEAD
D = 2432
SHARE = 608
PIECE = 152
ROWS = 3 * SHARE + PIECE
IMG = 128
TXT = 16
BLOCKS = 32
CHUNK = 192
IMAGE_KEYS = BLOCKS * IMG
TEXT_KEYS = BLOCKS * TXT
MAIN_Q = 48
CTL_Q = 64
MAIN_PARTS = 3
CTL_PARTS = 2
CTL_AT = HEADS * MAIN_PARTS
TQ = 512
TK = 512
F32 = jnp.float32
BF16 = jnp.bfloat16
NT = (((1,), (1,)), ((), ()))
VMEM = pl.BlockSpec(memory_space=pltpu.VMEM)
SMEM = pl.BlockSpec(memory_space=pltpu.SMEM)
ANY = pl.BlockSpec(memory_space=pl.ANY)
HBM = pl.BlockSpec(memory_space=pltpu.HBM)


def params(mib):
    return pltpu.CompilerParams(vmem_limit_bytes=mib * 1024 * 1024)


def dot(a, b):
    return jnp.dot(a, b, preferred_element_type=F32)


def dot_nt(a, b):
    return lax.dot_general(a, b, NT, preferred_element_type=F32)


def head(values, h):
    return values[:, h * HEAD : (h + 1) * HEAD]


def inverse_rms(values):
    return lax.rsqrt(jnp.mean(values * values, axis=-1, keepdims=True) + EPS)


def spread_text(packed):
    return jnp.concatenate([packed] + [pltpu.roll(packed, 128 - 32 * a, 1) for a in (1, 2, 3)], 0)


def pack_text(columns):
    pieces = [columns[PIECE * a : PIECE * (a + 1)] for a in range(4)]
    return pieces[0] + sum(pltpu.roll(pieces[a], 32 * a, 1) for a in (1, 2, 3))


def weight_copies(sources, wq, wo, sems):
    return [
        [pltpu.make_async_copy(sources[s].at[j], wq.at[s, j], sems.at[4 * s + j]) for j in range(3)]
        + [pltpu.make_async_copy(sources[3 + s], wo.at[s], sems.at[4 * s + 3])]
        for s in range(3)
    ]


def pack_kernel(img, ctl, dy, txt, dy_txt, out, text_rows, sems):
    copies = [
        pltpu.make_async_copy(part, text_rows.at[i], sems.at[3 + i]) for i, part in enumerate((txt, dy_txt))
    ] + [
        pltpu.make_async_copy(part, out.at[pl.ds(SHARE * i, SHARE)], sems.at[i])
        for i, part in enumerate((img, ctl, dy))
    ]
    for copy in copies:
        copy.start()
    copies[0].wait()
    copies[1].wait()
    text = text_rows[...].reshape(2 * TXT, SHARE).astype(F32)
    text = jnp.concatenate([text, jnp.zeros((IMG - 2 * TXT, SHARE), F32)], 0)
    text = jnp.concatenate([text, jnp.zeros((IMG, 640 - SHARE), F32)], 1)
    out[3 * SHARE :, :] = pack_text(text.T).astype(BF16)
    for copy in copies[2:]:
        copy.wait()


class Results:
    def __init__(self, sems):
        self.sems, self.copies = sems, []

    def send(self, source, target):
        copy = pltpu.make_async_copy(source, target, self.sems.at[len(self.copies)])
        copy.start()
        self.copies.append(copy)

    def finish(self):
        for copy in self.copies:
            copy.wait()


def pre_kernel(
    in0, in1, in2, in3, mod, gains, wq_img, wq_txt, wq_ctl, wo_img, wo_txt, wo_ctl,
    send_out, proj_out, xhat_out, rstd_out, nz0, nz1, nz2, nz3,
    wq, wo, gat, send, send_ctl, proj, xhat, rstd, nz, sems, in_sems, out_sems,
):
    arrivals = [
        pltpu.make_async_copy(part, gat.at[lax.axis_index("tp") ^ i], in_sems.at[i])
        for i, part in enumerate((in0, in1, in2, in3))
    ]
    for copy in arrivals:
        copy.start()
    copies = weight_copies((wq_img, wq_txt, wq_ctl, wo_img, wo_txt, wo_ctl), wq, wo, sems)
    for s in (0, 2, 1):
        for copy in copies[s]:
            copy.start()
    results = Results(out_sems)
    for copy in arrivals:
        copy.wait()

    def rows(slab):
        return gat[:, SHARE * slab : SHARE * (slab + 1), :].reshape(D, IMG).T.astype(F32)

    def stream(s, x, e, at):
        count = x.shape[0]
        centered = x - jnp.mean(x, axis=-1, keepdims=True)
        inverse = lax.rsqrt(jnp.mean(centered * centered, axis=-1, keepdims=True) + EPS)
        standard = centered * inverse
        xhat[at : at + count, :] = standard
        rstd[at : at + count, :] = jnp.broadcast_to(inverse, (count, 128))
        n = (standard * (1.0 + mod[s, 1:2, :]) + mod[s, 0:1, :]).astype(BF16)
        copies[s][0].wait()
        pq = dot(n, wq[s, 0])
        copies[s][1].wait()
        pk = dot(n, wq[s, 1])
        copies[s][2].wait()
        pv = dot(n, wq[s, 2])
        proj[at : at + count, 0:WIDTH] = pq
        proj[at : at + count, WIDTH : 2 * WIDTH] = pk
        for source, target in ((proj, proj_out), (xhat, xhat_out), (rstd, rstd_out)):
            results.send(source.at[pl.ds(at, count)], target.at[pl.ds(at, count)])
        copies[s][3].wait()
        g = dot_nt(e, wo[s])
        kv, qg = [], []
        for h in range(HEADS):
            q_h, k_h = head(pq, h), head(pk, h)
            q_h = q_h * inverse_rms(q_h) * (gains[s, 0:1, :] * 0.125)
            k_h = k_h * inverse_rms(k_h) * gains[s, 1:2, :]
            kv.append(jnp.concatenate([k_h, head(pv, h)], 1).astype(BF16))
            qg.append(jnp.concatenate([q_h, head(g, h)], 1).astype(BF16))
        return n, kv, qg

    dy = rows(2)
    text = jnp.concatenate([spread_text(gat[c, 3 * SHARE :, :].astype(F32)) for c in range(4)], 0).astype(BF16).T.astype(F32)
    e_img = (mod[0, 2:3, :] * dy).astype(BF16)
    n, kv, qg = stream(0, rows(0), e_img, 0)
    for h in range(HEADS):
        for t in range(MAIN_PARTS):
            to = MAIN_PARTS * h + t
            send[to, 0:IMG, :] = kv[h]
            last = min(IMG, MAIN_Q * (t + 1))
            send[to, IMG + TXT : IMG + TXT + last - MAIN_Q * t, :] = qg[h][MAIN_Q * t : last]
    e_ctl = mod[2, 2:3, :] * dy
    n, kv, qg = stream(2, rows(1), e_ctl.astype(BF16), IMG + TXT)
    for h in range(HEADS):
        for u in range(CTL_PARTS):
            to = CTL_PARTS * h + u
            send_ctl[to, 0:IMG, :] = kv[h]
            send_ctl[to, IMG:CHUNK, :] = qg[h][CTL_Q * u : CTL_Q * (u + 1)]
    for to in range(CTL_PARTS * HEADS, BLOCKS - CTL_AT):
        send_ctl[to] = jnp.zeros((CHUNK, 128), BF16)
    results.send(send_ctl, send_out.at[pl.ds(CTL_AT, BLOCKS - CTL_AT)])
    nz[:, 0] = n.T.reshape(4, SHARE, IMG)
    nz[:, 1] = e_ctl.astype(BF16).T.reshape(4, SHARE, IMG)
    for d, out in enumerate((nz0, nz1, nz2, nz3)):
        results.send(nz.at[lax.rem(lax.axis_index("z") + d, 4)], out)
    e_txt = (mod[1, 2:3, :] * text[TXT : 2 * TXT]).astype(BF16)
    unused, kv, qg = stream(1, text[0:TXT], e_txt, IMG)
    for h in range(HEADS):
        for t in range(MAIN_PARTS):
            send[MAIN_PARTS * h + t, IMG : IMG + TXT, :] = kv[h]
        send[MAIN_PARTS * h + 2, CHUNK - TXT : CHUNK, :] = qg[h]
    results.send(send, send_out.at[pl.ds(0, CTL_AT)])
    results.finish()


def attention_kernel(role, recv, after, dkv_out, odq, kv, kt, vt, qg, probs, dkv):
    is_main = role[0]
    live = role[1]

    for b in range(BLOCKS):
        kv[IMG * b : IMG * (b + 1), :] = recv[b, 0:IMG, :]

    @pl.when(is_main == 1)
    def _():
        for b in range(BLOCKS):
            kv[IMAGE_KEYS + TXT * b : IMAGE_KEYS + TXT * (b + 1), :] = recv[b, IMG : IMG + TXT, :]
            qg[MAIN_Q * b : MAIN_Q * (b + 1), :] = recv[b, IMG + TXT : CHUNK, :]

    @pl.when(is_main == 0)
    def _():
        kv[IMAGE_KEYS:, :] = jnp.zeros((TEXT_KEYS, 128), BF16)
        for b in range(BLOCKS):
            qg[CTL_Q * b : CTL_Q * (b + 1), :] = recv[b, IMG:CHUNK, :]

    for i in range((IMAGE_KEYS + TEXT_KEYS) // 128):
        block = kv[128 * i : 128 * (i + 1), :].T
        kt[:, 128 * i : 128 * (i + 1)] = block[0:HEAD]
        vt[:, 128 * i : 128 * (i + 1)] = block[HEAD:128]
    dkv[...] = jnp.zeros_like(dkv)
    zeros_half = jnp.zeros((HEAD, TQ), BF16)
    low_lanes = lax.broadcasted_iota(jnp.int32, (TQ, 128), 1) < HEAD

    def q_tile(i, carry):
        q_at = pl.multiple_of(i * TQ, TQ)
        tile = qg[pl.ds(q_at, TQ), :]
        tile_t = tile.T
        g_t = tile_t[HEAD:128].astype(F32)
        q_rhs = jnp.concatenate([tile_t[0:HEAD], zeros_half], 0)
        g_rhs = jnp.concatenate([zeros_half, tile_t[HEAD:128]], 0)
        tile = tile.astype(F32)
        q_only = jnp.where(low_lanes, tile, 0.0).astype(BF16)
        g_only = jnp.where(low_lanes, 0.0, tile).astype(BF16)
        qg_rhs = jnp.concatenate([q_only, g_only], 0)

        def forward(at, state, masked):
            total, o_t = state
            p = jnp.exp(dot(kv[pl.ds(at, TK), :], q_rhs))
            if masked:
                p = jnp.where(lax.broadcasted_iota(jnp.int32, (TK, TQ), 0) < live, p, 0.0)
            probs[pl.ds(at, TK), :] = p
            total = total + jnp.sum(p.reshape(TK // 8, 8, TQ), 0)
            o_t = o_t + dot(vt[:, pl.ds(at, TK)], p.astype(BF16))
            return total, o_t

        state = (jnp.zeros((8, TQ), F32), jnp.zeros((HEAD, TQ), F32))
        state = lax.fori_loop(
            0, IMAGE_KEYS // TK, lambda j, c: forward(pl.multiple_of(j * TK, TK), c, False), state,
            unroll=8,
        )
        total, o_t = lax.fori_loop(0, is_main, lambda j, c: forward(IMAGE_KEYS, c, True), state)
        inverse = 1.0 / jnp.sum(total, axis=0, keepdims=True)
        o_t = (o_t * inverse).astype(BF16).astype(F32)
        delta = jnp.sum(g_t * o_t, axis=0, keepdims=True)

        def backward(at, dq_t):
            p = probs[pl.ds(at, TK), :] * inverse
            ds = (p * (dot(kv[pl.ds(at, TK), :], g_rhs) - delta)).astype(BF16)
            dkv[pl.ds(at, TK), :] += dot(jnp.concatenate([ds, p.astype(BF16)], 1), qg_rhs)
            return dq_t + dot(kt[:, pl.ds(at, TK)], ds)

        dq_t = jnp.zeros((HEAD, TQ), F32)
        dq_t = lax.fori_loop(
            0, IMAGE_KEYS // TK, lambda j, c: backward(pl.multiple_of(j * TK, TK), c), dq_t, unroll=8
        )
        dq_t = lax.fori_loop(0, is_main, lambda j, c: backward(IMAGE_KEYS, c), dq_t)
        odq[pl.ds(q_at, TQ), :] = jnp.concatenate([o_t, dq_t * 0.125], 0).astype(BF16).T
        return carry

    tiles = jnp.where(is_main == 1, BLOCKS * MAIN_Q // TQ, BLOCKS * CTL_Q // TQ)
    lax.fori_loop(0, tiles, q_tile, 0)

    dkv_out[...] = dkv[...].astype(BF16)


def scatter_kernel(role, dkv, odq, after0, after1, out):
    for b in range(BLOCKS):
        out[b, 0:IMG, :] = dkv[IMG * b : IMG * (b + 1), :]

    @pl.when(role[0] == 1)
    def _():
        for b in range(BLOCKS):
            out[b, IMG : IMG + TXT, :] = dkv[IMAGE_KEYS + TXT * b : IMAGE_KEYS + TXT * (b + 1), :]
            out[b, IMG + TXT : CHUNK, :] = odq[MAIN_Q * b : MAIN_Q * (b + 1), :]

    @pl.when(role[0] == 0)
    def _():
        for b in range(BLOCKS):
            out[b, IMG:CHUNK, :] = odq[CTL_Q * b : CTL_Q * (b + 1), :]


def head_norm_back(x, gain, dy):
    inverse = inverse_rms(x)
    dy = dy * gain
    return inverse * dy - x * (inverse * inverse * inverse * jnp.mean(x * dy, axis=-1, keepdims=True))


def head_back(s, at, count, dkv, odq, proj, gains):
    o, dq, dk, dv = [], [], [], []
    for h in range(HEADS):
        x_q = proj[at : at + count, h * HEAD : (h + 1) * HEAD]
        x_k = proj[at : at + count, WIDTH + h * HEAD : WIDTH + (h + 1) * HEAD]
        o.append(odq[h][:, 0:HEAD])
        dq.append(head_norm_back(x_q, gains[s, 0:1, :], odq[h][:, HEAD:128]))
        dk.append(head_norm_back(x_k, gains[s, 1:2, :], dkv[h][:, 0:HEAD]))
        dv.append(dkv[h][:, HEAD:128])
    return [jnp.concatenate(parts, 1).astype(BF16) for parts in (dq, dk, dv, o)]


def head_back_ctl_kernel(recv, proj, gains, out):
    dkv, odq = [], []
    for h in range(HEADS):
        parts = [recv[CTL_AT + CTL_PARTS * h + u].astype(F32) for u in range(CTL_PARTS)]
        dkv.append(parts[0][0:IMG] + parts[1][0:IMG])
        odq.append(jnp.concatenate([parts[0][IMG:], parts[1][IMG:]], 0))
    for j, part in enumerate(head_back(2, IMG + TXT, IMG, dkv, odq, proj, gains)):
        out[:, j * WIDTH : (j + 1) * WIDTH] = part


def head_back_main(recv, proj, gains, main):
    kv_img, kv_txt, oq_img, oq_txt = [], [], [], []
    for h in range(HEADS):
        parts = [recv[MAIN_PARTS * h + t].astype(F32) for t in range(MAIN_PARTS)]
        kv = parts[0][0 : IMG + TXT] + parts[1][0 : IMG + TXT] + parts[2][0 : IMG + TXT]
        kv_img.append(kv[0:IMG])
        kv_txt.append(kv[IMG:])
        oq_img.append(
            jnp.concatenate(
                [parts[0][IMG + TXT :], parts[1][IMG + TXT :], parts[2][IMG + TXT : CHUNK - TXT]], 0
            )
        )
        oq_txt.append(parts[2][CHUNK - TXT :])
    for j, part in enumerate(head_back(0, 0, IMG, kv_img, oq_img, proj, gains)):
        main[0:IMG, j * WIDTH : (j + 1) * WIDTH] = part
    for j, part in enumerate(head_back(1, IMG, TXT, kv_txt, oq_txt, proj, gains)):
        main[IMG:, j * WIDTH : (j + 1) * WIDTH] = part


def back(s, dq, dk, dv, o, wq, wo, mod, standard, inverse):
    u = dot_nt(dq, wq[0]) + dot_nt(dk, wq[1]) + dot_nt(dv, wq[2])
    u = u * (1.0 + mod[s, 1:2, :])
    u = u - jnp.mean(u, axis=-1, keepdims=True) - standard * jnp.mean(u * standard, axis=-1, keepdims=True)
    return u * inverse, mod[s, 2:3, :] * dot(o, wo[...])


def slab(values):
    return values.astype(BF16).T.reshape(4, SHARE, IMG)


def post_kernel(
    recv, proj, gains, ctl_rows, xhat_in, rstd_in, mod, wq_img, wq_txt, wq_ctl, wo_img, wo_txt, wo_ctl,
    mine0, mine1, theirs0, theirs1,
    wq, wo, main, xhat, rstd, slabs, sems, in_sems, out_sems,
):
    arrivals = [
        pltpu.make_async_copy(xhat_in, xhat, in_sems.at[0]),
        pltpu.make_async_copy(rstd_in, rstd, in_sems.at[1]),
    ]
    for copy in arrivals:
        copy.start()
    results = Results(out_sems)
    copies = weight_copies((wq_img, wq_txt, wq_ctl, wo_img, wo_txt, wo_ctl), wq, wo, sems)
    for s in (2, 0, 1):
        for copy in copies[s]:
            copy.start()

    def stream(s, parts, at):
        count = parts[0].shape[0]
        for copy in copies[s]:
            copy.wait()
        return back(s, *parts, wq.at[s], wo.at[s], mod, xhat[at : at + count, :], rstd[at : at + count, 0:1])

    def joint(at, count):
        return [main[at : at + count, j * WIDTH : (j + 1) * WIDTH] for j in range(4)]

    def leave(at, count):
        for other, out in enumerate((mine0, theirs0, mine1, theirs1)):
            results.send(slabs.at[lax.axis_index("tp") ^ other, pl.ds(at, count)], out.at[pl.ds(at, count)])

    head_back_main(recv, proj, gains, main)
    for copy in arrivals:
        copy.wait()
    u, y_ctl = stream(2, [ctl_rows[:, j * WIDTH : (j + 1) * WIDTH] for j in range(4)], IMG + TXT)
    slabs[:, 2 * SHARE : 3 * SHARE, :] = slab(u)
    leave(2 * SHARE, SHARE)
    u, y = stream(0, joint(0, IMG), 0)
    slabs[:, SHARE : 2 * SHARE, :] = slab(u)
    slabs[:, 0:SHARE, :] = slab(y + y_ctl)
    leave(0, 2 * SHARE)
    u, y = stream(1, joint(IMG, TXT), IMG)
    text = jnp.concatenate([y, u, jnp.zeros((IMG - 2 * TXT, D), F32)], 0).astype(BF16).T.astype(F32)
    for c in range(4):
        slabs[c, 3 * SHARE :, :] = pack_text(text[SHARE * c : SHARE * (c + 1)]).astype(BF16)
    leave(3 * SHARE, PIECE)
    results.finish()


def weight_kernel(nz0, nz1, nz2, nz3, b0, b1, b2, b3, out):
    nz, blocks = (nz0, nz1, nz2, nz3), (b0, b1, b2, b3)
    total = jnp.concatenate(
        [
            dot(
                jnp.concatenate([r[j] for r in nz], 1),
                jnp.concatenate([r[:, 3 * j * WIDTH : (3 + j) * WIDTH] for r in blocks], 0),
            )
            for j in range(2)
        ],
        1,
    )
    for p in range(4):
        out[p] = total[PIECE * p : PIECE * (p + 1)].astype(BF16)


def weight_sum_kernel(terms, mine, theirs):
    half = PIECE // 2
    low = lax.axis_index("w") == 0
    total = sum(terms[p].astype(F32) for p in range(4))
    first, second = total[0:half], total[half:]
    mine[...] = jnp.where(low, first, second)
    theirs[...] = jnp.where(low, second, first).astype(BF16)


def weight_out_kernel(mine, other, qkv, out):
    for j in range(4):
        columns = slice(WIDTH * j, WIDTH * (j + 1))
        total = mine[:, columns] + other[:, columns].astype(F32)
        if j < 3:
            qkv[j] = total
        else:
            out[...] = total


def final_kernel(img, dy, txt, dy_txt, part0, part1, part2, y_img, d_img, d_ctl, y_txt, d_txt):
    total = part0[...].astype(F32) + part1[...].astype(F32) + part2[...].astype(F32)
    y_img[...] = (img[...].astype(F32) + total[0:SHARE]).astype(BF16)
    d_img[...] = (dy[...].astype(F32) + total[SHARE : 2 * SHARE]).astype(BF16)
    d_ctl[...] = total[2 * SHARE : 3 * SHARE].astype(BF16)
    text = jnp.concatenate([spread_text(total[3 * SHARE :]), jnp.zeros((640 - SHARE, IMG), F32)], 0).T
    y_txt[...] = (txt[...].astype(F32) + text[0:TXT, 0:SHARE]).astype(BF16)
    d_txt[...] = (dy_txt[...].astype(F32) + text[TXT : 2 * TXT, 0:SHARE]).astype(BF16)


def shifted(parts, axis):
    return [parts[0]] + [
        lax.ppermute(parts[d], axis, [(i, (i + d) % 4) for i in range(4)]) for d in (1, 2, 3)
    ]


def per_device(
    img, txt, ctl, dy_img, dy_txt, live_text_length, modulation, query_key_gains,
    w_qkv_img, wo_img, w_qkv_txt, wo_txt, w_qkv_ctl, wo_ctl,
):
    seq = ("z", "y", "w")
    seq_pos = lax.axis_index(seq)
    role = jnp.stack([(seq_pos < CTL_AT).astype(jnp.int32), live_text_length[0]])
    mod, gains = modulation, query_key_gains
    weights = (
        w_qkv_img.transpose(1, 0, 2), w_qkv_txt.transpose(1, 0, 2), w_qkv_ctl.transpose(1, 0, 2),
        wo_img, wo_txt, wo_ctl,
    )
    shape = jax.ShapeDtypeStruct
    rows = shape((ROWS, IMG), BF16)
    other_core = [(i, i ^ 1) for i in range(4)]
    other_chip = [(i, i ^ 2) for i in range(4)]

    own = pl.pallas_call(
        pack_kernel,
        out_shape=rows,
        in_specs=[HBM] * 5,
        out_specs=VMEM,
        scratch_shapes=[pltpu.VMEM((2, TXT, SHARE), BF16), pltpu.SemaphoreType.DMA((5,))],
        compiler_params=pltpu.CompilerParams(vmem_limit_bytes=63_400_000),
        name="pack",
    )(img.T, ctl.T, dy_img.T, txt, dy_txt)
    from_chip = lax.ppermute(own, "tp", other_chip)
    from_core = lax.ppermute(own, "tp", other_core)
    from_both = lax.ppermute(from_chip, "tp", other_core)

    send, proj, xhat, rstd, *slabs = pl.pallas_call(
        pre_kernel,
        out_shape=[
            shape((BLOCKS, CHUNK, 128), BF16),
            shape((2 * IMG + TXT, 2 * WIDTH), F32),
            shape((2 * IMG + TXT, D), F32),
            shape((2 * IMG + TXT, 128), F32),
        ] + [shape((2, SHARE, IMG), BF16)] * 4,
        in_specs=[HBM] * 4 + [VMEM] * 2 + [HBM] * 6,
        out_specs=[ANY] * 8,
        scratch_shapes=[
            pltpu.VMEM((3, 3, D, WIDTH), BF16),
            pltpu.VMEM((3, WIDTH, D), BF16),
            pltpu.VMEM((4, ROWS, IMG), BF16),
            pltpu.VMEM((CTL_AT, CHUNK, 128), BF16),
            pltpu.VMEM((BLOCKS - CTL_AT, CHUNK, 128), BF16),
            pltpu.VMEM((2 * IMG + TXT, 2 * WIDTH), F32),
            pltpu.VMEM((2 * IMG + TXT, D), F32),
            pltpu.VMEM((2 * IMG + TXT, 128), F32),
            pltpu.VMEM((4, 2, SHARE, IMG), BF16),
            pltpu.SemaphoreType.DMA((12,)),
            pltpu.SemaphoreType.DMA((4,)),
            pltpu.SemaphoreType.DMA((15,)),
        ],
        compiler_params=params(56),
        name="pre",
    )(own, from_core, from_chip, from_both, mod, gains, *weights)

    recv = lax.all_to_all(send, seq, 0, 0, tiled=True)
    nz = shifted(slabs, "z")
    keys = IMAGE_KEYS + TEXT_KEYS
    dkv, odq = pl.pallas_call(
        attention_kernel,
        out_shape=[shape((keys, 128), BF16), shape((BLOCKS * CTL_Q, 128), BF16)],
        in_specs=[SMEM, VMEM, ANY],
        out_specs=[VMEM] * 2,
        scratch_shapes=[
            pltpu.VMEM((keys, 128), BF16),
            pltpu.VMEM((HEAD, keys), BF16),
            pltpu.VMEM((HEAD, keys), BF16),
            pltpu.VMEM((BLOCKS * CTL_Q, 128), BF16),
            pltpu.VMEM((keys, TQ), F32),
            pltpu.VMEM((keys, 128), F32),
        ],
        compiler_params=params(32),
        cost_estimate=pl.CostEstimate(flops=40_000_000_000, bytes_accessed=3_200_000, transcendentals=8_400_000),
        name="attention",
    )(role, recv, nz[3])
    back = pl.pallas_call(
        scatter_kernel,
        out_shape=shape((BLOCKS, CHUNK, 128), BF16),
        in_specs=[SMEM] + [VMEM] * 2 + [ANY] * 2,
        out_specs=VMEM,
        compiler_params=params(16),
        name="scatter",
    )(role, dkv, odq, *nz[1:3])
    back = lax.all_to_all(back, seq, 0, 0, tiled=True)

    ctl_rows = pl.pallas_call(
        head_back_ctl_kernel,
        out_shape=shape((IMG, 4 * WIDTH), BF16),
        in_specs=[VMEM] * 3,
        out_specs=VMEM,
        compiler_params=params(16),
        name="head_back_ctl",
    )(back, proj, gains)
    blocks = shifted([ctl_rows] * 4, "z")
    mine0, mine1, theirs0, theirs1 = pl.pallas_call(
        post_kernel,
        out_shape=[rows] * 4,
        in_specs=[VMEM] * 4 + [HBM] * 2 + [VMEM] + [HBM] * 6,
        out_specs=[ANY] * 4,
        scratch_shapes=[
            pltpu.VMEM((3, 3, D, WIDTH), BF16),
            pltpu.VMEM((3, WIDTH, D), BF16),
            pltpu.VMEM((IMG + TXT, 4 * WIDTH), BF16),
            pltpu.VMEM((2 * IMG + TXT, D), F32),
            pltpu.VMEM((2 * IMG + TXT, 128), F32),
            pltpu.VMEM((4, ROWS, IMG), BF16),
            pltpu.SemaphoreType.DMA((12,)),
            pltpu.SemaphoreType.DMA((2,)),
            pltpu.SemaphoreType.DMA((12,)),
        ],
        compiler_params=params(54),
        cost_estimate=pl.CostEstimate(flops=14_000_000_000, bytes_accessed=30_000_000, transcendentals=0),
        name="post",
    )(back, proj, gains, ctl_rows, xhat, rstd, mod, *weights)
    terms = pl.pallas_call(
        weight_kernel,
        out_shape=shape((4, PIECE, 4 * WIDTH), BF16),
        in_specs=[VMEM] * 8,
        out_specs=VMEM,
        compiler_params=params(24),
        cost_estimate=pl.CostEstimate(flops=3_000_000_000, bytes_accessed=5_000_000, transcendentals=0),
        name="weight",
    )(*nz, *blocks)
    got1 = lax.ppermute(theirs1, "tp", other_core)
    got0 = lax.ppermute(theirs0, "tp", other_core)
    passed = (mine1.astype(F32) + got1.astype(F32)).astype(BF16)
    passed = lax.ppermute(passed, "tp", other_chip)
    terms = lax.all_to_all(terms, "y", 0, 0, tiled=True)
    mine, theirs = pl.pallas_call(
        weight_sum_kernel,
        out_shape=[shape((PIECE // 2, 4 * WIDTH), F32), shape((PIECE // 2, 4 * WIDTH), BF16)],
        in_specs=[VMEM],
        out_specs=[VMEM] * 2,
        compiler_params=params(16),
        name="weight_sum",
    )(terms)
    theirs = lax.ppermute(theirs, "w", [(0, 1), (1, 0)])
    grad_qkv, grad_out = pl.pallas_call(
        weight_out_kernel,
        out_shape=[shape((3, PIECE // 2, WIDTH), F32), shape((PIECE // 2, WIDTH), F32)],
        in_specs=[VMEM] * 2,
        out_specs=[VMEM] * 2,
        compiler_params=params(16),
        name="weight_out",
    )(mine, theirs)

    y_img, d_img, d_ctl, y_txt, d_txt = pl.pallas_call(
        final_kernel,
        out_shape=[shape((SHARE, IMG), BF16)] * 3 + [shape((TXT, SHARE), BF16)] * 2,
        in_specs=[VMEM] * 7,
        out_specs=[VMEM] * 5,
        compiler_params=params(16),
        name="final",
    )(img.T, dy_img.T, txt, dy_txt, mine0, got0, passed)
    return y_img.T, y_txt, d_img.T, d_txt, d_ctl.T, grad_qkv.transpose(1, 0, 2), grad_out.T


def solution(mesh):
    fine = Mesh(mesh.devices.reshape(4, 4, 2, 4), ("z", "y", "w", "tp"))
    seq = ("z", "y", "w")
    rows = P(seq, "tp")
    qkv = P(None, None, "tp")
    out = P("tp", None)
    in_specs = (rows,) * 5 + (P(), P(), P(), qkv, out, qkv, out, qkv, out)
    out_specs = (rows,) * 5 + (P(seq, None, "tp"), P("tp", seq))
    return jax.shard_map(
        per_device, mesh=fine, in_specs=in_specs, out_specs=out_specs, check_vma=False
    )
```

```python
import jax
import jax.numpy as jnp
from jax import lax
from jax.experimental import pallas as pl
from jax.experimental.pallas import tpu as pltpu
from jax.sharding import Mesh, PartitionSpec as P

EPS = 1e-06
HEAD = 64
HEADS = 6
WIDTH = HEADS * HEAD
D = 2432
SHARE = 608
PIECE = 152
ROWS = 3 * SHARE + PIECE
IMG = 128
TXT = 16
BLOCKS = 32
CHUNK = 192
IMAGE_KEYS = BLOCKS * IMG
TEXT_KEYS = BLOCKS * TXT
MAIN_Q = 48
CTL_Q = 64
MAIN_PARTS = 3
CTL_PARTS = 2
CTL_AT = HEADS * MAIN_PARTS
TQ = 512
TK = 512
F32 = jnp.float32
BF16 = jnp.bfloat16
NT = (((1,), (1,)), ((), ()))
VMEM = pl.BlockSpec(memory_space=pltpu.VMEM)
SMEM = pl.BlockSpec(memory_space=pltpu.SMEM)
ANY = pl.BlockSpec(memory_space=pl.ANY)
HBM = pl.BlockSpec(memory_space=pltpu.HBM)


def params(mib):
    return pltpu.CompilerParams(vmem_limit_bytes=mib * 1024 * 1024)


def dot(a, b):
    return jnp.dot(a, b, preferred_element_type=F32)


def dot_nt(a, b):
    return lax.dot_general(a, b, NT, preferred_element_type=F32)


def head(values, h):
    return values[:, h * HEAD : (h + 1) * HEAD]


def inverse_rms(values):
    return lax.rsqrt(jnp.mean(values * values, axis=-1, keepdims=True) + EPS)


def spread_text(packed):
    return jnp.concatenate([packed] + [pltpu.roll(packed, 128 - 32 * a, 1) for a in (1, 2, 3)], 0)


def pack_text(columns):
    pieces = [columns[PIECE * a : PIECE * (a + 1)] for a in range(4)]
    return pieces[0] + sum(pltpu.roll(pieces[a], 32 * a, 1) for a in (1, 2, 3))


def weight_copies(sources, wq, wo, sems):
    return [
        (
            pltpu.make_async_copy(sources[s], wq.at[s], sems.at[s]),
            pltpu.make_async_copy(sources[3 + s], wo.at[s], sems.at[3 + s]),
        )
        for s in range(3)
    ]


def pack_kernel(img, ctl, dy, txt, dy_txt, out, text_rows, sems):
    copies = [
        pltpu.make_async_copy(part, text_rows.at[i], sems.at[3 + i]) for i, part in enumerate((txt, dy_txt))
    ] + [
        pltpu.make_async_copy(part, out.at[pl.ds(SHARE * i, SHARE)], sems.at[i])
        for i, part in enumerate((img, ctl, dy))
    ]
    for copy in copies:
        copy.start()
    copies[0].wait()
    copies[1].wait()
    text = text_rows[...].reshape(2 * TXT, SHARE).astype(F32)
    text = jnp.concatenate([text, jnp.zeros((IMG - 2 * TXT, SHARE), F32)], 0)
    text = jnp.concatenate([text, jnp.zeros((IMG, 640 - SHARE), F32)], 1)
    out[3 * SHARE :, :] = pack_text(text.T).astype(BF16)
    for copy in copies[2:]:
        copy.wait()


class Results:
    def __init__(self, sems):
        self.sems, self.copies = sems, []

    def send(self, source, target):
        copy = pltpu.make_async_copy(source, target, self.sems.at[len(self.copies)])
        copy.start()
        self.copies.append(copy)

    def finish(self):
        for copy in self.copies:
            copy.wait()


def pre_kernel(
    in0, in1, in2, in3, mod, gains, wq_img, wq_txt, wq_ctl, wo_img, wo_txt, wo_ctl,
    send, proj, xhat, rstd, nz0, nz1, nz2, nz3,
    wq, wo, gat, nz, sems,
):
    copies = weight_copies((wq_img, wq_txt, wq_ctl, wo_img, wo_txt, wo_ctl), wq, wo, sems)
    for s in range(3):
        copies[s][0].start()
        copies[s][1].start()

    for i, part in enumerate((in0, in1, in2, in3)):
        gat[lax.axis_index("tp") ^ i] = part[...]

    def rows(slab):
        return gat[:, SHARE * slab : SHARE * (slab + 1), :].reshape(D, IMG).T.astype(F32)

    def stream(s, x, e, at):
        count = x.shape[0]
        centered = x - jnp.mean(x, axis=-1, keepdims=True)
        inverse = lax.rsqrt(jnp.mean(centered * centered, axis=-1, keepdims=True) + EPS)
        standard = centered * inverse
        xhat[at : at + count, :] = standard
        rstd[at : at + count, :] = jnp.broadcast_to(inverse, (count, 128))
        n = (standard * (1.0 + mod[s, 1:2, :]) + mod[s, 0:1, :]).astype(BF16)
        copies[s][0].wait()
        pq = dot(n, wq[s, 0])
        pk = dot(n, wq[s, 1])
        pv = dot(n, wq[s, 2])
        proj[at : at + count, 0:WIDTH] = pq
        proj[at : at + count, WIDTH : 2 * WIDTH] = pk
        copies[s][1].wait()
        g = dot_nt(e, wo[s])
        kv, qg = [], []
        for h in range(HEADS):
            q_h, k_h = head(pq, h), head(pk, h)
            q_h = q_h * inverse_rms(q_h) * (gains[s, 0:1, :] * 0.125)
            k_h = k_h * inverse_rms(k_h) * gains[s, 1:2, :]
            kv.append(jnp.concatenate([k_h, head(pv, h)], 1).astype(BF16))
            qg.append(jnp.concatenate([q_h, head(g, h)], 1).astype(BF16))
        return n, kv, qg

    dy = rows(2)
    text = jnp.concatenate([spread_text(gat[c, 3 * SHARE :, :].astype(F32)) for c in range(4)], 0).astype(BF16).T.astype(F32)
    e_img = (mod[0, 2:3, :] * dy).astype(BF16)
    n, kv, qg = stream(0, rows(0), e_img, 0)
    for h in range(HEADS):
        for t in range(MAIN_PARTS):
            to = MAIN_PARTS * h + t
            send[to, 0:IMG, :] = kv[h]
            last = min(IMG, MAIN_Q * (t + 1))
            send[to, IMG + TXT : IMG + TXT + last - MAIN_Q * t, :] = qg[h][MAIN_Q * t : last]
    e_txt = (mod[1, 2:3, :] * text[TXT : 2 * TXT]).astype(BF16)
    n, kv, qg = stream(1, text[0:TXT], e_txt, IMG)
    for h in range(HEADS):
        for t in range(MAIN_PARTS):
            send[MAIN_PARTS * h + t, IMG : IMG + TXT, :] = kv[h]
        send[MAIN_PARTS * h + 2, CHUNK - TXT : CHUNK, :] = qg[h]
    e_ctl = mod[2, 2:3, :] * dy
    n, kv, qg = stream(2, rows(1), e_ctl.astype(BF16), IMG + TXT)
    for h in range(HEADS):
        for u in range(CTL_PARTS):
            to = CTL_AT + CTL_PARTS * h + u
            send[to, 0:IMG, :] = kv[h]
            send[to, IMG:CHUNK, :] = qg[h][CTL_Q * u : CTL_Q * (u + 1)]
    for to in range(CTL_AT + CTL_PARTS * HEADS, BLOCKS):
        send[to] = jnp.zeros((CHUNK, 128), BF16)
    nz[:, 0] = n.T.reshape(4, SHARE, IMG)
    nz[:, 1] = e_ctl.astype(BF16).T.reshape(4, SHARE, IMG)
    for d, out in enumerate((nz0, nz1, nz2, nz3)):
        out[...] = nz[lax.rem(lax.axis_index("z") + d, 4)]


def attention_kernel(role, recv, after, dkv_out, odq, kv, kt, vt, qg, probs, dkv):
    is_main = role[0]
    live = role[1]

    for b in range(BLOCKS):
        kv[IMG * b : IMG * (b + 1), :] = recv[b, 0:IMG, :]

    @pl.when(is_main == 1)
    def _():
        for b in range(BLOCKS):
            kv[IMAGE_KEYS + TXT * b : IMAGE_KEYS + TXT * (b + 1), :] = recv[b, IMG : IMG + TXT, :]
            qg[MAIN_Q * b : MAIN_Q * (b + 1), :] = recv[b, IMG + TXT : CHUNK, :]

    @pl.when(is_main == 0)
    def _():
        kv[IMAGE_KEYS:, :] = jnp.zeros((TEXT_KEYS, 128), BF16)
        for b in range(BLOCKS):
            qg[CTL_Q * b : CTL_Q * (b + 1), :] = recv[b, IMG:CHUNK, :]

    for i in range((IMAGE_KEYS + TEXT_KEYS) // 128):
        block = kv[128 * i : 128 * (i + 1), :].T
        kt[:, 128 * i : 128 * (i + 1)] = block[0:HEAD]
        vt[:, 128 * i : 128 * (i + 1)] = block[HEAD:128]
    dkv[...] = jnp.zeros_like(dkv)
    zeros_half = jnp.zeros((HEAD, TQ), BF16)
    low_lanes = lax.broadcasted_iota(jnp.int32, (TQ, 128), 1) < HEAD

    def q_tile(i, carry):
        q_at = pl.multiple_of(i * TQ, TQ)
        tile = qg[pl.ds(q_at, TQ), :]
        tile_t = tile.T
        g_t = tile_t[HEAD:128].astype(F32)
        q_rhs = jnp.concatenate([tile_t[0:HEAD], zeros_half], 0)
        g_rhs = jnp.concatenate([zeros_half, tile_t[HEAD:128]], 0)
        tile = tile.astype(F32)
        q_only = jnp.where(low_lanes, tile, 0.0).astype(BF16)
        g_only = jnp.where(low_lanes, 0.0, tile).astype(BF16)
        qg_rhs = jnp.concatenate([q_only, g_only], 0)

        def forward(at, state, masked):
            total, o_t = state
            p = jnp.exp(dot(kv[pl.ds(at, TK), :], q_rhs))
            if masked:
                p = jnp.where(lax.broadcasted_iota(jnp.int32, (TK, TQ), 0) < live, p, 0.0)
            probs[pl.ds(at, TK), :] = p
            total = total + jnp.sum(p.reshape(TK // 8, 8, TQ), 0)
            o_t = o_t + dot(vt[:, pl.ds(at, TK)], p.astype(BF16))
            return total, o_t

        state = (jnp.zeros((8, TQ), F32), jnp.zeros((HEAD, TQ), F32))
        state = lax.fori_loop(
            0, IMAGE_KEYS // TK, lambda j, c: forward(pl.multiple_of(j * TK, TK), c, False), state,
            unroll=8,
        )
        total, o_t = lax.fori_loop(0, is_main, lambda j, c: forward(IMAGE_KEYS, c, True), state)
        inverse = 1.0 / jnp.sum(total, axis=0, keepdims=True)
        o_t = (o_t * inverse).astype(BF16).astype(F32)
        delta = jnp.sum(g_t * o_t, axis=0, keepdims=True)

        def backward(at, dq_t):
            p = probs[pl.ds(at, TK), :] * inverse
            ds = (p * (dot(kv[pl.ds(at, TK), :], g_rhs) - delta)).astype(BF16)
            dkv[pl.ds(at, TK), :] += dot(jnp.concatenate([ds, p.astype(BF16)], 1), qg_rhs)
            return dq_t + dot(kt[:, pl.ds(at, TK)], ds)

        dq_t = jnp.zeros((HEAD, TQ), F32)
        dq_t = lax.fori_loop(
            0, IMAGE_KEYS // TK, lambda j, c: backward(pl.multiple_of(j * TK, TK), c), dq_t, unroll=8
        )
        dq_t = lax.fori_loop(0, is_main, lambda j, c: backward(IMAGE_KEYS, c), dq_t)
        odq[pl.ds(q_at, TQ), :] = jnp.concatenate([o_t, dq_t * 0.125], 0).astype(BF16).T
        return carry

    tiles = jnp.where(is_main == 1, BLOCKS * MAIN_Q // TQ, BLOCKS * CTL_Q // TQ)
    lax.fori_loop(0, tiles, q_tile, 0)

    dkv_out[...] = dkv[...].astype(BF16)


def scatter_kernel(role, dkv, odq, after0, after1, out):
    for b in range(BLOCKS):
        out[b, 0:IMG, :] = dkv[IMG * b : IMG * (b + 1), :]

    @pl.when(role[0] == 1)
    def _():
        for b in range(BLOCKS):
            out[b, IMG : IMG + TXT, :] = dkv[IMAGE_KEYS + TXT * b : IMAGE_KEYS + TXT * (b + 1), :]
            out[b, IMG + TXT : CHUNK, :] = odq[MAIN_Q * b : MAIN_Q * (b + 1), :]

    @pl.when(role[0] == 0)
    def _():
        for b in range(BLOCKS):
            out[b, IMG:CHUNK, :] = odq[CTL_Q * b : CTL_Q * (b + 1), :]


def head_norm_back(x, gain, dy):
    inverse = inverse_rms(x)
    dy = dy * gain
    return inverse * dy - x * (inverse * inverse * inverse * jnp.mean(x * dy, axis=-1, keepdims=True))


def head_back(s, at, count, dkv, odq, proj, gains):
    o, dq, dk, dv = [], [], [], []
    for h in range(HEADS):
        x_q = proj[at : at + count, h * HEAD : (h + 1) * HEAD]
        x_k = proj[at : at + count, WIDTH + h * HEAD : WIDTH + (h + 1) * HEAD]
        o.append(odq[h][:, 0:HEAD])
        dq.append(head_norm_back(x_q, gains[s, 0:1, :], odq[h][:, HEAD:128]))
        dk.append(head_norm_back(x_k, gains[s, 1:2, :], dkv[h][:, 0:HEAD]))
        dv.append(dkv[h][:, HEAD:128])
    return [jnp.concatenate(parts, 1).astype(BF16) for parts in (dq, dk, dv, o)]


def head_back_ctl_kernel(recv, proj, gains, out):
    dkv, odq = [], []
    for h in range(HEADS):
        parts = [recv[CTL_AT + CTL_PARTS * h + u].astype(F32) for u in range(CTL_PARTS)]
        dkv.append(parts[0][0:IMG] + parts[1][0:IMG])
        odq.append(jnp.concatenate([parts[0][IMG:], parts[1][IMG:]], 0))
    for j, part in enumerate(head_back(2, IMG + TXT, IMG, dkv, odq, proj, gains)):
        out[:, j * WIDTH : (j + 1) * WIDTH] = part


def head_back_main(recv, proj, gains, main):
    kv_img, kv_txt, oq_img, oq_txt = [], [], [], []
    for h in range(HEADS):
        parts = [recv[MAIN_PARTS * h + t].astype(F32) for t in range(MAIN_PARTS)]
        kv = parts[0][0 : IMG + TXT] + parts[1][0 : IMG + TXT] + parts[2][0 : IMG + TXT]
        kv_img.append(kv[0:IMG])
        kv_txt.append(kv[IMG:])
        oq_img.append(
            jnp.concatenate(
                [parts[0][IMG + TXT :], parts[1][IMG + TXT :], parts[2][IMG + TXT : CHUNK - TXT]], 0
            )
        )
        oq_txt.append(parts[2][CHUNK - TXT :])
    for j, part in enumerate(head_back(0, 0, IMG, kv_img, oq_img, proj, gains)):
        main[0:IMG, j * WIDTH : (j + 1) * WIDTH] = part
    for j, part in enumerate(head_back(1, IMG, TXT, kv_txt, oq_txt, proj, gains)):
        main[IMG:, j * WIDTH : (j + 1) * WIDTH] = part


def back(s, dq, dk, dv, o, wq, wo, mod, standard, inverse):
    u = dot_nt(dq, wq[0]) + dot_nt(dk, wq[1]) + dot_nt(dv, wq[2])
    u = u * (1.0 + mod[s, 1:2, :])
    u = u - jnp.mean(u, axis=-1, keepdims=True) - standard * jnp.mean(u * standard, axis=-1, keepdims=True)
    return u * inverse, mod[s, 2:3, :] * dot(o, wo[...])


def slab(values):
    return values.astype(BF16).T.reshape(4, SHARE, IMG)


def post_kernel(
    recv, proj, gains, ctl_rows, xhat_in, rstd_in, mod, wq_img, wq_txt, wq_ctl, wo_img, wo_txt, wo_ctl,
    mine0, mine1, theirs0, theirs1, token,
    wq, wo, main, xhat, rstd, slabs, sems, in_sems, out_sems,
):
    arrivals = [
        pltpu.make_async_copy(xhat_in, xhat, in_sems.at[0]),
        pltpu.make_async_copy(rstd_in, rstd, in_sems.at[1]),
    ]
    for copy in arrivals:
        copy.start()
    results = Results(out_sems)
    token[...] = jnp.zeros_like(token)
    copies = weight_copies((wq_img, wq_txt, wq_ctl, wo_img, wo_txt, wo_ctl), wq, wo, sems)
    for copy in (copies[2][0], copies[2][1], copies[0][0]):
        copy.start()

    def stream(s, parts, at, later):
        count = parts[0].shape[0]
        copies[s][0].wait()
        copies[s][1].wait()
        for copy in later:
            copy.start()
        return back(s, *parts, wq.at[s], wo.at[s], mod, xhat[at : at + count, :], rstd[at : at + count, 0:1])

    def joint(at, count):
        return [main[at : at + count, j * WIDTH : (j + 1) * WIDTH] for j in range(4)]

    def leave(at, count):
        for other, out in enumerate((mine0, theirs0, mine1, theirs1)):
            results.send(slabs.at[lax.axis_index("tp") ^ other, pl.ds(at, count)], out.at[pl.ds(at, count)])

    head_back_main(recv, proj, gains, main)
    for copy in arrivals:
        copy.wait()
    u, y_ctl = stream(2, [ctl_rows[:, j * WIDTH : (j + 1) * WIDTH] for j in range(4)], IMG + TXT, (copies[0][1], copies[1][0]))
    slabs[:, 2 * SHARE : 3 * SHARE, :] = slab(u)
    leave(2 * SHARE, SHARE)
    u, y = stream(0, joint(0, IMG), 0, (copies[1][1],))
    slabs[:, SHARE : 2 * SHARE, :] = slab(u)
    slabs[:, 0:SHARE, :] = slab(y + y_ctl)
    leave(0, 2 * SHARE)
    u, y = stream(1, joint(IMG, TXT), IMG, ())
    text = jnp.concatenate([y, u, jnp.zeros((IMG - 2 * TXT, D), F32)], 0).astype(BF16).T.astype(F32)
    for c in range(4):
        slabs[c, 3 * SHARE :, :] = pack_text(text[SHARE * c : SHARE * (c + 1)]).astype(BF16)
    leave(3 * SHARE, PIECE)
    results.finish()


def weight_kernel(nz0, nz1, nz2, nz3, b0, b1, b2, b3, after, out):
    nz, blocks = (nz0, nz1, nz2, nz3), (b0, b1, b2, b3)
    total = jnp.concatenate(
        [
            dot(
                jnp.concatenate([r[j] for r in nz], 1),
                jnp.concatenate([r[:, 3 * j * WIDTH : (3 + j) * WIDTH] for r in blocks], 0),
            )
            for j in range(2)
        ],
        1,
    )
    for p in range(4):
        out[p] = total[PIECE * p : PIECE * (p + 1)].astype(BF16)


def weight_sum_kernel(terms, mine, theirs):
    half = PIECE // 2
    low = lax.axis_index("w") == 0
    total = sum(terms[p].astype(F32) for p in range(4))
    first, second = total[0:half], total[half:]
    mine[...] = jnp.where(low, first, second)
    theirs[...] = jnp.where(low, second, first).astype(BF16)


def weight_out_kernel(mine, other, qkv, out):
    for j in range(4):
        columns = slice(WIDTH * j, WIDTH * (j + 1))
        total = mine[:, columns] + other[:, columns].astype(F32)
        if j < 3:
            qkv[j] = total
        else:
            out[...] = total


def final_kernel(img, dy, txt, dy_txt, part0, part1, part2, y_img, d_img, d_ctl, y_txt, d_txt):
    total = part0[...].astype(F32) + part1[...].astype(F32) + part2[...].astype(F32)
    y_img[...] = (img[...].astype(F32) + total[0:SHARE]).astype(BF16)
    d_img[...] = (dy[...].astype(F32) + total[SHARE : 2 * SHARE]).astype(BF16)
    d_ctl[...] = total[2 * SHARE : 3 * SHARE].astype(BF16)
    text = jnp.concatenate([spread_text(total[3 * SHARE :]), jnp.zeros((640 - SHARE, IMG), F32)], 0).T
    y_txt[...] = (txt[...].astype(F32) + text[0:TXT, 0:SHARE]).astype(BF16)
    d_txt[...] = (dy_txt[...].astype(F32) + text[TXT : 2 * TXT, 0:SHARE]).astype(BF16)


def shifted(parts, axis):
    return [parts[0]] + [
        lax.ppermute(parts[d], axis, [(i, (i + d) % 4) for i in range(4)]) for d in (1, 2, 3)
    ]


def per_device(
    img, txt, ctl, dy_img, dy_txt, live_text_length, modulation, query_key_gains,
    w_qkv_img, wo_img, w_qkv_txt, wo_txt, w_qkv_ctl, wo_ctl,
):
    seq = ("z", "y", "w")
    seq_pos = lax.axis_index(seq)
    role = jnp.stack([(seq_pos < CTL_AT).astype(jnp.int32), live_text_length[0]])
    mod, gains = modulation, query_key_gains
    weights = (
        w_qkv_img.transpose(1, 0, 2), w_qkv_txt.transpose(1, 0, 2), w_qkv_ctl.transpose(1, 0, 2),
        wo_img, wo_txt, wo_ctl,
    )
    shape = jax.ShapeDtypeStruct
    rows = shape((ROWS, IMG), BF16)
    other_core = [(i, i ^ 1) for i in range(4)]
    other_chip = [(i, i ^ 2) for i in range(4)]

    own = pl.pallas_call(
        pack_kernel,
        out_shape=rows,
        in_specs=[HBM] * 5,
        out_specs=VMEM,
        scratch_shapes=[pltpu.VMEM((2, TXT, SHARE), BF16), pltpu.SemaphoreType.DMA((5,))],
        compiler_params=pltpu.CompilerParams(vmem_limit_bytes=63_400_000),
        name="pack",
    )(img.T, ctl.T, dy_img.T, txt, dy_txt)
    from_chip = lax.ppermute(own, "tp", other_chip)
    from_core = lax.ppermute(own, "tp", other_core)
    from_both = lax.ppermute(from_chip, "tp", other_core)

    send, proj, xhat, rstd, *slabs = pl.pallas_call(
        pre_kernel,
        out_shape=[
            shape((BLOCKS, CHUNK, 128), BF16),
            shape((2 * IMG + TXT, 2 * WIDTH), F32),
            shape((2 * IMG + TXT, D), F32),
            shape((2 * IMG + TXT, 128), F32),
        ] + [shape((2, SHARE, IMG), BF16)] * 4,
        in_specs=[VMEM] * 6 + [HBM] * 6,
        out_specs=[VMEM] * 8,
        scratch_shapes=[
            pltpu.VMEM((3, 3, D, WIDTH), BF16),
            pltpu.VMEM((3, WIDTH, D), BF16),
            pltpu.VMEM((4, ROWS, IMG), BF16),
            pltpu.VMEM((4, 2, SHARE, IMG), BF16),
            pltpu.SemaphoreType.DMA((6,)),
        ],
        compiler_params=params(56),
        name="pre",
    )(own, from_core, from_chip, from_both, mod, gains, *weights)

    recv = lax.all_to_all(send, seq, 0, 0, tiled=True)
    nz = shifted(slabs, "z")
    keys = IMAGE_KEYS + TEXT_KEYS
    dkv, odq = pl.pallas_call(
        attention_kernel,
        out_shape=[shape((keys, 128), BF16), shape((BLOCKS * CTL_Q, 128), BF16)],
        in_specs=[SMEM, VMEM, ANY],
        out_specs=[VMEM] * 2,
        scratch_shapes=[
            pltpu.VMEM((keys, 128), BF16),
            pltpu.VMEM((HEAD, keys), BF16),
            pltpu.VMEM((HEAD, keys), BF16),
            pltpu.VMEM((BLOCKS * CTL_Q, 128), BF16),
            pltpu.VMEM((keys, TQ), F32),
            pltpu.VMEM((keys, 128), F32),
        ],
        compiler_params=params(32),
        cost_estimate=pl.CostEstimate(flops=40_000_000_000, bytes_accessed=3_200_000, transcendentals=8_400_000),
        name="attention",
    )(role, recv, nz[3])
    back = pl.pallas_call(
        scatter_kernel,
        out_shape=shape((BLOCKS, CHUNK, 128), BF16),
        in_specs=[SMEM] + [VMEM] * 2 + [ANY] * 2,
        out_specs=VMEM,
        compiler_params=params(16),
        name="scatter",
    )(role, dkv, odq, *nz[1:3])
    back = lax.all_to_all(back, seq, 0, 0, tiled=True)

    ctl_rows = pl.pallas_call(
        head_back_ctl_kernel,
        out_shape=shape((IMG, 4 * WIDTH), BF16),
        in_specs=[VMEM] * 3,
        out_specs=VMEM,
        compiler_params=params(16),
        name="head_back_ctl",
    )(back, proj, gains)
    blocks = shifted([ctl_rows] * 4, "z")
    mine0, mine1, theirs0, theirs1, token = pl.pallas_call(
        post_kernel,
        out_shape=[rows] * 4 + [shape((8, 128), F32)],
        in_specs=[VMEM] * 4 + [HBM] * 2 + [VMEM] + [HBM] * 6,
        out_specs=[ANY] * 4 + [VMEM],
        scratch_shapes=[
            pltpu.VMEM((3, 3, D, WIDTH), BF16),
            pltpu.VMEM((3, WIDTH, D), BF16),
            pltpu.VMEM((IMG + TXT, 4 * WIDTH), BF16),
            pltpu.VMEM((2 * IMG + TXT, D), F32),
            pltpu.VMEM((2 * IMG + TXT, 128), F32),
            pltpu.VMEM((4, ROWS, IMG), BF16),
            pltpu.SemaphoreType.DMA((6,)),
            pltpu.SemaphoreType.DMA((2,)),
            pltpu.SemaphoreType.DMA((12,)),
        ],
        compiler_params=params(54),
        cost_estimate=pl.CostEstimate(flops=14_000_000_000, bytes_accessed=30_000_000, transcendentals=0),
        name="post",
    )(back, proj, gains, ctl_rows, xhat, rstd, mod, *weights)
    terms = pl.pallas_call(
        weight_kernel,
        out_shape=shape((4, PIECE, 4 * WIDTH), BF16),
        in_specs=[VMEM] * 8 + [SMEM],
        out_specs=VMEM,
        compiler_params=params(24),
        cost_estimate=pl.CostEstimate(flops=3_000_000_000, bytes_accessed=5_000_000, transcendentals=0),
        name="weight",
    )(*nz, *blocks, token)
    got1 = lax.ppermute(theirs1, "tp", other_core)
    got0 = lax.ppermute(theirs0, "tp", other_core)
    passed = (mine1.astype(F32) + got1.astype(F32)).astype(BF16)
    passed = lax.ppermute(passed, "tp", other_chip)
    terms = lax.all_to_all(terms, "y", 0, 0, tiled=True)
    mine, theirs = pl.pallas_call(
        weight_sum_kernel,
        out_shape=[shape((PIECE // 2, 4 * WIDTH), F32), shape((PIECE // 2, 4 * WIDTH), BF16)],
        in_specs=[VMEM],
        out_specs=[VMEM] * 2,
        compiler_params=params(16),
        name="weight_sum",
    )(terms)
    theirs = lax.ppermute(theirs, "w", [(0, 1), (1, 0)])
    grad_qkv, grad_out = pl.pallas_call(
        weight_out_kernel,
        out_shape=[shape((3, PIECE // 2, WIDTH), F32), shape((PIECE // 2, WIDTH), F32)],
        in_specs=[VMEM] * 2,
        out_specs=[VMEM] * 2,
        compiler_params=params(16),
        name="weight_out",
    )(mine, theirs)

    y_img, d_img, d_ctl, y_txt, d_txt = pl.pallas_call(
        final_kernel,
        out_shape=[shape((SHARE, IMG), BF16)] * 3 + [shape((TXT, SHARE), BF16)] * 2,
        in_specs=[VMEM] * 7,
        out_specs=[VMEM] * 5,
        compiler_params=params(16),
        name="final",
    )(img.T, dy_img.T, txt, dy_txt, mine0, got0, passed)
    return y_img.T, y_txt, d_img.T, d_txt, d_ctl.T, grad_qkv.transpose(1, 0, 2), grad_out.T


def solution(mesh):
    fine = Mesh(mesh.devices.reshape(4, 4, 2, 4), ("z", "y", "w", "tp"))
    seq = ("z", "y", "w")
    rows = P(seq, "tp")
    qkv = P(None, None, "tp")
    out = P("tp", None)
    in_specs = (rows,) * 5 + (P(), P(), P(), qkv, out, qkv, out, qkv, out)
    out_specs = (rows,) * 5 + (P(seq, None, "tp"), P("tp", seq))
    return jax.shard_map(
        per_device, mesh=fine, in_specs=in_specs, out_specs=out_specs, check_vma=False
    )
```

```python
import jax
import jax.numpy as jnp
from jax import lax
from jax.experimental import pallas as pl
from jax.experimental.pallas import tpu as pltpu
from jax.sharding import Mesh, PartitionSpec as P

EPS = 1e-06
HEAD = 64
HEADS = 6
WIDTH = HEADS * HEAD
D = 2432
SHARE = 608
PIECE = 152
ROWS = 3 * SHARE + PIECE
IMG = 128
TXT = 16
BLOCKS = 32
CHUNK = 192
IMAGE_KEYS = BLOCKS * IMG
TEXT_KEYS = BLOCKS * TXT
MAIN_Q = 48
CTL_Q = 64
MAIN_PARTS = 3
CTL_PARTS = 2
CTL_AT = HEADS * MAIN_PARTS
TQ = 512
TK = 512
F32 = jnp.float32
BF16 = jnp.bfloat16
NT = (((1,), (1,)), ((), ()))
VMEM = pl.BlockSpec(memory_space=pltpu.VMEM)
SMEM = pl.BlockSpec(memory_space=pltpu.SMEM)
ANY = pl.BlockSpec(memory_space=pl.ANY)
HBM = pl.BlockSpec(memory_space=pltpu.HBM)


def params(mib):
    return pltpu.CompilerParams(vmem_limit_bytes=mib * 1024 * 1024)


def dot(a, b):
    return jnp.dot(a, b, preferred_element_type=F32)


def dot_nt(a, b):
    return lax.dot_general(a, b, NT, preferred_element_type=F32)


def head(values, h):
    return values[:, h * HEAD : (h + 1) * HEAD]


def inverse_rms(values):
    return lax.rsqrt(jnp.mean(values * values, axis=-1, keepdims=True) + EPS)


def spread_text(packed):
    return jnp.concatenate([packed] + [pltpu.roll(packed, 128 - 32 * a, 1) for a in (1, 2, 3)], 0)


def pack_text(columns):
    pieces = [columns[PIECE * a : PIECE * (a + 1)] for a in range(4)]
    return pieces[0] + sum(pltpu.roll(pieces[a], 32 * a, 1) for a in (1, 2, 3))


def weight_copies(sources, wq, wo, sems):
    return [
        (
            pltpu.make_async_copy(sources[s], wq.at[s], sems.at[s]),
            pltpu.make_async_copy(sources[3 + s], wo.at[s], sems.at[3 + s]),
        )
        for s in range(3)
    ]


def order_kernel(after, *refs):
    pass


def ordered(arrays, after):
    return pl.pallas_call(
        order_kernel,
        out_shape=[jax.ShapeDtypeStruct(x.shape, x.dtype) for x in arrays],
        in_specs=[ANY] * (1 + len(arrays)),
        out_specs=[ANY] * len(arrays),
        input_output_aliases={1 + i: i for i in range(len(arrays))},
        compiler_params=params(1),
        name="order",
    )(after, *arrays)


def pack_kernel(img, ctl, dy, txt, dy_txt, out, text_rows, sems):
    copies = [
        pltpu.make_async_copy(part, text_rows.at[i], sems.at[3 + i]) for i, part in enumerate((txt, dy_txt))
    ] + [
        pltpu.make_async_copy(part, out.at[pl.ds(SHARE * i, SHARE)], sems.at[i])
        for i, part in enumerate((img, ctl, dy))
    ]
    for copy in copies:
        copy.start()
    copies[0].wait()
    copies[1].wait()
    text = text_rows[...].reshape(2 * TXT, SHARE).astype(F32)
    text = jnp.concatenate([text, jnp.zeros((IMG - 2 * TXT, SHARE), F32)], 0)
    text = jnp.concatenate([text, jnp.zeros((IMG, 640 - SHARE), F32)], 1)
    out[3 * SHARE :, :] = pack_text(text.T).astype(BF16)
    for copy in copies[2:]:
        copy.wait()


class Results:
    def __init__(self, sems):
        self.sems, self.copies = sems, []

    def send(self, source, target):
        copy = pltpu.make_async_copy(source, target, self.sems.at[len(self.copies)])
        copy.start()
        self.copies.append(copy)

    def finish(self):
        for copy in self.copies:
            copy.wait()


def pre_kernel(
    in0, in1, in2, in3, mod, gains, wq_img, wq_txt, wq_ctl, wo_img, wo_txt, wo_ctl,
    send, proj, xhat, rstd, nz0, nz1, nz2, nz3,
    wq, wo, gat, nz, sems,
):
    copies = weight_copies((wq_img, wq_txt, wq_ctl, wo_img, wo_txt, wo_ctl), wq, wo, sems)
    for s in range(3):
        copies[s][0].start()
        copies[s][1].start()

    for i, part in enumerate((in0, in1, in2, in3)):
        gat[lax.axis_index("tp") ^ i] = part[...]

    def rows(slab):
        return gat[:, SHARE * slab : SHARE * (slab + 1), :].reshape(D, IMG).T.astype(F32)

    def stream(s, x, e, at):
        count = x.shape[0]
        centered = x - jnp.mean(x, axis=-1, keepdims=True)
        inverse = lax.rsqrt(jnp.mean(centered * centered, axis=-1, keepdims=True) + EPS)
        standard = centered * inverse
        xhat[at : at + count, :] = standard.astype(BF16)
        rstd[at : at + count, :] = jnp.broadcast_to(inverse, (count, 128))
        n = (standard * (1.0 + mod[s, 1:2, :]) + mod[s, 0:1, :]).astype(BF16)
        copies[s][0].wait()
        pq = dot(n, wq[s, 0])
        pk = dot(n, wq[s, 1])
        pv = dot(n, wq[s, 2])
        proj[at : at + count, 0:WIDTH] = pq
        proj[at : at + count, WIDTH : 2 * WIDTH] = pk
        copies[s][1].wait()
        g = dot_nt(e, wo[s])
        kv, qg = [], []
        for h in range(HEADS):
            q_h, k_h = head(pq, h), head(pk, h)
            q_h = q_h * inverse_rms(q_h) * (gains[s, 0:1, :] * 0.125)
            k_h = k_h * inverse_rms(k_h) * gains[s, 1:2, :]
            kv.append(jnp.concatenate([k_h, head(pv, h)], 1).astype(BF16))
            qg.append(jnp.concatenate([q_h, head(g, h)], 1).astype(BF16))
        return n, kv, qg

    dy = rows(2)
    text = jnp.concatenate([spread_text(gat[c, 3 * SHARE :, :].astype(F32)) for c in range(4)], 0).astype(BF16).T.astype(F32)
    e_img = (mod[0, 2:3, :] * dy).astype(BF16)
    n, kv, qg = stream(0, rows(0), e_img, 0)
    for h in range(HEADS):
        for t in range(MAIN_PARTS):
            to = MAIN_PARTS * h + t
            send[to, 0:IMG, :] = kv[h]
            last = min(IMG, MAIN_Q * (t + 1))
            send[to, IMG + TXT : IMG + TXT + last - MAIN_Q * t, :] = qg[h][MAIN_Q * t : last]
    e_txt = (mod[1, 2:3, :] * text[TXT : 2 * TXT]).astype(BF16)
    n, kv, qg = stream(1, text[0:TXT], e_txt, IMG)
    for h in range(HEADS):
        for t in range(MAIN_PARTS):
            send[MAIN_PARTS * h + t, IMG : IMG + TXT, :] = kv[h]
        send[MAIN_PARTS * h + 2, CHUNK - TXT : CHUNK, :] = qg[h]
    e_ctl = mod[2, 2:3, :] * dy
    n, kv, qg = stream(2, rows(1), e_ctl.astype(BF16), IMG + TXT)
    for h in range(HEADS):
        for u in range(CTL_PARTS):
            to = CTL_AT + CTL_PARTS * h + u
            send[to, 0:IMG, :] = kv[h]
            send[to, IMG:CHUNK, :] = qg[h][CTL_Q * u : CTL_Q * (u + 1)]
    for to in range(CTL_AT + CTL_PARTS * HEADS, BLOCKS):
        send[to] = jnp.zeros((CHUNK, 128), BF16)
    nz[:, 0] = n.T.reshape(4, SHARE, IMG)
    nz[:, 1] = e_ctl.astype(BF16).T.reshape(4, SHARE, IMG)
    for d, out in enumerate((nz0, nz1, nz2, nz3)):
        out[...] = nz[lax.rem(lax.axis_index("z") + d, 4)]


def attention_kernel(role, recv, dkv_out, odq, kv, kt, vt, qg, probs, dkv):
    is_main = role[0]
    live = role[1]

    for b in range(BLOCKS):
        kv[IMG * b : IMG * (b + 1), :] = recv[b, 0:IMG, :]

    @pl.when(is_main == 1)
    def _():
        for b in range(BLOCKS):
            kv[IMAGE_KEYS + TXT * b : IMAGE_KEYS + TXT * (b + 1), :] = recv[b, IMG : IMG + TXT, :]
            qg[MAIN_Q * b : MAIN_Q * (b + 1), :] = recv[b, IMG + TXT : CHUNK, :]

    @pl.when(is_main == 0)
    def _():
        kv[IMAGE_KEYS:, :] = jnp.zeros((TEXT_KEYS, 128), BF16)
        for b in range(BLOCKS):
            qg[CTL_Q * b : CTL_Q * (b + 1), :] = recv[b, IMG:CHUNK, :]

    for i in range((IMAGE_KEYS + TEXT_KEYS) // 128):
        block = kv[128 * i : 128 * (i + 1), :].T
        kt[:, 128 * i : 128 * (i + 1)] = block[0:HEAD]
        vt[:, 128 * i : 128 * (i + 1)] = block[HEAD:128]
    dkv[...] = jnp.zeros_like(dkv)
    zeros_half = jnp.zeros((HEAD, TQ), BF16)
    low_lanes = lax.broadcasted_iota(jnp.int32, (TQ, 128), 1) < HEAD

    def q_tile(i, carry):
        q_at = pl.multiple_of(i * TQ, TQ)
        tile = qg[pl.ds(q_at, TQ), :]
        tile_t = tile.T
        g_t = tile_t[HEAD:128].astype(F32)
        q_rhs = jnp.concatenate([tile_t[0:HEAD], zeros_half], 0)
        g_rhs = jnp.concatenate([zeros_half, tile_t[HEAD:128]], 0)
        tile = tile.astype(F32)
        q_only = jnp.where(low_lanes, tile, 0.0).astype(BF16)
        g_only = jnp.where(low_lanes, 0.0, tile).astype(BF16)
        qg_rhs = jnp.concatenate([q_only, g_only], 0)

        def forward(at, state, masked):
            total, o_t = state
            p = jnp.exp(dot(kv[pl.ds(at, TK), :], q_rhs))
            if masked:
                p = jnp.where(lax.broadcasted_iota(jnp.int32, (TK, TQ), 0) < live, p, 0.0)
            probs[pl.ds(at, TK), :] = p
            total = total + jnp.sum(p.reshape(TK // 8, 8, TQ), 0)
            o_t = o_t + dot(vt[:, pl.ds(at, TK)], p.astype(BF16))
            return total, o_t

        state = (jnp.zeros((8, TQ), F32), jnp.zeros((HEAD, TQ), F32))
        state = lax.fori_loop(
            0, IMAGE_KEYS // TK, lambda j, c: forward(pl.multiple_of(j * TK, TK), c, False), state,
            unroll=8,
        )
        total, o_t = lax.fori_loop(0, is_main, lambda j, c: forward(IMAGE_KEYS, c, True), state)
        inverse = 1.0 / jnp.sum(total, axis=0, keepdims=True)
        o_t = (o_t * inverse).astype(BF16).astype(F32)
        delta = jnp.sum(g_t * o_t, axis=0, keepdims=True)

        def backward(at, dq_t):
            p = probs[pl.ds(at, TK), :] * inverse
            ds = (p * (dot(kv[pl.ds(at, TK), :], g_rhs) - delta)).astype(BF16)
            dkv[pl.ds(at, TK), :] += dot(jnp.concatenate([ds, p.astype(BF16)], 1), qg_rhs)
            return dq_t + dot(kt[:, pl.ds(at, TK)], ds)

        dq_t = jnp.zeros((HEAD, TQ), F32)
        dq_t = lax.fori_loop(
            0, IMAGE_KEYS // TK, lambda j, c: backward(pl.multiple_of(j * TK, TK), c), dq_t, unroll=8
        )
        dq_t = lax.fori_loop(0, is_main, lambda j, c: backward(IMAGE_KEYS, c), dq_t)
        odq[pl.ds(q_at, TQ), :] = jnp.concatenate([o_t, dq_t * 0.125], 0).astype(BF16).T
        return carry

    tiles = jnp.where(is_main == 1, BLOCKS * MAIN_Q // TQ, BLOCKS * CTL_Q // TQ)
    lax.fori_loop(0, tiles, q_tile, 0)

    dkv_out[...] = dkv[...].astype(BF16)


def scatter_kernel(role, dkv, odq, after0, after1, after2, out):
    for b in range(BLOCKS):
        out[b, 0:IMG, :] = dkv[IMG * b : IMG * (b + 1), :]

    @pl.when(role[0] == 1)
    def _():
        for b in range(BLOCKS):
            out[b, IMG : IMG + TXT, :] = dkv[IMAGE_KEYS + TXT * b : IMAGE_KEYS + TXT * (b + 1), :]
            out[b, IMG + TXT : CHUNK, :] = odq[MAIN_Q * b : MAIN_Q * (b + 1), :]

    @pl.when(role[0] == 0)
    def _():
        for b in range(BLOCKS):
            out[b, IMG:CHUNK, :] = odq[CTL_Q * b : CTL_Q * (b + 1), :]


def head_norm_back(x, gain, dy):
    inverse = inverse_rms(x)
    dy = dy * gain
    return inverse * dy - x * (inverse * inverse * inverse * jnp.mean(x * dy, axis=-1, keepdims=True))


def head_back(s, at, count, dkv, odq, proj, gains):
    o, dq, dk, dv = [], [], [], []
    for h in range(HEADS):
        x_q = proj[at : at + count, h * HEAD : (h + 1) * HEAD]
        x_k = proj[at : at + count, WIDTH + h * HEAD : WIDTH + (h + 1) * HEAD]
        o.append(odq[h][:, 0:HEAD])
        dq.append(head_norm_back(x_q, gains[s, 0:1, :], odq[h][:, HEAD:128]))
        dk.append(head_norm_back(x_k, gains[s, 1:2, :], dkv[h][:, 0:HEAD]))
        dv.append(dkv[h][:, HEAD:128])
    return [jnp.concatenate(parts, 1).astype(BF16) for parts in (dq, dk, dv, o)]


def head_back_ctl_kernel(recv, proj, gains, out):
    dkv, odq = [], []
    for h in range(HEADS):
        parts = [recv[CTL_AT + CTL_PARTS * h + u].astype(F32) for u in range(CTL_PARTS)]
        dkv.append(parts[0][0:IMG] + parts[1][0:IMG])
        odq.append(jnp.concatenate([parts[0][IMG:], parts[1][IMG:]], 0))
    for j, part in enumerate(head_back(2, IMG + TXT, IMG, dkv, odq, proj, gains)):
        out[:, j * WIDTH : (j + 1) * WIDTH] = part


def head_back_main(recv, proj, gains, main):
    kv_img, kv_txt, oq_img, oq_txt = [], [], [], []
    for h in range(HEADS):
        parts = [recv[MAIN_PARTS * h + t].astype(F32) for t in range(MAIN_PARTS)]
        kv = parts[0][0 : IMG + TXT] + parts[1][0 : IMG + TXT] + parts[2][0 : IMG + TXT]
        kv_img.append(kv[0:IMG])
        kv_txt.append(kv[IMG:])
        oq_img.append(
            jnp.concatenate(
                [parts[0][IMG + TXT :], parts[1][IMG + TXT :], parts[2][IMG + TXT : CHUNK - TXT]], 0
            )
        )
        oq_txt.append(parts[2][CHUNK - TXT :])
    for j, part in enumerate(head_back(0, 0, IMG, kv_img, oq_img, proj, gains)):
        main[0:IMG, j * WIDTH : (j + 1) * WIDTH] = part
    for j, part in enumerate(head_back(1, IMG, TXT, kv_txt, oq_txt, proj, gains)):
        main[IMG:, j * WIDTH : (j + 1) * WIDTH] = part


def back(s, dq, dk, dv, o, wq, wo, mod, standard, inverse):
    u = dot_nt(dq, wq[0]) + dot_nt(dk, wq[1]) + dot_nt(dv, wq[2])
    u = u * (1.0 + mod[s, 1:2, :])
    u = u - jnp.mean(u, axis=-1, keepdims=True) - standard * jnp.mean(u * standard, axis=-1, keepdims=True)
    return u * inverse, mod[s, 2:3, :] * dot(o, wo[...])


def slab(values):
    return values.astype(BF16).T.reshape(4, SHARE, IMG)


def post_kernel(
    recv, proj, gains, ctl_rows, xhat_in, rstd_in, mod, wq_img, wq_txt, wq_ctl, wo_img, wo_txt, wo_ctl,
    mine0, mine1, theirs0, theirs1, token,
    wq, wo, main, xhat, rstd, slabs, sems, in_sems, out_sems,
):
    arrivals = [
        pltpu.make_async_copy(xhat_in, xhat, in_sems.at[0]),
        pltpu.make_async_copy(rstd_in, rstd, in_sems.at[1]),
    ]
    for copy in arrivals:
        copy.start()
    results = Results(out_sems)
    token[...] = jnp.zeros_like(token)
    copies = weight_copies((wq_img, wq_txt, wq_ctl, wo_img, wo_txt, wo_ctl), wq, wo, sems)
    for copy in (copies[2][0], copies[2][1], copies[0][0]):
        copy.start()

    def stream(s, parts, at, later):
        count = parts[0].shape[0]
        copies[s][0].wait()
        copies[s][1].wait()
        for copy in later:
            copy.start()
        return back(s, *parts, wq.at[s], wo.at[s], mod, xhat[at : at + count, :].astype(F32), rstd[at : at + count, 0:1])

    def joint(at, count):
        return [main[at : at + count, j * WIDTH : (j + 1) * WIDTH] for j in range(4)]

    def leave(at, count):
        for other, out in enumerate((mine0, theirs0, mine1, theirs1)):
            results.send(slabs.at[lax.axis_index("tp") ^ other, pl.ds(at, count)], out.at[pl.ds(at, count)])

    head_back_main(recv, proj, gains, main)
    for copy in arrivals:
        copy.wait()
    u, y_ctl = stream(2, [ctl_rows[:, j * WIDTH : (j + 1) * WIDTH] for j in range(4)], IMG + TXT, (copies[0][1], copies[1][0]))
    slabs[:, 2 * SHARE : 3 * SHARE, :] = slab(u)
    leave(2 * SHARE, SHARE)
    u, y = stream(0, joint(0, IMG), 0, (copies[1][1],))
    slabs[:, SHARE : 2 * SHARE, :] = slab(u)
    slabs[:, 0:SHARE, :] = slab(y + y_ctl)
    leave(0, 2 * SHARE)
    u, y = stream(1, joint(IMG, TXT), IMG, ())
    text = jnp.concatenate([y, u, jnp.zeros((IMG - 2 * TXT, D), F32)], 0).astype(BF16).T.astype(F32)
    for c in range(4):
        slabs[c, 3 * SHARE :, :] = pack_text(text[SHARE * c : SHARE * (c + 1)]).astype(BF16)
    leave(3 * SHARE, PIECE)
    results.finish()


def weight_kernel(nz0, nz1, nz2, nz3, b0, b1, b2, b3, after, out):
    nz, blocks = (nz0, nz1, nz2, nz3), (b0, b1, b2, b3)
    total = jnp.concatenate(
        [
            dot(
                jnp.concatenate([r[j] for r in nz], 1),
                jnp.concatenate([r[:, 3 * j * WIDTH : (3 + j) * WIDTH] for r in blocks], 0),
            )
            for j in range(2)
        ],
        1,
    )
    for p in range(4):
        out[p] = total[PIECE * p : PIECE * (p + 1)].astype(BF16)


def weight_sum_kernel(terms, mine, theirs):
    half = PIECE // 2
    low = lax.axis_index("w") == 0
    total = sum(terms[p].astype(F32) for p in range(4))
    first, second = total[0:half], total[half:]
    mine[...] = jnp.where(low, first, second)
    theirs[...] = jnp.where(low, second, first).astype(BF16)


def weight_out_kernel(mine, other, qkv, out):
    for j in range(4):
        columns = slice(WIDTH * j, WIDTH * (j + 1))
        total = mine[:, columns] + other[:, columns].astype(F32)
        if j < 3:
            qkv[j] = total
        else:
            out[...] = total


def final_kernel(img, dy, txt, dy_txt, part0, part1, part2, y_img, d_img, d_ctl, y_txt, d_txt):
    total = part0[...].astype(F32) + part1[...].astype(F32) + part2[...].astype(F32)
    y_img[...] = (img[...].astype(F32) + total[0:SHARE]).astype(BF16)
    d_img[...] = (dy[...].astype(F32) + total[SHARE : 2 * SHARE]).astype(BF16)
    d_ctl[...] = total[2 * SHARE : 3 * SHARE].astype(BF16)
    text = jnp.concatenate([spread_text(total[3 * SHARE :]), jnp.zeros((640 - SHARE, IMG), F32)], 0).T
    y_txt[...] = (txt[...].astype(F32) + text[0:TXT, 0:SHARE]).astype(BF16)
    d_txt[...] = (dy_txt[...].astype(F32) + text[TXT : 2 * TXT, 0:SHARE]).astype(BF16)


def shifted(parts, axis):
    return [parts[0]] + [
        lax.ppermute(parts[d], axis, [(i, (i + d) % 4) for i in range(4)]) for d in (1, 2, 3)
    ]


def per_device(
    img, txt, ctl, dy_img, dy_txt, live_text_length, modulation, query_key_gains,
    w_qkv_img, wo_img, w_qkv_txt, wo_txt, w_qkv_ctl, wo_ctl,
):
    seq = ("z", "y", "w")
    seq_pos = lax.axis_index(seq)
    role = jnp.stack([(seq_pos < CTL_AT).astype(jnp.int32), live_text_length[0]])
    mod, gains = modulation, query_key_gains
    weights = (
        w_qkv_img.transpose(1, 0, 2), w_qkv_txt.transpose(1, 0, 2), w_qkv_ctl.transpose(1, 0, 2),
        wo_img, wo_txt, wo_ctl,
    )
    shape = jax.ShapeDtypeStruct
    rows = shape((ROWS, IMG), BF16)
    other_core = [(i, i ^ 1) for i in range(4)]
    other_chip = [(i, i ^ 2) for i in range(4)]

    own = pl.pallas_call(
        pack_kernel,
        out_shape=rows,
        in_specs=[HBM] * 5,
        out_specs=VMEM,
        scratch_shapes=[pltpu.VMEM((2, TXT, SHARE), BF16), pltpu.SemaphoreType.DMA((5,))],
        compiler_params=pltpu.CompilerParams(vmem_limit_bytes=63_400_000),
        name="pack",
    )(img.T, ctl.T, dy_img.T, txt, dy_txt)
    from_chip = lax.ppermute(own, "tp", other_chip)
    from_core = lax.ppermute(own, "tp", other_core)
    from_both = lax.ppermute(from_chip, "tp", other_core)

    send, proj, xhat, rstd, *slabs = pl.pallas_call(
        pre_kernel,
        out_shape=[
            shape((BLOCKS, CHUNK, 128), BF16),
            shape((2 * IMG + TXT, 2 * WIDTH), F32),
            shape((2 * IMG + TXT, D), BF16),
            shape((2 * IMG + TXT, 128), F32),
        ] + [shape((2, SHARE, IMG), BF16)] * 4,
        in_specs=[VMEM] * 6 + [HBM] * 6,
        out_specs=[VMEM] * 8,
        scratch_shapes=[
            pltpu.VMEM((3, 3, D, WIDTH), BF16),
            pltpu.VMEM((3, WIDTH, D), BF16),
            pltpu.VMEM((4, ROWS, IMG), BF16),
            pltpu.VMEM((4, 2, SHARE, IMG), BF16),
            pltpu.SemaphoreType.DMA((6,)),
        ],
        compiler_params=params(56),
        name="pre",
    )(own, from_core, from_chip, from_both, mod, gains, *weights)

    recv = lax.all_to_all(send, seq, 0, 0, tiled=True)
    nz = shifted([slabs[0], *ordered(slabs[1:], recv)], "z")
    keys = IMAGE_KEYS + TEXT_KEYS
    dkv, odq = pl.pallas_call(
        attention_kernel,
        out_shape=[shape((keys, 128), BF16), shape((BLOCKS * CTL_Q, 128), BF16)],
        in_specs=[SMEM, VMEM],
        out_specs=[VMEM] * 2,
        scratch_shapes=[
            pltpu.VMEM((keys, 128), BF16),
            pltpu.VMEM((HEAD, keys), BF16),
            pltpu.VMEM((HEAD, keys), BF16),
            pltpu.VMEM((BLOCKS * CTL_Q, 128), BF16),
            pltpu.VMEM((keys, TQ), F32),
            pltpu.VMEM((keys, 128), F32),
        ],
        compiler_params=params(32),
        cost_estimate=pl.CostEstimate(flops=40_000_000_000, bytes_accessed=3_200_000, transcendentals=8_400_000),
        name="attention",
    )(role, recv)
    back = pl.pallas_call(
        scatter_kernel,
        out_shape=shape((BLOCKS, CHUNK, 128), BF16),
        in_specs=[SMEM] + [VMEM] * 2 + [ANY] * 3,
        out_specs=VMEM,
        compiler_params=params(16),
        name="scatter",
    )(role, dkv, odq, *nz[1:])
    back = lax.all_to_all(back, seq, 0, 0, tiled=True)

    ctl_rows = pl.pallas_call(
        head_back_ctl_kernel,
        out_shape=shape((IMG, 4 * WIDTH), BF16),
        in_specs=[VMEM] * 3,
        out_specs=VMEM,
        compiler_params=params(16),
        name="head_back_ctl",
    )(back, proj, gains)
    blocks = shifted([ctl_rows] * 4, "z")
    mine0, mine1, theirs0, theirs1, token = pl.pallas_call(
        post_kernel,
        out_shape=[rows] * 4 + [shape((8, 128), F32)],
        in_specs=[VMEM] * 4 + [HBM] * 2 + [VMEM] + [HBM] * 6,
        out_specs=[ANY] * 4 + [VMEM],
        scratch_shapes=[
            pltpu.VMEM((3, 3, D, WIDTH), BF16),
            pltpu.VMEM((3, WIDTH, D), BF16),
            pltpu.VMEM((IMG + TXT, 4 * WIDTH), BF16),
            pltpu.VMEM((2 * IMG + TXT, D), BF16),
            pltpu.VMEM((2 * IMG + TXT, 128), F32),
            pltpu.VMEM((4, ROWS, IMG), BF16),
            pltpu.SemaphoreType.DMA((6,)),
            pltpu.SemaphoreType.DMA((2,)),
            pltpu.SemaphoreType.DMA((12,)),
        ],
        compiler_params=params(54),
        cost_estimate=pl.CostEstimate(flops=14_000_000_000, bytes_accessed=30_000_000, transcendentals=0),
        name="post",
    )(back, proj, gains, ctl_rows, xhat, rstd, mod, *weights)
    terms = pl.pallas_call(
        weight_kernel,
        out_shape=shape((4, PIECE, 4 * WIDTH), BF16),
        in_specs=[VMEM] * 8 + [SMEM],
        out_specs=VMEM,
        compiler_params=params(24),
        cost_estimate=pl.CostEstimate(flops=3_000_000_000, bytes_accessed=5_000_000, transcendentals=0),
        name="weight",
    )(*nz, *blocks, token)
    got1 = lax.ppermute(theirs1, "tp", other_core)
    got0 = lax.ppermute(theirs0, "tp", other_core)
    passed = (mine1.astype(F32) + got1.astype(F32)).astype(BF16)
    passed = lax.ppermute(passed, "tp", other_chip)
    terms = lax.all_to_all(terms, "y", 0, 0, tiled=True)
    mine, theirs = pl.pallas_call(
        weight_sum_kernel,
        out_shape=[shape((PIECE // 2, 4 * WIDTH), F32), shape((PIECE // 2, 4 * WIDTH), BF16)],
        in_specs=[VMEM],
        out_specs=[VMEM] * 2,
        compiler_params=params(16),
        name="weight_sum",
    )(terms)
    theirs = lax.ppermute(theirs, "w", [(0, 1), (1, 0)])
    grad_qkv, grad_out = pl.pallas_call(
        weight_out_kernel,
        out_shape=[shape((3, PIECE // 2, WIDTH), F32), shape((PIECE // 2, WIDTH), F32)],
        in_specs=[VMEM] * 2,
        out_specs=[VMEM] * 2,
        compiler_params=params(16),
        name="weight_out",
    )(mine, theirs)

    y_img, d_img, d_ctl, y_txt, d_txt = pl.pallas_call(
        final_kernel,
        out_shape=[shape((SHARE, IMG), BF16)] * 3 + [shape((TXT, SHARE), BF16)] * 2,
        in_specs=[VMEM] * 7,
        out_specs=[VMEM] * 5,
        compiler_params=params(16),
        name="final",
    )(img.T, dy_img.T, txt, dy_txt, mine0, got0, passed)
    return y_img.T, y_txt, d_img.T, d_txt, d_ctl.T, grad_qkv.transpose(1, 0, 2), grad_out.T


def solution(mesh):
    fine = Mesh(mesh.devices.reshape(4, 4, 2, 4), ("z", "y", "w", "tp"))
    seq = ("z", "y", "w")
    rows = P(seq, "tp")
    qkv = P(None, None, "tp")
    out = P("tp", None)
    in_specs = (rows,) * 5 + (P(), P(), P(), qkv, out, qkv, out, qkv, out)
    out_specs = (rows,) * 5 + (P(seq, None, "tp"), P("tp", seq))
    return jax.shard_map(
        per_device, mesh=fine, in_specs=in_specs, out_specs=out_specs, check_vma=False
    )
```

```python
import jax
import jax.numpy as jnp
from jax import lax
from jax.experimental import pallas as pl
from jax.experimental.pallas import tpu as pltpu
from jax.sharding import Mesh, PartitionSpec as P

EPS = 1e-06
HEAD = 64
HEADS = 6
WIDTH = HEADS * HEAD
D = 2432
SHARE = 608
PIECE = 152
TEXT_ROWS = 160
ROWS = 3 * SHARE + TEXT_ROWS
IMG = 128
TXT = 16
BLOCKS = 32
CHUNK = 192
IMAGE_KEYS = BLOCKS * IMG
TEXT_KEYS = BLOCKS * TXT
MAIN_Q = 48
CTL_Q = 64
MAIN_PARTS = 3
CTL_PARTS = 2
CTL_AT = HEADS * MAIN_PARTS
TQ = 512
TK = 512
F32 = jnp.float32
BF16 = jnp.bfloat16
NT = (((1,), (1,)), ((), ()))
VMEM = pl.BlockSpec(memory_space=pltpu.VMEM)
SMEM = pl.BlockSpec(memory_space=pltpu.SMEM)
ANY = pl.BlockSpec(memory_space=pl.ANY)
HBM = pl.BlockSpec(memory_space=pltpu.HBM)


def params(mib):
    return pltpu.CompilerParams(vmem_limit_bytes=mib * 1024 * 1024)


def dot(a, b):
    return jnp.dot(a, b, preferred_element_type=F32)


def dot_nt(a, b):
    return lax.dot_general(a, b, NT, preferred_element_type=F32)


def head(values, h):
    return values[:, h * HEAD : (h + 1) * HEAD]


def inverse_rms(values):
    return lax.rsqrt(jnp.mean(values * values, axis=-1, keepdims=True) + EPS)


def spread_text(packed):
    packed = packed[0:PIECE]
    return jnp.concatenate([packed] + [pltpu.roll(packed, 128 - 32 * a, 1) for a in (1, 2, 3)], 0)


def pack_text(columns):
    pieces = [columns[PIECE * a : PIECE * (a + 1)] for a in range(4)]
    packed = pieces[0] + sum(pltpu.roll(pieces[a], 32 * a, 1) for a in (1, 2, 3))
    return jnp.concatenate([packed, jnp.zeros((TEXT_ROWS - PIECE, IMG), F32)], 0)


def weight_copies(sources, wq, wo, sems):
    return [
        (
            pltpu.make_async_copy(sources[s], wq.at[s], sems.at[s]),
            pltpu.make_async_copy(sources[3 + s], wo.at[s], sems.at[3 + s]),
        )
        for s in range(3)
    ]


def order_kernel(after, *refs):
    pass


def ordered(arrays, after):
    return pl.pallas_call(
        order_kernel,
        out_shape=[jax.ShapeDtypeStruct(x.shape, x.dtype) for x in arrays],
        in_specs=[ANY] * (1 + len(arrays)),
        out_specs=[ANY] * len(arrays),
        input_output_aliases={1 + i: i for i in range(len(arrays))},
        compiler_params=params(1),
        name="order",
    )(after, *arrays)


def pack_kernel(img, ctl, dy, txt, dy_txt, out, text_rows, sems):
    copies = [
        pltpu.make_async_copy(part, text_rows.at[i], sems.at[3 + i]) for i, part in enumerate((txt, dy_txt))
    ] + [
        pltpu.make_async_copy(part, out.at[pl.ds(SHARE * i, SHARE)], sems.at[i])
        for i, part in enumerate((img, ctl, dy))
    ]
    for copy in copies:
        copy.start()
    copies[0].wait()
    copies[1].wait()
    text = text_rows[...].reshape(2 * TXT, SHARE).astype(F32)
    text = jnp.concatenate([text, jnp.zeros((IMG - 2 * TXT, SHARE), F32)], 0)
    text = jnp.concatenate([text, jnp.zeros((IMG, 640 - SHARE), F32)], 1)
    out[3 * SHARE :, :] = pack_text(text.T).astype(BF16)
    for copy in copies[2:]:
        copy.wait()


class Results:
    def __init__(self, sems):
        self.sems, self.copies = sems, []

    def send(self, source, target):
        copy = pltpu.make_async_copy(source, target, self.sems.at[len(self.copies)])
        copy.start()
        self.copies.append(copy)

    def finish(self):
        for copy in self.copies:
            copy.wait()


def pre_kernel(
    in0, in1, in2, in3, mod, gains, wq_img, wq_txt, wq_ctl, wo_img, wo_txt, wo_ctl,
    send, proj, xhat, rstd, nz0, nz1, nz2, nz3,
    wq, wo, gat, nz, sems,
):
    copies = weight_copies((wq_img, wq_txt, wq_ctl, wo_img, wo_txt, wo_ctl), wq, wo, sems)
    for s in range(3):
        copies[s][0].start()
        copies[s][1].start()

    for i, part in enumerate((in0, in1, in2, in3)):
        gat[lax.axis_index("tp") ^ i] = part[...]

    def rows(slab):
        return gat[:, SHARE * slab : SHARE * (slab + 1), :].reshape(D, IMG).T.astype(F32)

    def stream(s, x, e, at):
        count = x.shape[0]
        centered = x - jnp.mean(x, axis=-1, keepdims=True)
        inverse = lax.rsqrt(jnp.mean(centered * centered, axis=-1, keepdims=True) + EPS)
        standard = centered * inverse
        xhat[at : at + count, :] = standard.astype(BF16)
        rstd[at : at + count, :] = jnp.broadcast_to(inverse, (count, 128))
        n = (standard * (1.0 + mod[s, 1:2, :]) + mod[s, 0:1, :]).astype(BF16)
        copies[s][0].wait()
        pq = dot(n, wq[s, 0])
        pk = dot(n, wq[s, 1])
        pv = dot(n, wq[s, 2])
        proj[at : at + count, 0:WIDTH] = pq
        proj[at : at + count, WIDTH : 2 * WIDTH] = pk
        copies[s][1].wait()
        g = dot_nt(e, wo[s])
        kv, qg = [], []
        for h in range(HEADS):
            q_h, k_h = head(pq, h), head(pk, h)
            q_h = q_h * inverse_rms(q_h) * (gains[s, 0:1, :] * 0.125)
            k_h = k_h * inverse_rms(k_h) * gains[s, 1:2, :]
            kv.append(jnp.concatenate([k_h, head(pv, h)], 1).astype(BF16))
            qg.append(jnp.concatenate([q_h, head(g, h)], 1).astype(BF16))
        return n, kv, qg

    dy = rows(2)
    text = jnp.concatenate([spread_text(gat[c, 3 * SHARE :, :].astype(F32)) for c in range(4)], 0).astype(BF16).T.astype(F32)
    e_img = (mod[0, 2:3, :] * dy).astype(BF16)
    n, kv, qg = stream(0, rows(0), e_img, 0)
    for h in range(HEADS):
        for t in range(MAIN_PARTS):
            to = MAIN_PARTS * h + t
            send[to, 0:IMG, :] = kv[h]
            last = min(IMG, MAIN_Q * (t + 1))
            send[to, IMG + TXT : IMG + TXT + last - MAIN_Q * t, :] = qg[h][MAIN_Q * t : last]
    e_txt = (mod[1, 2:3, :] * text[TXT : 2 * TXT]).astype(BF16)
    n, kv, qg = stream(1, text[0:TXT], e_txt, IMG)
    for h in range(HEADS):
        for t in range(MAIN_PARTS):
            send[MAIN_PARTS * h + t, IMG : IMG + TXT, :] = kv[h]
        send[MAIN_PARTS * h + 2, CHUNK - TXT : CHUNK, :] = qg[h]
    e_ctl = mod[2, 2:3, :] * dy
    n, kv, qg = stream(2, rows(1), e_ctl.astype(BF16), IMG + TXT)
    for h in range(HEADS):
        for u in range(CTL_PARTS):
            to = CTL_AT + CTL_PARTS * h + u
            send[to, 0:IMG, :] = kv[h]
            send[to, IMG:CHUNK, :] = qg[h][CTL_Q * u : CTL_Q * (u + 1)]
    for to in range(CTL_AT + CTL_PARTS * HEADS, BLOCKS):
        send[to] = jnp.zeros((CHUNK, 128), BF16)
    nz[:, 0] = n.T.reshape(4, SHARE, IMG)
    nz[:, 1] = e_ctl.astype(BF16).T.reshape(4, SHARE, IMG)
    for d, out in enumerate((nz0, nz1, nz2, nz3)):
        out[...] = nz[lax.rem(lax.axis_index("z") + d, 4)]


def attention_kernel(role, recv, dkv_out, odq, kv, kt, vt, qg, probs, dkv):
    is_main = role[0]
    live = role[1]

    for b in range(BLOCKS):
        kv[IMG * b : IMG * (b + 1), :] = recv[b, 0:IMG, :]

    @pl.when(is_main == 1)
    def _():
        for b in range(BLOCKS):
            kv[IMAGE_KEYS + TXT * b : IMAGE_KEYS + TXT * (b + 1), :] = recv[b, IMG : IMG + TXT, :]
            qg[MAIN_Q * b : MAIN_Q * (b + 1), :] = recv[b, IMG + TXT : CHUNK, :]

    @pl.when(is_main == 0)
    def _():
        kv[IMAGE_KEYS:, :] = jnp.zeros((TEXT_KEYS, 128), BF16)
        for b in range(BLOCKS):
            qg[CTL_Q * b : CTL_Q * (b + 1), :] = recv[b, IMG:CHUNK, :]

    for i in range((IMAGE_KEYS + TEXT_KEYS) // 128):
        block = kv[128 * i : 128 * (i + 1), :].T
        kt[:, 128 * i : 128 * (i + 1)] = block[0:HEAD]
        vt[:, 128 * i : 128 * (i + 1)] = block[HEAD:128]
    dkv[...] = jnp.zeros_like(dkv)
    zeros_half = jnp.zeros((HEAD, TQ), BF16)
    low_lanes = lax.broadcasted_iota(jnp.int32, (TQ, 128), 1) < HEAD

    def q_tile(i, carry):
        q_at = pl.multiple_of(i * TQ, TQ)
        tile = qg[pl.ds(q_at, TQ), :]
        tile_t = tile.T
        g_t = tile_t[HEAD:128].astype(F32)
        q_rhs = jnp.concatenate([tile_t[0:HEAD], zeros_half], 0)
        g_rhs = jnp.concatenate([zeros_half, tile_t[HEAD:128]], 0)
        tile = tile.astype(F32)
        q_only = jnp.where(low_lanes, tile, 0.0).astype(BF16)
        g_only = jnp.where(low_lanes, 0.0, tile).astype(BF16)
        qg_rhs = jnp.concatenate([q_only, g_only], 0)

        def forward(at, state, masked):
            total, o_t = state
            p = jnp.exp(dot(kv[pl.ds(at, TK), :], q_rhs))
            if masked:
                p = jnp.where(lax.broadcasted_iota(jnp.int32, (TK, TQ), 0) < live, p, 0.0)
            probs[pl.ds(at, TK), :] = p
            total = total + jnp.sum(p.reshape(TK // 8, 8, TQ), 0)
            o_t = o_t + dot(vt[:, pl.ds(at, TK)], p.astype(BF16))
            return total, o_t

        state = (jnp.zeros((8, TQ), F32), jnp.zeros((HEAD, TQ), F32))
        state = lax.fori_loop(
            0, IMAGE_KEYS // TK, lambda j, c: forward(pl.multiple_of(j * TK, TK), c, False), state,
            unroll=8,
        )
        total, o_t = lax.fori_loop(0, is_main, lambda j, c: forward(IMAGE_KEYS, c, True), state)
        inverse = 1.0 / jnp.sum(total, axis=0, keepdims=True)
        o_t = (o_t * inverse).astype(BF16).astype(F32)
        delta = jnp.sum(g_t * o_t, axis=0, keepdims=True)

        def backward(at, dq_t):
            p = probs[pl.ds(at, TK), :] * inverse
            ds = (p * (dot(kv[pl.ds(at, TK), :], g_rhs) - delta)).astype(BF16)
            dkv[pl.ds(at, TK), :] += dot(jnp.concatenate([ds, p.astype(BF16)], 1), qg_rhs)
            return dq_t + dot(kt[:, pl.ds(at, TK)], ds)

        dq_t = jnp.zeros((HEAD, TQ), F32)
        dq_t = lax.fori_loop(
            0, IMAGE_KEYS // TK, lambda j, c: backward(pl.multiple_of(j * TK, TK), c), dq_t, unroll=8
        )
        dq_t = lax.fori_loop(0, is_main, lambda j, c: backward(IMAGE_KEYS, c), dq_t)
        odq[pl.ds(q_at, TQ), :] = jnp.concatenate([o_t, dq_t * 0.125], 0).astype(BF16).T
        return carry

    tiles = jnp.where(is_main == 1, BLOCKS * MAIN_Q // TQ, BLOCKS * CTL_Q // TQ)
    lax.fori_loop(0, tiles, q_tile, 0)

    dkv_out[...] = dkv[...].astype(BF16)


def scatter_kernel(role, dkv, odq, after0, after1, after2, out):
    for b in range(BLOCKS):
        out[b, 0:IMG, :] = dkv[IMG * b : IMG * (b + 1), :]

    @pl.when(role[0] == 1)
    def _():
        for b in range(BLOCKS):
            out[b, IMG : IMG + TXT, :] = dkv[IMAGE_KEYS + TXT * b : IMAGE_KEYS + TXT * (b + 1), :]
            out[b, IMG + TXT : CHUNK, :] = odq[MAIN_Q * b : MAIN_Q * (b + 1), :]

    @pl.when(role[0] == 0)
    def _():
        for b in range(BLOCKS):
            out[b, IMG:CHUNK, :] = odq[CTL_Q * b : CTL_Q * (b + 1), :]


def head_norm_back(x, gain, dy):
    inverse = inverse_rms(x)
    dy = dy * gain
    return inverse * dy - x * (inverse * inverse * inverse * jnp.mean(x * dy, axis=-1, keepdims=True))


def head_back(s, at, count, dkv, odq, proj, gains):
    o, dq, dk, dv = [], [], [], []
    for h in range(HEADS):
        x_q = proj[at : at + count, h * HEAD : (h + 1) * HEAD]
        x_k = proj[at : at + count, WIDTH + h * HEAD : WIDTH + (h + 1) * HEAD]
        o.append(odq[h][:, 0:HEAD])
        dq.append(head_norm_back(x_q, gains[s, 0:1, :], odq[h][:, HEAD:128]))
        dk.append(head_norm_back(x_k, gains[s, 1:2, :], dkv[h][:, 0:HEAD]))
        dv.append(dkv[h][:, HEAD:128])
    return [jnp.concatenate(parts, 1).astype(BF16) for parts in (dq, dk, dv, o)]


def head_back_ctl_kernel(recv, proj, gains, out):
    dkv, odq = [], []
    for h in range(HEADS):
        parts = [recv[CTL_AT + CTL_PARTS * h + u].astype(F32) for u in range(CTL_PARTS)]
        dkv.append(parts[0][0:IMG] + parts[1][0:IMG])
        odq.append(jnp.concatenate([parts[0][IMG:], parts[1][IMG:]], 0))
    for j, part in enumerate(head_back(2, IMG + TXT, IMG, dkv, odq, proj, gains)):
        out[:, j * WIDTH : (j + 1) * WIDTH] = part


def head_back_main(recv, proj, gains, main):
    kv_img, kv_txt, oq_img, oq_txt = [], [], [], []
    for h in range(HEADS):
        parts = [recv[MAIN_PARTS * h + t].astype(F32) for t in range(MAIN_PARTS)]
        kv = parts[0][0 : IMG + TXT] + parts[1][0 : IMG + TXT] + parts[2][0 : IMG + TXT]
        kv_img.append(kv[0:IMG])
        kv_txt.append(kv[IMG:])
        oq_img.append(
            jnp.concatenate(
                [parts[0][IMG + TXT :], parts[1][IMG + TXT :], parts[2][IMG + TXT : CHUNK - TXT]], 0
            )
        )
        oq_txt.append(parts[2][CHUNK - TXT :])
    for j, part in enumerate(head_back(0, 0, IMG, kv_img, oq_img, proj, gains)):
        main[0:IMG, j * WIDTH : (j + 1) * WIDTH] = part
    for j, part in enumerate(head_back(1, IMG, TXT, kv_txt, oq_txt, proj, gains)):
        main[IMG:, j * WIDTH : (j + 1) * WIDTH] = part


def back(s, dq, dk, dv, o, wq, wo, mod, standard, inverse):
    u = dot_nt(dq, wq[0]) + dot_nt(dk, wq[1]) + dot_nt(dv, wq[2])
    u = u * (1.0 + mod[s, 1:2, :])
    u = u - jnp.mean(u, axis=-1, keepdims=True) - standard * jnp.mean(u * standard, axis=-1, keepdims=True)
    return u * inverse, mod[s, 2:3, :] * dot(o, wo[...])


def slab(values):
    return values.astype(BF16).T.reshape(4, SHARE, IMG)


def post_kernel(
    recv, proj, gains, ctl_rows, xhat_in, rstd_in, mod, wq_img, wq_txt, wq_ctl, wo_img, wo_txt, wo_ctl,
    mine0, mine1, theirs0, theirs1, token,
    wq, wo, main, xhat, rstd, slabs, sems, in_sems, out_sems,
):
    arrivals = [
        pltpu.make_async_copy(xhat_in, xhat, in_sems.at[0]),
        pltpu.make_async_copy(rstd_in, rstd, in_sems.at[1]),
    ]
    for copy in arrivals:
        copy.start()
    results = Results(out_sems)
    token[...] = jnp.zeros_like(token)
    copies = weight_copies((wq_img, wq_txt, wq_ctl, wo_img, wo_txt, wo_ctl), wq, wo, sems)
    for copy in (copies[2][0], copies[2][1], copies[0][0]):
        copy.start()

    def stream(s, parts, at, later):
        count = parts[0].shape[0]
        copies[s][0].wait()
        copies[s][1].wait()
        for copy in later:
            copy.start()
        return back(s, *parts, wq.at[s], wo.at[s], mod, xhat[at : at + count, :].astype(F32), rstd[at : at + count, 0:1])

    def joint(at, count):
        return [main[at : at + count, j * WIDTH : (j + 1) * WIDTH] for j in range(4)]

    def leave(at, count):
        for other, out in enumerate((mine0, theirs0, mine1, theirs1)):
            results.send(slabs.at[lax.axis_index("tp") ^ other, pl.ds(at, count)], out.at[pl.ds(at, count)])

    head_back_main(recv, proj, gains, main)
    for copy in arrivals:
        copy.wait()
    u, y_ctl = stream(2, [ctl_rows[:, j * WIDTH : (j + 1) * WIDTH] for j in range(4)], IMG + TXT, (copies[0][1], copies[1][0]))
    slabs[:, 2 * SHARE : 3 * SHARE, :] = slab(u)
    leave(2 * SHARE, SHARE)
    u, y = stream(0, joint(0, IMG), 0, (copies[1][1],))
    slabs[:, SHARE : 2 * SHARE, :] = slab(u)
    slabs[:, 0:SHARE, :] = slab(y + y_ctl)
    leave(0, 2 * SHARE)
    u, y = stream(1, joint(IMG, TXT), IMG, ())
    text = jnp.concatenate([y, u, jnp.zeros((IMG - 2 * TXT, D), F32)], 0).astype(BF16).T.astype(F32)
    for c in range(4):
        slabs[c, 3 * SHARE :, :] = pack_text(text[SHARE * c : SHARE * (c + 1)]).astype(BF16)
    leave(3 * SHARE, TEXT_ROWS)
    results.finish()


def weight_kernel(nz0, nz1, nz2, nz3, b0, b1, b2, b3, after, out):
    nz, blocks = (nz0, nz1, nz2, nz3), (b0, b1, b2, b3)
    total = jnp.concatenate(
        [
            dot(
                jnp.concatenate([r[j] for r in nz], 1),
                jnp.concatenate([r[:, 3 * j * WIDTH : (3 + j) * WIDTH] for r in blocks], 0),
            )
            for j in range(2)
        ],
        1,
    )
    for p in range(4):
        out[p] = total[PIECE * p : PIECE * (p + 1)].astype(BF16)


def weight_sum_kernel(terms, mine, theirs):
    half = PIECE // 2
    low = lax.axis_index("w") == 0
    total = sum(terms[p].astype(F32) for p in range(4))
    first, second = total[0:half], total[half:]
    mine[...] = jnp.where(low, first, second)
    theirs[...] = jnp.where(low, second, first).astype(BF16)


def weight_out_kernel(mine, other, qkv, out):
    for j in range(4):
        columns = slice(WIDTH * j, WIDTH * (j + 1))
        total = mine[:, columns] + other[:, columns].astype(F32)
        if j < 3:
            qkv[j] = total
        else:
            out[...] = total


def final_kernel(img, dy, txt, dy_txt, part0, part1, part2, y_img, d_img, d_ctl, y_txt, d_txt):
    total = part0[...].astype(F32) + part1[...].astype(F32) + part2[...].astype(F32)
    y_img[...] = (img[...].astype(F32) + total[0:SHARE]).astype(BF16)
    d_img[...] = (dy[...].astype(F32) + total[SHARE : 2 * SHARE]).astype(BF16)
    d_ctl[...] = total[2 * SHARE : 3 * SHARE].astype(BF16)
    text = jnp.concatenate([spread_text(total[3 * SHARE :]), jnp.zeros((640 - SHARE, IMG), F32)], 0).T
    y_txt[...] = (txt[...].astype(F32) + text[0:TXT, 0:SHARE]).astype(BF16)
    d_txt[...] = (dy_txt[...].astype(F32) + text[TXT : 2 * TXT, 0:SHARE]).astype(BF16)


def shifted(parts, axis):
    return [parts[0]] + [
        lax.ppermute(parts[d], axis, [(i, (i + d) % 4) for i in range(4)]) for d in (1, 2, 3)
    ]


def per_device(
    img, txt, ctl, dy_img, dy_txt, live_text_length, modulation, query_key_gains,
    w_qkv_img, wo_img, w_qkv_txt, wo_txt, w_qkv_ctl, wo_ctl,
):
    seq = ("z", "y", "w")
    seq_pos = lax.axis_index(seq)
    role = jnp.stack([(seq_pos < CTL_AT).astype(jnp.int32), live_text_length[0]])
    mod, gains = modulation, query_key_gains
    weights = (
        w_qkv_img.transpose(1, 0, 2), w_qkv_txt.transpose(1, 0, 2), w_qkv_ctl.transpose(1, 0, 2),
        wo_img, wo_txt, wo_ctl,
    )
    shape = jax.ShapeDtypeStruct
    rows = shape((ROWS, IMG), BF16)
    other_core = [(i, i ^ 1) for i in range(4)]
    other_chip = [(i, i ^ 2) for i in range(4)]

    own = pl.pallas_call(
        pack_kernel,
        out_shape=rows,
        in_specs=[HBM] * 5,
        out_specs=VMEM,
        scratch_shapes=[pltpu.VMEM((2, TXT, SHARE), BF16), pltpu.SemaphoreType.DMA((5,))],
        compiler_params=pltpu.CompilerParams(vmem_limit_bytes=63_400_000),
        name="pack",
    )(img.T, ctl.T, dy_img.T, txt, dy_txt)
    from_chip = lax.ppermute(own, "tp", other_chip)
    from_core = lax.ppermute(own, "tp", other_core)
    from_both = lax.ppermute(from_chip, "tp", other_core)

    send, proj, xhat, rstd, *slabs = pl.pallas_call(
        pre_kernel,
        out_shape=[
            shape((BLOCKS, CHUNK, 128), BF16),
            shape((2 * IMG + TXT, 2 * WIDTH), F32),
            shape((2 * IMG + TXT, D), BF16),
            shape((2 * IMG + TXT, 128), F32),
        ] + [shape((2, SHARE, IMG), BF16)] * 4,
        in_specs=[VMEM] * 6 + [HBM] * 6,
        out_specs=[VMEM] * 8,
        scratch_shapes=[
            pltpu.VMEM((3, 3, D, WIDTH), BF16),
            pltpu.VMEM((3, WIDTH, D), BF16),
            pltpu.VMEM((4, ROWS, IMG), BF16),
            pltpu.VMEM((4, 2, SHARE, IMG), BF16),
            pltpu.SemaphoreType.DMA((6,)),
        ],
        compiler_params=params(56),
        name="pre",
    )(own, from_core, from_chip, from_both, mod, gains, *weights)

    recv = lax.all_to_all(send, seq, 0, 0, tiled=True)
    nz = shifted([slabs[0], *ordered(slabs[1:], recv)], "z")
    keys = IMAGE_KEYS + TEXT_KEYS
    dkv, odq = pl.pallas_call(
        attention_kernel,
        out_shape=[shape((keys, 128), BF16), shape((BLOCKS * CTL_Q, 128), BF16)],
        in_specs=[SMEM, VMEM],
        out_specs=[VMEM] * 2,
        scratch_shapes=[
            pltpu.VMEM((keys, 128), BF16),
            pltpu.VMEM((HEAD, keys), BF16),
            pltpu.VMEM((HEAD, keys), BF16),
            pltpu.VMEM((BLOCKS * CTL_Q, 128), BF16),
            pltpu.VMEM((keys, TQ), F32),
            pltpu.VMEM((keys, 128), F32),
        ],
        compiler_params=params(32),
        cost_estimate=pl.CostEstimate(flops=40_000_000_000, bytes_accessed=3_200_000, transcendentals=8_400_000),
        name="attention",
    )(role, recv)
    back = pl.pallas_call(
        scatter_kernel,
        out_shape=shape((BLOCKS, CHUNK, 128), BF16),
        in_specs=[SMEM] + [VMEM] * 2 + [ANY] * 3,
        out_specs=VMEM,
        compiler_params=params(16),
        name="scatter",
    )(role, dkv, odq, *nz[1:])
    back = lax.all_to_all(back, seq, 0, 0, tiled=True)

    ctl_rows = pl.pallas_call(
        head_back_ctl_kernel,
        out_shape=shape((IMG, 4 * WIDTH), BF16),
        in_specs=[VMEM] * 3,
        out_specs=VMEM,
        compiler_params=params(16),
        name="head_back_ctl",
    )(back, proj, gains)
    blocks = shifted([ctl_rows] * 4, "z")
    mine0, mine1, theirs0, theirs1, token = pl.pallas_call(
        post_kernel,
        out_shape=[rows] * 4 + [shape((8, 128), F32)],
        in_specs=[VMEM] * 4 + [HBM] * 2 + [VMEM] + [HBM] * 6,
        out_specs=[ANY] * 4 + [VMEM],
        scratch_shapes=[
            pltpu.VMEM((3, 3, D, WIDTH), BF16),
            pltpu.VMEM((3, WIDTH, D), BF16),
            pltpu.VMEM((IMG + TXT, 4 * WIDTH), BF16),
            pltpu.VMEM((2 * IMG + TXT, D), BF16),
            pltpu.VMEM((2 * IMG + TXT, 128), F32),
            pltpu.VMEM((4, ROWS, IMG), BF16),
            pltpu.SemaphoreType.DMA((6,)),
            pltpu.SemaphoreType.DMA((2,)),
            pltpu.SemaphoreType.DMA((12,)),
        ],
        compiler_params=params(54),
        cost_estimate=pl.CostEstimate(flops=14_000_000_000, bytes_accessed=30_000_000, transcendentals=0),
        name="post",
    )(back, proj, gains, ctl_rows, xhat, rstd, mod, *weights)
    terms = pl.pallas_call(
        weight_kernel,
        out_shape=shape((4, PIECE, 4 * WIDTH), BF16),
        in_specs=[VMEM] * 8 + [SMEM],
        out_specs=VMEM,
        compiler_params=params(24),
        cost_estimate=pl.CostEstimate(flops=3_000_000_000, bytes_accessed=5_000_000, transcendentals=0),
        name="weight",
    )(*nz, *blocks, token)
    got1 = lax.ppermute(theirs1, "tp", other_core)
    got0 = lax.ppermute(theirs0, "tp", other_core)
    passed = (mine1.astype(F32) + got1.astype(F32)).astype(BF16)
    passed = lax.ppermute(passed, "tp", other_chip)
    terms = lax.all_to_all(terms, "y", 0, 0, tiled=True)
    mine, theirs = pl.pallas_call(
        weight_sum_kernel,
        out_shape=[shape((PIECE // 2, 4 * WIDTH), F32), shape((PIECE // 2, 4 * WIDTH), BF16)],
        in_specs=[VMEM],
        out_specs=[VMEM] * 2,
        compiler_params=params(16),
        name="weight_sum",
    )(terms)
    theirs = lax.ppermute(theirs, "w", [(0, 1), (1, 0)])
    grad_qkv, grad_out = pl.pallas_call(
        weight_out_kernel,
        out_shape=[shape((3, PIECE // 2, WIDTH), F32), shape((PIECE // 2, WIDTH), F32)],
        in_specs=[VMEM] * 2,
        out_specs=[VMEM] * 2,
        compiler_params=params(16),
        name="weight_out",
    )(mine, theirs)

    y_img, d_img, d_ctl, y_txt, d_txt = pl.pallas_call(
        final_kernel,
        out_shape=[shape((SHARE, IMG), BF16)] * 3 + [shape((TXT, SHARE), BF16)] * 2,
        in_specs=[VMEM] * 7,
        out_specs=[VMEM] * 5,
        compiler_params=params(16),
        name="final",
    )(img.T, dy_img.T, txt, dy_txt, mine0, got0, passed)
    return y_img.T, y_txt, d_img.T, d_txt, d_ctl.T, grad_qkv.transpose(1, 0, 2), grad_out.T


def solution(mesh):
    fine = Mesh(mesh.devices.reshape(4, 4, 2, 4), ("z", "y", "w", "tp"))
    seq = ("z", "y", "w")
    rows = P(seq, "tp")
    qkv = P(None, None, "tp")
    out = P("tp", None)
    in_specs = (rows,) * 5 + (P(), P(), P(), qkv, out, qkv, out, qkv, out)
    out_specs = (rows,) * 5 + (P(seq, None, "tp"), P("tp", seq))
    return jax.shard_map(
        per_device, mesh=fine, in_specs=in_specs, out_specs=out_specs, check_vma=False
    )
```

```python
import jax
import jax.numpy as jnp
from jax import lax
from jax.experimental import pallas as pl
from jax.experimental.pallas import tpu as pltpu
from jax.sharding import Mesh, PartitionSpec as P

EPS = 1e-06
HEAD = 64
HEADS = 6
WIDTH = HEADS * HEAD
D = 2432
SHARE = 608
PIECE = 152
TEXT_ROWS = 160
ROWS = 3 * SHARE + TEXT_ROWS
IMG = 128
TXT = 16
BLOCKS = 32
CHUNK = 192
IMAGE_KEYS = BLOCKS * IMG
TEXT_KEYS = BLOCKS * TXT
MAIN_Q = 48
CTL_Q = 64
MAIN_PARTS = 3
CTL_PARTS = 2
CTL_AT = HEADS * MAIN_PARTS
TQ = 512
TK = 512
F32 = jnp.float32
BF16 = jnp.bfloat16
NT = (((1,), (1,)), ((), ()))
VMEM = pl.BlockSpec(memory_space=pltpu.VMEM)
SMEM = pl.BlockSpec(memory_space=pltpu.SMEM)
ANY = pl.BlockSpec(memory_space=pl.ANY)
HBM = pl.BlockSpec(memory_space=pltpu.HBM)


def params(mib):
    return pltpu.CompilerParams(vmem_limit_bytes=mib * 1024 * 1024)


def dot(a, b):
    return jnp.dot(a, b, preferred_element_type=F32)


def dot_nt(a, b):
    return lax.dot_general(a, b, NT, preferred_element_type=F32)


def head(values, h):
    return values[:, h * HEAD : (h + 1) * HEAD]


def inverse_rms(values):
    return lax.rsqrt(jnp.mean(values * values, axis=-1, keepdims=True) + EPS)


def spread_text(packed):
    packed = packed[0:PIECE]
    return jnp.concatenate([packed] + [pltpu.roll(packed, 128 - 32 * a, 1) for a in (1, 2, 3)], 0)


def pack_text(columns):
    pieces = [columns[PIECE * a : PIECE * (a + 1)] for a in range(4)]
    packed = pieces[0] + sum(pltpu.roll(pieces[a], 32 * a, 1) for a in (1, 2, 3))
    return jnp.concatenate([packed, jnp.zeros((TEXT_ROWS - PIECE, IMG), F32)], 0)


def weight_copies(sources, wq, wo, sems):
    return [
        (
            pltpu.make_async_copy(sources[s], wq.at[s], sems.at[s]),
            pltpu.make_async_copy(sources[3 + s], wo.at[s], sems.at[3 + s]),
        )
        for s in range(3)
    ]


def order_kernel(after, *refs):
    pass


def ordered(arrays, after):
    return pl.pallas_call(
        order_kernel,
        out_shape=[jax.ShapeDtypeStruct(x.shape, x.dtype) for x in arrays],
        in_specs=[ANY] * (1 + len(arrays)),
        out_specs=[ANY] * len(arrays),
        input_output_aliases={1 + i: i for i in range(len(arrays))},
        compiler_params=params(1),
        name="order",
    )(after, *arrays)


def pack_kernel(img, ctl, dy, txt, dy_txt, out, text_rows, sems):
    copies = [
        pltpu.make_async_copy(part, text_rows.at[i], sems.at[3 + i]) for i, part in enumerate((txt, dy_txt))
    ] + [
        pltpu.make_async_copy(part, out.at[pl.ds(SHARE * i, SHARE)], sems.at[i])
        for i, part in enumerate((img, ctl, dy))
    ]
    for copy in copies:
        copy.start()
    copies[0].wait()
    copies[1].wait()
    text = text_rows[...].reshape(2 * TXT, SHARE).astype(F32)
    text = jnp.concatenate([text, jnp.zeros((IMG - 2 * TXT, SHARE), F32)], 0)
    text = jnp.concatenate([text, jnp.zeros((IMG, 640 - SHARE), F32)], 1)
    out[3 * SHARE :, :] = pack_text(text.T).astype(BF16)
    for copy in copies[2:]:
        copy.wait()


class Results:
    def __init__(self, sems):
        self.sems, self.copies = sems, []

    def send(self, source, target):
        copy = pltpu.make_async_copy(source, target, self.sems.at[len(self.copies)])
        copy.start()
        self.copies.append(copy)

    def finish(self):
        for copy in self.copies:
            copy.wait()


def pre_kernel(
    in0, in1, in2, in3, mod, gains, wq_img, wq_txt, wq_ctl, wo_img, wo_txt, wo_ctl,
    send, proj, xhat, rstd, nz0, nz1, nz2, nz3,
    wq, wo, gat, nz, sems,
):
    copies = weight_copies((wq_img, wq_txt, wq_ctl, wo_img, wo_txt, wo_ctl), wq, wo, sems)
    for s in range(3):
        copies[s][0].start()
        copies[s][1].start()

    for i, part in enumerate((in0, in1, in2, in3)):
        gat[lax.axis_index("tp") ^ i] = part[...]

    def rows(slab):
        return gat[:, SHARE * slab : SHARE * (slab + 1), :].reshape(D, IMG).T.astype(F32)

    def stream(s, x, e, at):
        count = x.shape[0]
        centered = x - jnp.mean(x, axis=-1, keepdims=True)
        inverse = lax.rsqrt(jnp.mean(centered * centered, axis=-1, keepdims=True) + EPS)
        standard = centered * inverse
        xhat[at : at + count, :] = standard.astype(BF16)
        rstd[at : at + count, :] = jnp.broadcast_to(inverse, (count, 128))
        n = (standard * (1.0 + mod[s, 1:2, :]) + mod[s, 0:1, :]).astype(BF16)
        copies[s][0].wait()
        pq = dot(n, wq[s, 0])
        pk = dot(n, wq[s, 1])
        pv = dot(n, wq[s, 2])
        proj[at : at + count, 0:WIDTH] = pq
        proj[at : at + count, WIDTH : 2 * WIDTH] = pk
        copies[s][1].wait()
        g = dot_nt(e, wo[s])
        kv, qg = [], []
        for h in range(HEADS):
            q_h, k_h = head(pq, h), head(pk, h)
            q_h = q_h * inverse_rms(q_h) * (gains[s, 0:1, :] * 0.125)
            k_h = k_h * inverse_rms(k_h) * gains[s, 1:2, :]
            kv.append(jnp.concatenate([k_h, head(pv, h)], 1).astype(BF16))
            qg.append(jnp.concatenate([q_h, head(g, h)], 1).astype(BF16))
        return n, kv, qg

    dy = rows(2)
    text = jnp.concatenate([spread_text(gat[c, 3 * SHARE :, :].astype(F32)) for c in range(4)], 0).astype(BF16).T.astype(F32)
    e_img = (mod[0, 2:3, :] * dy).astype(BF16)
    n, kv, qg = stream(0, rows(0), e_img, 0)
    for h in range(HEADS):
        for t in range(MAIN_PARTS):
            to = MAIN_PARTS * h + t
            send[to, 0:IMG, :] = kv[h]
            last = min(IMG, MAIN_Q * (t + 1))
            send[to, IMG + TXT : IMG + TXT + last - MAIN_Q * t, :] = qg[h][MAIN_Q * t : last]
    e_txt = (mod[1, 2:3, :] * text[TXT : 2 * TXT]).astype(BF16)
    n, kv, qg = stream(1, text[0:TXT], e_txt, IMG)
    for h in range(HEADS):
        for t in range(MAIN_PARTS):
            send[MAIN_PARTS * h + t, IMG : IMG + TXT, :] = kv[h]
        send[MAIN_PARTS * h + 2, CHUNK - TXT : CHUNK, :] = qg[h]
    e_ctl = mod[2, 2:3, :] * dy
    n, kv, qg = stream(2, rows(1), e_ctl.astype(BF16), IMG + TXT)
    for h in range(HEADS):
        for u in range(CTL_PARTS):
            to = CTL_AT + CTL_PARTS * h + u
            send[to, 0:IMG, :] = kv[h]
            send[to, IMG:CHUNK, :] = qg[h][CTL_Q * u : CTL_Q * (u + 1)]
    for to in range(CTL_AT + CTL_PARTS * HEADS, BLOCKS):
        send[to] = jnp.zeros((CHUNK, 128), BF16)
    nz[:, 0] = n.T.reshape(4, SHARE, IMG)
    nz[:, 1] = e_ctl.astype(BF16).T.reshape(4, SHARE, IMG)
    for d, out in enumerate((nz0, nz1, nz2, nz3)):
        out[...] = nz[lax.rem(lax.axis_index("z") + d, 4)]


def attention_kernel(role, recv, dkv_out, odq, kv, kt, vt, qg, probs, dkv):
    is_main = role[0]
    live = role[1]

    for b in range(BLOCKS):
        kv[IMG * b : IMG * (b + 1), :] = recv[b, 0:IMG, :]

    @pl.when(is_main == 1)
    def _():
        for b in range(BLOCKS):
            kv[IMAGE_KEYS + TXT * b : IMAGE_KEYS + TXT * (b + 1), :] = recv[b, IMG : IMG + TXT, :]
            qg[MAIN_Q * b : MAIN_Q * (b + 1), :] = recv[b, IMG + TXT : CHUNK, :]

    @pl.when(is_main == 0)
    def _():
        kv[IMAGE_KEYS:, :] = jnp.zeros((TEXT_KEYS, 128), BF16)
        for b in range(BLOCKS):
            qg[CTL_Q * b : CTL_Q * (b + 1), :] = recv[b, IMG:CHUNK, :]

    for i in range((IMAGE_KEYS + TEXT_KEYS) // 128):
        block = kv[128 * i : 128 * (i + 1), :].T
        kt[:, 128 * i : 128 * (i + 1)] = block[0:HEAD]
        vt[:, 128 * i : 128 * (i + 1)] = block[HEAD:128]
    dkv[...] = jnp.zeros_like(dkv)
    zeros_half = jnp.zeros((HEAD, TQ), BF16)
    low_lanes = lax.broadcasted_iota(jnp.int32, (TQ, 128), 1) < HEAD

    def q_tile(i, carry):
        q_at = pl.multiple_of(i * TQ, TQ)
        tile = qg[pl.ds(q_at, TQ), :]
        tile_t = tile.T
        g_t = tile_t[HEAD:128].astype(F32)
        q_rhs = jnp.concatenate([tile_t[0:HEAD], zeros_half], 0)
        g_rhs = jnp.concatenate([zeros_half, tile_t[HEAD:128]], 0)
        tile = tile.astype(F32)
        q_only = jnp.where(low_lanes, tile, 0.0).astype(BF16)
        g_only = jnp.where(low_lanes, 0.0, tile).astype(BF16)
        qg_rhs = jnp.concatenate([q_only, g_only], 0)

        def forward(at, state, masked):
            total, o_t = state
            p = jnp.exp(dot(kv[pl.ds(at, TK), :], q_rhs))
            if masked:
                p = jnp.where(lax.broadcasted_iota(jnp.int32, (TK, TQ), 0) < live, p, 0.0)
            probs[pl.ds(at, TK), :] = p
            total = total + jnp.sum(p.reshape(TK // 8, 8, TQ), 0)
            o_t = o_t + dot(vt[:, pl.ds(at, TK)], p.astype(BF16))
            return total, o_t

        state = (jnp.zeros((8, TQ), F32), jnp.zeros((HEAD, TQ), F32))
        state = lax.fori_loop(
            0, IMAGE_KEYS // TK, lambda j, c: forward(pl.multiple_of(j * TK, TK), c, False), state,
            unroll=8,
        )
        total, o_t = lax.fori_loop(0, is_main, lambda j, c: forward(IMAGE_KEYS, c, True), state)
        inverse = 1.0 / jnp.sum(total, axis=0, keepdims=True)
        o_t = (o_t * inverse).astype(BF16).astype(F32)
        delta = jnp.sum(g_t * o_t, axis=0, keepdims=True)

        def backward(at, dq_t):
            p = probs[pl.ds(at, TK), :] * inverse
            ds = (p * (dot(kv[pl.ds(at, TK), :], g_rhs) - delta)).astype(BF16)
            dkv[pl.ds(at, TK), :] += dot(jnp.concatenate([ds, p.astype(BF16)], 1), qg_rhs)
            return dq_t + dot(kt[:, pl.ds(at, TK)], ds)

        dq_t = jnp.zeros((HEAD, TQ), F32)
        dq_t = lax.fori_loop(
            0, IMAGE_KEYS // TK, lambda j, c: backward(pl.multiple_of(j * TK, TK), c), dq_t, unroll=8
        )
        dq_t = lax.fori_loop(0, is_main, lambda j, c: backward(IMAGE_KEYS, c), dq_t)
        odq[pl.ds(q_at, TQ), :] = jnp.concatenate([o_t, dq_t * 0.125], 0).astype(BF16).T
        return carry

    tiles = jnp.where(is_main == 1, BLOCKS * MAIN_Q // TQ, BLOCKS * CTL_Q // TQ)
    lax.fori_loop(0, tiles, q_tile, 0)

    dkv_out[...] = dkv[...].astype(BF16)


def scatter_kernel(role, dkv, odq, after0, after1, after2, out):
    for b in range(BLOCKS):
        out[b, 0:IMG, :] = dkv[IMG * b : IMG * (b + 1), :]

    @pl.when(role[0] == 1)
    def _():
        for b in range(BLOCKS):
            out[b, IMG : IMG + TXT, :] = dkv[IMAGE_KEYS + TXT * b : IMAGE_KEYS + TXT * (b + 1), :]
            out[b, IMG + TXT : CHUNK, :] = odq[MAIN_Q * b : MAIN_Q * (b + 1), :]

    @pl.when(role[0] == 0)
    def _():
        for b in range(BLOCKS):
            out[b, IMG:CHUNK, :] = odq[CTL_Q * b : CTL_Q * (b + 1), :]


def head_norm_back(x, gain, dy):
    inverse = inverse_rms(x)
    dy = dy * gain
    return inverse * dy - x * (inverse * inverse * inverse * jnp.mean(x * dy, axis=-1, keepdims=True))


def head_back(s, at, count, dkv, odq, proj, gains):
    o, dq, dk, dv = [], [], [], []
    for h in range(HEADS):
        x_q = proj[at : at + count, h * HEAD : (h + 1) * HEAD]
        x_k = proj[at : at + count, WIDTH + h * HEAD : WIDTH + (h + 1) * HEAD]
        o.append(odq[h][:, 0:HEAD])
        dq.append(head_norm_back(x_q, gains[s, 0:1, :], odq[h][:, HEAD:128]))
        dk.append(head_norm_back(x_k, gains[s, 1:2, :], dkv[h][:, 0:HEAD]))
        dv.append(dkv[h][:, HEAD:128])
    return [jnp.concatenate(parts, 1).astype(BF16) for parts in (dq, dk, dv, o)]


def head_back_ctl_kernel(recv, proj, gains, out):
    dkv, odq = [], []
    for h in range(HEADS):
        parts = [recv[CTL_AT + CTL_PARTS * h + u].astype(F32) for u in range(CTL_PARTS)]
        dkv.append(parts[0][0:IMG] + parts[1][0:IMG])
        odq.append(jnp.concatenate([parts[0][IMG:], parts[1][IMG:]], 0))
    for j, part in enumerate(head_back(2, IMG + TXT, IMG, dkv, odq, proj, gains)):
        out[:, j * WIDTH : (j + 1) * WIDTH] = part


def head_back_main(recv, proj, gains, main):
    kv_img, kv_txt, oq_img, oq_txt = [], [], [], []
    for h in range(HEADS):
        parts = [recv[MAIN_PARTS * h + t].astype(F32) for t in range(MAIN_PARTS)]
        kv = parts[0][0 : IMG + TXT] + parts[1][0 : IMG + TXT] + parts[2][0 : IMG + TXT]
        kv_img.append(kv[0:IMG])
        kv_txt.append(kv[IMG:])
        oq_img.append(
            jnp.concatenate(
                [parts[0][IMG + TXT :], parts[1][IMG + TXT :], parts[2][IMG + TXT : CHUNK - TXT]], 0
            )
        )
        oq_txt.append(parts[2][CHUNK - TXT :])
    for j, part in enumerate(head_back(0, 0, IMG, kv_img, oq_img, proj, gains)):
        main[0:IMG, j * WIDTH : (j + 1) * WIDTH] = part
    for j, part in enumerate(head_back(1, IMG, TXT, kv_txt, oq_txt, proj, gains)):
        main[IMG:, j * WIDTH : (j + 1) * WIDTH] = part


def back(s, dq, dk, dv, o, wq, wo, mod, standard, inverse):
    u = dot_nt(dq, wq[0]) + dot_nt(dk, wq[1]) + dot_nt(dv, wq[2])
    u = u * (1.0 + mod[s, 1:2, :])
    u = u - jnp.mean(u, axis=-1, keepdims=True) - standard * jnp.mean(u * standard, axis=-1, keepdims=True)
    return u * inverse, mod[s, 2:3, :] * dot(o, wo[...])


def slab(values):
    return values.astype(BF16).T.reshape(4, SHARE, IMG)


def post_kernel(
    recv, proj, gains, ctl_rows, xhat_in, rstd_in, mod, wq_img, wq_txt, wq_ctl, wo_img, wo_txt, wo_ctl,
    mine0, mine1, theirs0, theirs1, token,
    wq, wo, main, xhat, rstd, slabs, sems, in_sems, out_sems,
):
    arrivals = [
        pltpu.make_async_copy(xhat_in, xhat, in_sems.at[0]),
        pltpu.make_async_copy(rstd_in, rstd, in_sems.at[1]),
    ]
    for copy in arrivals:
        copy.start()
    results = Results(out_sems)
    token[...] = jnp.zeros_like(token)
    copies = weight_copies((wq_img, wq_txt, wq_ctl, wo_img, wo_txt, wo_ctl), wq, wo, sems)
    for copy in (copies[2][0], copies[2][1], copies[0][0]):
        copy.start()

    def stream(s, parts, at, later):
        count = parts[0].shape[0]
        copies[s][0].wait()
        copies[s][1].wait()
        for copy in later:
            copy.start()
        return back(s, *parts, wq.at[s], wo.at[s], mod, xhat[at : at + count, :].astype(F32), rstd[at : at + count, 0:1])

    def joint(at, count):
        return [main[at : at + count, j * WIDTH : (j + 1) * WIDTH] for j in range(4)]

    def leave(at, count):
        for other, out in enumerate((mine0, theirs0, mine1, theirs1)):
            results.send(slabs.at[lax.axis_index("tp") ^ other, pl.ds(at, count)], out.at[pl.ds(at, count)])

    head_back_main(recv, proj, gains, main)
    for copy in arrivals:
        copy.wait()
    u, y_ctl = stream(2, [ctl_rows[:, j * WIDTH : (j + 1) * WIDTH] for j in range(4)], IMG + TXT, (copies[0][1], copies[1][0]))
    slabs[:, 2 * SHARE : 3 * SHARE, :] = slab(u)
    leave(2 * SHARE, SHARE)
    u, y = stream(0, joint(0, IMG), 0, (copies[1][1],))
    slabs[:, SHARE : 2 * SHARE, :] = slab(u)
    slabs[:, 0:SHARE, :] = slab(y + y_ctl)
    leave(0, 2 * SHARE)
    u, y = stream(1, joint(IMG, TXT), IMG, ())
    text = jnp.concatenate([y, u, jnp.zeros((IMG - 2 * TXT, D), F32)], 0).astype(BF16).T.astype(F32)
    for c in range(4):
        slabs[c, 3 * SHARE :, :] = pack_text(text[SHARE * c : SHARE * (c + 1)]).astype(BF16)
    leave(3 * SHARE, TEXT_ROWS)
    results.finish()


def weight_kernel(nz0, nz1, nz2, nz3, b0, b1, b2, b3, after, out):
    nz, blocks = (nz0, nz1, nz2, nz3), (b0, b1, b2, b3)
    total = jnp.concatenate(
        [
            dot(
                jnp.concatenate([r[j] for r in nz], 1),
                jnp.concatenate([r[:, 3 * j * WIDTH : (3 + j) * WIDTH] for r in blocks], 0),
            )
            for j in range(2)
        ],
        1,
    )
    for p in range(4):
        out[p] = total[PIECE * p : PIECE * (p + 1)].astype(BF16)


def weight_sum_kernel(terms, mine, theirs):
    half = PIECE // 2
    low = lax.axis_index("w") == 0
    total = sum(terms[p].astype(F32) for p in range(4))
    first, second = total[0:half], total[half:]
    mine[...] = jnp.where(low, first, second)
    theirs[...] = jnp.where(low, second, first).astype(BF16)


def weight_out_kernel(mine, other, qkv, out):
    for j in range(4):
        columns = slice(WIDTH * j, WIDTH * (j + 1))
        total = mine[:, columns] + other[:, columns].astype(F32)
        if j < 3:
            qkv[j] = total
        else:
            out[...] = total


def final_kernel(img, dy, txt, dy_txt, part0, part1, part2, y_img, d_img, d_ctl, y_txt, d_txt):
    total = part0[...].astype(F32) + part1[...].astype(F32) + part2[...].astype(F32)
    y_img[...] = (img[...].astype(F32) + total[0:SHARE]).astype(BF16)
    d_img[...] = (dy[...].astype(F32) + total[SHARE : 2 * SHARE]).astype(BF16)
    d_ctl[...] = total[2 * SHARE : 3 * SHARE].astype(BF16)
    text = jnp.concatenate([spread_text(total[3 * SHARE :]), jnp.zeros((640 - SHARE, IMG), F32)], 0).T
    y_txt[...] = (txt[...].astype(F32) + text[0:TXT, 0:SHARE]).astype(BF16)
    d_txt[...] = (dy_txt[...].astype(F32) + text[TXT : 2 * TXT, 0:SHARE]).astype(BF16)


def shifted(parts, axis):
    return [parts[0]] + [
        lax.ppermute(parts[d], axis, [(i, (i + d) % 4) for i in range(4)]) for d in (1, 2, 3)
    ]


def per_device(
    img, txt, ctl, dy_img, dy_txt, live_text_length, modulation, query_key_gains,
    w_qkv_img, wo_img, w_qkv_txt, wo_txt, w_qkv_ctl, wo_ctl,
):
    seq = ("z", "y", "w")
    seq_pos = lax.axis_index(seq)
    role = jnp.stack([(seq_pos < CTL_AT).astype(jnp.int32), live_text_length[0]])
    mod, gains = modulation, query_key_gains
    weights = (
        w_qkv_img.transpose(1, 0, 2), w_qkv_txt.transpose(1, 0, 2), w_qkv_ctl.transpose(1, 0, 2),
        wo_img, wo_txt, wo_ctl,
    )
    shape = jax.ShapeDtypeStruct
    rows = shape((ROWS, IMG), BF16)
    other_core = [(i, i ^ 1) for i in range(4)]
    other_chip = [(i, i ^ 2) for i in range(4)]

    own = pl.pallas_call(
        pack_kernel,
        out_shape=rows,
        in_specs=[HBM] * 5,
        out_specs=VMEM,
        scratch_shapes=[pltpu.VMEM((2, TXT, SHARE), BF16), pltpu.SemaphoreType.DMA((5,))],
        compiler_params=pltpu.CompilerParams(vmem_limit_bytes=63_400_000),
        name="pack",
    )(img.T, ctl.T, dy_img.T, txt, dy_txt)
    from_chip = lax.ppermute(own, "tp", other_chip)
    from_core = lax.ppermute(own, "tp", other_core)
    from_both = lax.ppermute(from_chip, "tp", other_core)

    send, proj, xhat, rstd, *slabs = pl.pallas_call(
        pre_kernel,
        out_shape=[
            shape((BLOCKS, CHUNK, 128), BF16),
            shape((2 * IMG + TXT, 2 * WIDTH), F32),
            shape((2 * IMG + TXT, D), BF16),
            shape((2 * IMG + TXT, 128), F32),
        ] + [shape((2, SHARE, IMG), BF16)] * 4,
        in_specs=[VMEM] * 6 + [HBM] * 6,
        out_specs=[VMEM] * 8,
        scratch_shapes=[
            pltpu.VMEM((3, 3, D, WIDTH), BF16),
            pltpu.VMEM((3, WIDTH, D), BF16),
            pltpu.VMEM((4, ROWS, IMG), BF16),
            pltpu.VMEM((4, 2, SHARE, IMG), BF16),
            pltpu.SemaphoreType.DMA((6,)),
        ],
        compiler_params=params(56),
        name="pre",
    )(own, from_core, from_chip, from_both, mod, gains, *weights)

    recv = lax.all_to_all(send, seq, 0, 0, tiled=True)
    nz = shifted([slabs[0], *ordered(slabs[1:], recv)], "z")
    keys = IMAGE_KEYS + TEXT_KEYS
    dkv, odq = pl.pallas_call(
        attention_kernel,
        out_shape=[shape((keys, 128), BF16), shape((BLOCKS * CTL_Q, 128), BF16)],
        in_specs=[SMEM, VMEM],
        out_specs=[VMEM] * 2,
        scratch_shapes=[
            pltpu.VMEM((keys, 128), BF16),
            pltpu.VMEM((HEAD, keys), BF16),
            pltpu.VMEM((HEAD, keys), BF16),
            pltpu.VMEM((BLOCKS * CTL_Q, 128), BF16),
            pltpu.VMEM((keys, TQ), F32),
            pltpu.VMEM((keys, 128), F32),
        ],
        compiler_params=params(32),
        cost_estimate=pl.CostEstimate(flops=40_000_000_000, bytes_accessed=3_200_000, transcendentals=8_400_000),
        name="attention",
    )(role, recv)
    back = pl.pallas_call(
        scatter_kernel,
        out_shape=shape((BLOCKS, CHUNK, 128), BF16),
        in_specs=[SMEM] + [VMEM] * 2 + [ANY] * 3,
        out_specs=VMEM,
        compiler_params=params(16),
        name="scatter",
    )(role, dkv, odq, *nz[1:])
    back = lax.all_to_all(back, seq, 0, 0, tiled=True)

    ctl_rows = pl.pallas_call(
        head_back_ctl_kernel,
        out_shape=shape((IMG, 4 * WIDTH), BF16),
        in_specs=[VMEM] * 3,
        out_specs=VMEM,
        compiler_params=params(16),
        name="head_back_ctl",
    )(back, proj, gains)
    blocks = shifted([ctl_rows] * 4, "z")
    mine0, mine1, theirs0, theirs1, token = pl.pallas_call(
        post_kernel,
        out_shape=[rows] * 4 + [shape((8, 128), F32)],
        in_specs=[VMEM] * 4 + [HBM] * 2 + [VMEM] + [HBM] * 6,
        out_specs=[ANY] * 4 + [VMEM],
        scratch_shapes=[
            pltpu.VMEM((3, 3, D, WIDTH), BF16),
            pltpu.VMEM((3, WIDTH, D), BF16),
            pltpu.VMEM((IMG + TXT, 4 * WIDTH), BF16),
            pltpu.VMEM((2 * IMG + TXT, D), BF16),
            pltpu.VMEM((2 * IMG + TXT, 128), F32),
            pltpu.VMEM((4, ROWS, IMG), BF16),
            pltpu.SemaphoreType.DMA((6,)),
            pltpu.SemaphoreType.DMA((2,)),
            pltpu.SemaphoreType.DMA((12,)),
        ],
        compiler_params=params(54),
        cost_estimate=pl.CostEstimate(flops=14_000_000_000, bytes_accessed=30_000_000, transcendentals=0),
        name="post",
    )(back, proj, gains, ctl_rows, xhat, rstd, mod, *weights)
    terms = pl.pallas_call(
        weight_kernel,
        out_shape=shape((4, PIECE, 4 * WIDTH), BF16),
        in_specs=[VMEM] * 8 + [SMEM],
        out_specs=VMEM,
        compiler_params=params(24),
        cost_estimate=pl.CostEstimate(flops=3_000_000_000, bytes_accessed=5_000_000, transcendentals=0),
        name="weight",
    )(*nz, *blocks, token)
    got1 = lax.ppermute(theirs1, "tp", other_core)
    got0 = lax.ppermute(theirs0, "tp", other_core)
    passed = (mine1.astype(F32) + got1.astype(F32)).astype(BF16)
    passed = lax.ppermute(passed, "tp", other_chip)
    terms = lax.all_to_all(terms, "y", 0, 0, tiled=True)
    mine, theirs = pl.pallas_call(
        weight_sum_kernel,
        out_shape=[shape((PIECE // 2, 4 * WIDTH), F32), shape((PIECE // 2, 4 * WIDTH), BF16)],
        in_specs=[VMEM],
        out_specs=[VMEM] * 2,
        compiler_params=params(16),
        name="weight_sum",
    )(terms)
    theirs = lax.ppermute(theirs, "w", [(0, 1), (1, 0)])
    grad_qkv, grad_out = pl.pallas_call(
        weight_out_kernel,
        out_shape=[shape((3, PIECE // 2, WIDTH), F32), shape((PIECE // 2, WIDTH), F32)],
        in_specs=[VMEM] * 2,
        out_specs=[VMEM] * 2,
        compiler_params=params(16),
        name="weight_out",
    )(mine, theirs)

    y_img, d_img, d_ctl, y_txt, d_txt = pl.pallas_call(
        final_kernel,
        out_shape=[shape((SHARE, IMG), BF16)] * 3 + [shape((TXT, SHARE), BF16)] * 2,
        in_specs=[VMEM] * 7,
        out_specs=[VMEM] * 5,
        compiler_params=pltpu.CompilerParams(vmem_limit_bytes=63_400_000),
        name="final",
    )(img.T, dy_img.T, txt, dy_txt, mine0, got0, passed)
    return y_img.T, y_txt, d_img.T, d_txt, d_ctl.T, grad_qkv.transpose(1, 0, 2), grad_out.T


def solution(mesh):
    fine = Mesh(mesh.devices.reshape(4, 4, 2, 4), ("z", "y", "w", "tp"))
    seq = ("z", "y", "w")
    rows = P(seq, "tp")
    qkv = P(None, None, "tp")
    out = P("tp", None)
    in_specs = (rows,) * 5 + (P(), P(), P(), qkv, out, qkv, out, qkv, out)
    out_specs = (rows,) * 5 + (P(seq, None, "tp"), P("tp", seq))
    return jax.shard_map(
        per_device, mesh=fine, in_specs=in_specs, out_specs=out_specs, check_vma=False
    )
```
